32 devices in a mesh: fsdp: 32 (over z, y, x, core).
Axes of the slice: x: 2, y: 2, z: 4, core: 2. Of those that a mesh axis runs over, the one named last changes fastest.
Arguments:
- patches: bfloat16 [12288, 768], P('fsdp'), may hold values from -6 to 6
- visible_index: int32 [12288], P('fsdp'), may hold values from 0 to 528, as said below
- segments: int32 [16928], P('fsdp'), may hold values from 0 to 1, as said below
- cotangent: bfloat16 [16928, 512], P('fsdp'), may hold values from -6 to 6
- enc_norm1_gain: bfloat16 [768], P('fsdp'), may hold values from 0.25 to 1.75
- enc_norm1_bias: bfloat16 [768], P('fsdp'), may hold values from -1.5 to 1.5
- enc_qkv: bfloat16 [768, 2304], P('fsdp'), may hold values from -0.21875 to 0.21875
- enc_query_bias: bfloat16 [768], P('fsdp'), may hold values from -1.5 to 1.5
- enc_value_bias: bfloat16 [768], P('fsdp'), may hold values from -1.5 to 1.5
- enc_out: bfloat16 [768, 768], P('fsdp'), may hold values from -0.875 to 0.875
- enc_out_bias: bfloat16 [768], P('fsdp'), may hold values from -1.5 to 1.5
- enc_norm2_gain: bfloat16 [768], P('fsdp'), may hold values from 0.25 to 1.75
- enc_norm2_bias: bfloat16 [768], P('fsdp'), may hold values from -1.5 to 1.5
- enc_up: bfloat16 [768, 3072], P('fsdp'), may hold values from -0.21875 to 0.21875
- enc_up_bias: bfloat16 [3072], P('fsdp'), may hold values from -2.5 to 2.5
- enc_down: bfloat16 [3072, 768], P('fsdp'), may hold values from -0.109375 to 0.109375
- enc_down_bias: bfloat16 [768], P('fsdp'), may hold values from -1.5 to 1.5
- embed_weight: bfloat16 [768, 512], P('fsdp'), may hold values from -0.21875 to 0.21875
- embed_bias: bfloat16 [512], P('fsdp'), may hold values from -1.5 to 1.5
- mask_token: bfloat16 [512], P('fsdp'), may hold values from -4 to 4
- dec_norm1_gain: bfloat16 [512], P('fsdp'), may hold values from 0.25 to 1.75
- dec_norm1_bias: bfloat16 [512], P('fsdp'), may hold values from -1.5 to 1.5
- dec_qkv: bfloat16 [512, 1536], P('fsdp'), may hold values from -0.25 to 0.25
- dec_query_bias: bfloat16 [512], P('fsdp'), may hold values from -1.5 to 1.5
- dec_value_bias: bfloat16 [512], P('fsdp'), may hold values from -1.5 to 1.5
- dec_out: bfloat16 [512, 512], P('fsdp'), may hold values from -1 to 1
- dec_out_bias: bfloat16 [512], P('fsdp'), may hold values from -1.5 to 1.5
- dec_norm2_gain: bfloat16 [512], P('fsdp'), may hold values from 0.25 to 1.75
- dec_norm2_bias: bfloat16 [512], P('fsdp'), may hold values from -1.5 to 1.5
- dec_up: bfloat16 [512, 2048], P('fsdp'), may hold values from -0.25 to 0.25
- dec_up_bias: bfloat16 [2048], P('fsdp'), may hold values from -2.5 to 2.5
- dec_down: bfloat16 [2048, 512], P('fsdp'), may hold values from -0.125 to 0.125
- dec_down_bias: bfloat16 [512], P('fsdp'), may hold values from -1.5 to 1.5
Outputs:
- decoder_out: bfloat16 [16928, 512], P('fsdp')
- patch_grad: float32 [12288, 768], P('fsdp')
- grad_enc_norm1_gain: float32 [768], P('fsdp')
- grad_enc_norm1_bias: float32 [768], P('fsdp')
- grad_enc_qkv: float32 [768, 2304], P('fsdp')
- grad_enc_query_bias: float32 [768], P('fsdp')
- grad_enc_value_bias: float32 [768], P('fsdp')
- grad_enc_out: float32 [768, 768], P('fsdp')
- grad_enc_out_bias: float32 [768], P('fsdp')
- grad_enc_norm2_gain: float32 [768], P('fsdp')
- grad_enc_norm2_bias: float32 [768], P('fsdp')
- grad_enc_up: float32 [768, 3072], P('fsdp')
- grad_enc_up_bias: float32 [3072], P('fsdp')
- grad_enc_down: float32 [3072, 768], P('fsdp')
- grad_enc_down_bias: float32 [768], P('fsdp')
- grad_embed_weight: float32 [768, 512], P('fsdp')
- grad_embed_bias: float32 [512], P('fsdp')
- grad_mask_token: float32 [512], P('fsdp')
- grad_dec_norm1_gain: float32 [512], P('fsdp')
- grad_dec_norm1_bias: float32 [512], P('fsdp')
- grad_dec_qkv: float32 [512, 1536], P('fsdp')
- grad_dec_query_bias: float32 [512], P('fsdp')
- grad_dec_value_bias: float32 [512], P('fsdp')
- grad_dec_out: float32 [512, 512], P('fsdp')
- grad_dec_out_bias: float32 [512], P('fsdp')
- grad_dec_norm2_gain: float32 [512], P('fsdp')
- grad_dec_norm2_bias: float32 [512], P('fsdp')
- grad_dec_up: float32 [512, 2048], P('fsdp')
- grad_dec_up_bias: float32 [2048], P('fsdp')
- grad_dec_down: float32 [2048, 512], P('fsdp')
- grad_dec_down_bias: float32 [512], P('fsdp')
The draws below stay inside these ranges and needn't reach their ends.
Inputs may be any that keep to these rules, and one draw needn't show every extreme that they name: `visible_index`: each sequence's block of 384 entries names distinct slots of that sequence in ascending order; its other 145 slots are masked. `segments`: each sequence of 529 slots is either one document (all ids 0) or two packed ones: id 0 on its first 264 slots and 1 on the rest.
All inputs are finite; a program needn't handle non-finite values.
Results may differ from the reference program's by a relative error of at most 0.025.
Values may be sent and summed in bfloat16 or wider, within the bound.
A program may use at most 256 MiB of HBM per device.

```python
import jax
import jax.numpy as jnp
from jax import lax

D = 768
HEADS = 12
FF = 3072
DD = 512
DHEADS = 16
DFF = 2048
ROW = 529
HALF = 264
VIS = 384
SEQS = 32
ENC_TOK = 12288
DEC_TOK = 16928


def draw_visible_index(key, part):
    key = jax.random.fold_in(key, 11)
    slot_ids = jnp.arange(ROW, dtype=jnp.int32)[None, :]
    scores = jax.random.randint(key, (SEQS, ROW), 0, 1 << 20, dtype=jnp.int32) * ROW + slot_ids
    chosen = lax.top_k(scores, VIS)[1]
    return jnp.sort(chosen, axis=1).reshape(-1).astype(jnp.int32)


def draw_segments(key, part):
    key = jax.random.fold_in(key, 12)
    packed = jax.random.randint(key, (SEQS, 1), 0, 2, dtype=jnp.int32)
    slot_ids = jnp.arange(ROW, dtype=jnp.int32)[None, :]
    return (packed * (slot_ids >= HALF).astype(jnp.int32)).reshape(-1).astype(jnp.int32)


def shard_levels(stream_key, dims, pieces, least, top_value):
    level = 1.0
    for position, shards_of in pieces:
        steps = jax.random.uniform(jax.random.fold_in(jax.random.fold_in(stream_key, 6), position), (shards_of,), jnp.float32, least / len(pieces), top_value / len(pieces))
        level = level * jnp.repeat(jnp.exp(steps), dims[position] // shards_of).reshape((-1,) + (1,) * (len(dims) - 1 - position))
    return level


def gaussian(stream_key, shape, width, limit, pieces=(), kind=jnp.bfloat16):
    values = jax.random.normal(stream_key, shape, jnp.float32) * width
    if len(pieces) > 0:
        values = shard_levels(stream_key, shape, pieces, -0.22, 0.18) * values
    return jnp.clip(values, min=-limit, max=limit).astype(kind)


def setup_inputs(seed: int = 0) -> dict:
    splits = jax.random.split(jax.random.key(seed), 34)
    return {
        "patches": gaussian(splits[0], (ENC_TOK, D), 1.0, 6.0, ((0, 32),)),
        "visible_index": draw_visible_index(jax.random.fold_in(splits[33], 71), 0),
        "segments": draw_segments(jax.random.fold_in(splits[33], 71), 0),
        "cotangent": gaussian(splits[3], (DEC_TOK, DD), 1.0, 6.0, ((0, 32),)),
        "enc_norm1_gain": jnp.clip(1.0 + 0.15 * jax.random.normal(splits[4], (D,), jnp.float32), 0.25, 1.75).astype(jnp.bfloat16),
        "enc_norm1_bias": gaussian(splits[5], (D,), 0.3, 1.5, ((0, 32),)),
        "enc_qkv": gaussian(splits[6], (D, 3 * D), D ** -0.5, 0.21875, ((0, 32),)),
        "enc_query_bias": gaussian(splits[7], (D,), 0.3, 1.5, ((0, 32),)),
        "enc_value_bias": gaussian(splits[8], (D,), 0.3, 1.5, ((0, 32),)),
        "enc_out": gaussian(splits[9], (D, D), (D // 16) ** -0.5, 0.875, ((0, 32),)),
        "enc_out_bias": gaussian(splits[10], (D,), 0.3, 1.5, ((0, 32),)),
        "enc_norm2_gain": jnp.clip(1.0 + 0.15 * jax.random.normal(splits[11], (D,), jnp.float32), 0.25, 1.75).astype(jnp.bfloat16),
        "enc_norm2_bias": gaussian(splits[12], (D,), 0.3, 1.5, ((0, 32),)),
        "enc_up": gaussian(splits[13], (D, FF), D ** -0.5, 0.21875, ((0, 32),)),
        "enc_up_bias": gaussian(splits[14], (FF,), 0.5, 2.5, ((0, 32),)),
        "enc_down": gaussian(splits[15], (FF, D), FF ** -0.5, 0.109375, ((0, 32),)),
        "enc_down_bias": gaussian(splits[16], (D,), 0.3, 1.5, ((0, 32),)),
        "embed_weight": gaussian(splits[17], (D, DD), D ** -0.5, 0.21875, ((0, 32),)),
        "embed_bias": gaussian(splits[18], (DD,), 0.3, 1.5, ((0, 32),)),
        "mask_token": gaussian(splits[19], (DD,), 1.0, 4.0, ((0, 32),)),
        "dec_norm1_gain": jnp.clip(1.0 + 0.15 * jax.random.normal(splits[20], (DD,), jnp.float32), 0.25, 1.75).astype(jnp.bfloat16),
        "dec_norm1_bias": gaussian(splits[21], (DD,), 0.3, 1.5, ((0, 32),)),
        "dec_qkv": gaussian(splits[22], (DD, 3 * DD), DD ** -0.5, 0.25, ((0, 32),)),
        "dec_query_bias": gaussian(splits[23], (DD,), 0.3, 1.5, ((0, 32),)),
        "dec_value_bias": gaussian(splits[24], (DD,), 0.3, 1.5, ((0, 32),)),
        "dec_out": gaussian(splits[25], (DD, DD), (DD // 16) ** -0.5, 1.0, ((0, 32),)),
        "dec_out_bias": gaussian(splits[26], (DD,), 0.3, 1.5, ((0, 32),)),
        "dec_norm2_gain": jnp.clip(1.0 + 0.15 * jax.random.normal(splits[27], (DD,), jnp.float32), 0.25, 1.75).astype(jnp.bfloat16),
        "dec_norm2_bias": gaussian(splits[28], (DD,), 0.3, 1.5, ((0, 32),)),
        "dec_up": gaussian(splits[29], (DD, DFF), DD ** -0.5, 0.25, ((0, 32),)),
        "dec_up_bias": gaussian(splits[30], (DFF,), 0.5, 2.5, ((0, 32),)),
        "dec_down": gaussian(splits[31], (DFF, DD), DFF ** -0.5, 0.125, ((0, 32),)),
        "dec_down_bias": gaussian(splits[32], (DD,), 0.3, 1.5, ((0, 32),)),
    }


PRECISE = lax.Precision.HIGHEST
EPSILON = 1e-06

@jax.custom_vjp
def low(v):
    return lax.optimization_barrier(v.astype(jnp.bfloat16)).astype(jnp.float32)

@jax.custom_vjp
def low_back(v):
    return v

def low_keep(v):
    return (low(v), None)

def low_pass(kept, grad):
    return (grad,)

def back_keep(v):
    return (v, None)

def back_low(kept, grad):
    return (low(grad),)
low.defvjp(low_keep, low_pass)
low_back.defvjp(back_keep, back_low)

def product(left, right):
    return jnp.matmul(left, right, precision=PRECISE)

def layer_norm(stream, gain, shift):
    row_mean = lax.optimization_barrier(jnp.mean(stream, -1, keepdims=True))
    centred = stream - row_mean
    row_var = lax.optimization_barrier(jnp.mean(centred * centred, -1, keepdims=True))
    return centred * lax.rsqrt(row_var + EPSILON) * gain + shift

def attend(query_rows, key_rows, value_rows, same_doc, head_count):
    length, model_width = query_rows.shape
    head_size = model_width // head_count
    score_scale = head_size ** (-0.5)
    query_heads = query_rows.reshape(length, head_count, head_size)
    key_heads = key_rows.reshape(length, head_count, head_size)
    value_heads = value_rows.reshape(length, head_count, head_size)
    raw_scores = low_back(jnp.einsum('qhd,khd->hqk', query_heads, key_heads, precision=PRECISE))
    scores = jnp.where(same_doc[None], raw_scores * score_scale, -1000000000.0)
    att_probs = low(jax.nn.softmax(scores, axis=-1))
    mixed = jnp.einsum('hqk,khd->qhd', att_probs, value_heads, precision=PRECISE)
    return mixed.reshape(length, model_width)

def block(stream, params, seg_ids, head_count):
    gain_one, shift_one, w_qkv, query_bias, value_bias, w_out, out_bias, gain_two, shift_two, w_up, up_bias, w_down, down_bias = params
    model_width = stream.shape[1]
    normed = low(layer_norm(stream, gain_one, shift_one))
    joined = low_back(product(normed, w_qkv))
    query_rows = low(joined[:, :model_width] + query_bias)
    key_rows = low(joined[:, model_width:2 * model_width])
    value_rows = low(joined[:, 2 * model_width:] + value_bias)
    same_doc = seg_ids[:, None] == seg_ids[None, :]
    attended = low(low_back(attend(query_rows, key_rows, value_rows, same_doc, head_count)))
    middle = stream + low_back(product(attended, w_out)) + out_bias
    normed_two = low(layer_norm(middle, gain_two, shift_two))
    hidden_up = low_back(product(normed_two, w_up)) + up_bias
    activated = low(jax.nn.gelu(hidden_up, approximate=False))
    return middle + low_back(product(activated, w_down)) + down_bias

def run_sequence(params, enc_rows, vis_slots, seg_ids):
    enc_params = params[:13]
    embed_w, embed_b, mask_vec = (params[13], params[14], params[15])
    dec_params = params[16:]
    enc_seg = seg_ids[vis_slots]
    hidden = block(enc_rows, enc_params, enc_seg, HEADS)
    embedded = low_back(product(low(hidden), embed_w)) + embed_b
    dec_in = jnp.broadcast_to(mask_vec, (ROW, DD)).at[vis_slots].set(embedded)
    return block(dec_in, dec_params, seg_ids, DHEADS)

def reference(patches, visible_index, segments, cotangent, enc_norm1_gain, enc_norm1_bias, enc_qkv, enc_query_bias, enc_value_bias, enc_out, enc_out_bias, enc_norm2_gain, enc_norm2_bias, enc_up, enc_up_bias, enc_down, enc_down_bias, embed_weight, embed_bias, mask_token, dec_norm1_gain, dec_norm1_bias, dec_qkv, dec_query_bias, dec_value_bias, dec_out, dec_out_bias, dec_norm2_gain, dec_norm2_bias, dec_up, dec_up_bias, dec_down, dec_down_bias):
    weights = (enc_norm1_gain, enc_norm1_bias, enc_qkv, enc_query_bias, enc_value_bias, enc_out, enc_out_bias, enc_norm2_gain, enc_norm2_bias, enc_up, enc_up_bias, enc_down, enc_down_bias, embed_weight, embed_bias, mask_token, dec_norm1_gain, dec_norm1_bias, dec_qkv, dec_query_bias, dec_value_bias, dec_out, dec_out_bias, dec_norm2_gain, dec_norm2_bias, dec_up, dec_up_bias, dec_down, dec_down_bias)
    params = tuple((piece.astype(jnp.float32) for piece in weights))
    inputs = patches.astype(jnp.float32).reshape(SEQS, VIS, D)
    vis_slots = visible_index.reshape(SEQS, VIS)
    seg_ids = segments.reshape(SEQS, ROW)
    checked = jax.checkpoint(run_sequence)

    def forward(params, inputs):
        results = lax.map(lambda sequence_in: checked(params, sequence_in[0], sequence_in[1], sequence_in[2]), (inputs, vis_slots, seg_ids))
        return results.reshape(SEQS * ROW, DD)
    result, pull = jax.vjp(forward, params, inputs)
    grads, patch_grad = pull(cotangent.astype(jnp.float32))
    return (result.astype(jnp.bfloat16), patch_grad.reshape(SEQS * VIS, D), grads[0], grads[1], grads[2], grads[3], grads[4], grads[5], grads[6], grads[7], grads[8], grads[9], grads[10], grads[11], grads[12], grads[13], grads[14], grads[15], grads[16], grads[17], grads[18], grads[19], grads[20], grads[21], grads[22], grads[23], grads[24], grads[25], grads[26], grads[27], grads[28])
```

```python
import jax
import jax.numpy as jnp
from jax import lax
from jax.experimental import pallas as pl
from jax.experimental.pallas import tpu as pltpu
from jax.sharding import PartitionSpec as P

HEADS = 12
DD = 512
DHEADS = 16
ROW = 529
VIS = 384


EPSILON = 1e-06


def widen(value):
    return value.astype(jnp.float32)


def layer_norm(stream, gain, shift):
    row_mean = jnp.mean(stream, -1, keepdims=True)
    centred = stream - row_mean
    row_var = jnp.mean(centred * centred, -1, keepdims=True)
    return centred * lax.rsqrt(row_var + EPSILON) * gain + shift


def norm_back(stream, gain, shift, grad_out):
    pull = jax.vjp(layer_norm, stream, gain, shift)[1]
    return pull(grad_out)


def gelu_exact(value):
    return jax.nn.gelu(value, approximate=False)


def split_heads(rows, head_count):
    batch, length, model_width = rows.shape
    return rows.reshape(batch, length, head_count, model_width // head_count)


def masked_scores(query_heads, key_heads, same_doc, score_scale):
    scores = (
        jnp.einsum("bqhd,bkhd->bhqk", query_heads, key_heads, preferred_element_type=jnp.float32)
        * score_scale
    )
    return jnp.where(same_doc[:, None], scores, -1000000000.0)


def attend_forward(query_rows, key_rows, value_rows, same_doc, head_count, score_scale):
    batch, length, model_width = query_rows.shape
    scores = masked_scores(
        split_heads(query_rows, head_count),
        split_heads(key_rows, head_count),
        same_doc,
        score_scale,
    )
    row_max = jnp.max(scores, -1, keepdims=True)
    expo = jnp.exp(scores - row_max)
    row_sum = jnp.sum(expo, -1, keepdims=True)
    att_probs = (expo / row_sum).astype(jnp.bfloat16)
    mixed = jnp.einsum(
        "bhqk,bkhd->bqhd",
        att_probs,
        split_heads(value_rows, head_count),
        preferred_element_type=jnp.float32,
    )
    return (mixed.reshape(batch, length, model_width), row_max + jnp.log(row_sum))


def attend_backward(
    query_rows, key_rows, value_rows, same_doc, log_total, grad_mixed, head_count, score_scale
):
    batch, length, model_width = query_rows.shape
    query_heads = split_heads(query_rows, head_count)
    key_heads = split_heads(key_rows, head_count)
    value_heads = split_heads(value_rows, head_count)
    grad_heads = split_heads(grad_mixed, head_count)
    att_probs = jnp.exp(masked_scores(query_heads, key_heads, same_doc, score_scale) - log_total)
    grad_value = jnp.einsum(
        "bhqk,bqhd->bkhd",
        att_probs.astype(jnp.bfloat16),
        grad_heads,
        preferred_element_type=jnp.float32,
    )
    grad_probs = jnp.einsum(
        "bqhd,bkhd->bhqk", grad_heads, value_heads, preferred_element_type=jnp.float32
    )
    centre = jnp.sum(att_probs * grad_probs, -1, keepdims=True)
    grad_scores = (att_probs * (grad_probs - centre) * score_scale).astype(jnp.bfloat16)
    grad_query = jnp.einsum(
        "bhqk,bkhd->bqhd", grad_scores, key_heads, preferred_element_type=jnp.float32
    )
    grad_key = jnp.einsum(
        "bhqk,bqhd->bkhd", grad_scores, query_heads, preferred_element_type=jnp.float32
    )
    rows = batch * length
    return (
        grad_query.reshape(rows, model_width),
        grad_key.reshape(rows, model_width),
        grad_value.reshape(rows, model_width),
    )


def block_forward(stream, params, seg_ids, head_count):
    (
        gain_one,
        shift_one,
        w_qkv,
        query_bias,
        value_bias,
        w_out,
        out_bias,
        gain_two,
        shift_two,
        w_up,
        up_bias,
        w_down,
        down_bias,
    ) = params
    row_count, model_width = stream.shape
    batch, length = seg_ids.shape
    score_scale = (model_width // head_count) ** (-0.5)
    normed = layer_norm(stream, widen(gain_one), widen(shift_one)).astype(jnp.bfloat16)
    joined = jnp.dot(normed, w_qkv, preferred_element_type=jnp.float32)
    query_rows = (joined[:, :model_width] + widen(query_bias)).astype(jnp.bfloat16)
    key_rows = joined[:, model_width : 2 * model_width].astype(jnp.bfloat16)
    value_rows = (joined[:, 2 * model_width :] + widen(value_bias)).astype(jnp.bfloat16)
    same_doc = seg_ids[:, :, None] == seg_ids[:, None, :]
    shape_three = (batch, length, model_width)
    mixed, log_total = attend_forward(
        query_rows.reshape(shape_three),
        key_rows.reshape(shape_three),
        value_rows.reshape(shape_three),
        same_doc,
        head_count,
        score_scale,
    )
    attended = mixed.reshape(row_count, model_width).astype(jnp.bfloat16)
    middle = stream + jnp.dot(attended, w_out, preferred_element_type=jnp.float32) + widen(out_bias)
    normed_two = layer_norm(middle, widen(gain_two), widen(shift_two)).astype(jnp.bfloat16)
    hidden_up = jnp.dot(normed_two, w_up, preferred_element_type=jnp.float32) + widen(up_bias)
    activated = gelu_exact(hidden_up).astype(jnp.bfloat16)
    result = (
        middle + jnp.dot(activated, w_down, preferred_element_type=jnp.float32) + widen(down_bias)
    )
    saved = (
        stream,
        middle,
        normed,
        query_rows,
        key_rows,
        value_rows,
        log_total,
        attended,
        normed_two,
        hidden_up,
        activated,
    )
    return (result, saved)


def back_feed(grad_out, params, saved):
    (
        gain_one,
        shift_one,
        w_qkv,
        query_bias,
        value_bias,
        w_out,
        out_bias,
        gain_two,
        shift_two,
        w_up,
        up_bias,
        w_down,
        down_bias,
    ) = params
    (
        stream,
        middle,
        normed,
        query_rows,
        key_rows,
        value_rows,
        log_total,
        attended,
        normed_two,
        hidden_up,
        activated,
    ) = saved
    grad_low = grad_out.astype(jnp.bfloat16)
    grad_down_bias = jnp.sum(grad_out, 0)
    grad_down = jnp.einsum("rf,rw->fw", activated, grad_low, preferred_element_type=jnp.float32).astype(jnp.bfloat16)
    grad_act = jnp.einsum("rw,fw->rf", grad_low, w_down, preferred_element_type=jnp.float32)
    grad_hidden = jax.vjp(gelu_exact, hidden_up)[1](grad_act)[0]
    grad_hidden_low = grad_hidden.astype(jnp.bfloat16)
    grad_up_bias = jnp.sum(grad_hidden, 0)
    grad_up = jnp.einsum(
        "rd,rf->df", normed_two, grad_hidden_low, preferred_element_type=jnp.float32
    ).astype(jnp.bfloat16)
    grad_normed_two = jnp.einsum(
        "rf,df->rd", grad_hidden_low, w_up, preferred_element_type=jnp.float32
    )
    grad_mid_norm, grad_gain_two, grad_shift_two = norm_back(
        middle, widen(gain_two), widen(shift_two), grad_normed_two
    )
    grad_middle = grad_out + grad_mid_norm
    return (
        grad_middle,
        (grad_gain_two, grad_shift_two, grad_up, grad_up_bias, grad_down, grad_down_bias),
    )


def back_attend(grad_middle, params, seg_ids, head_count, saved):
    (
        gain_one,
        shift_one,
        w_qkv,
        query_bias,
        value_bias,
        w_out,
        out_bias,
        gain_two,
        shift_two,
        w_up,
        up_bias,
        w_down,
        down_bias,
    ) = params
    (
        stream,
        middle,
        normed,
        query_rows,
        key_rows,
        value_rows,
        log_total,
        attended,
        normed_two,
        hidden_up,
        activated,
    ) = saved
    row_count, model_width = stream.shape
    batch, length = seg_ids.shape
    score_scale = (model_width // head_count) ** (-0.5)
    grad_middle_low = grad_middle.astype(jnp.bfloat16)
    grad_out_bias = jnp.sum(grad_middle, 0)
    grad_w_out = jnp.einsum(
        "rv,rw->vw", attended, grad_middle_low, preferred_element_type=jnp.float32
    ).astype(jnp.bfloat16)
    grad_attended = jnp.einsum(
        "rw,vw->rv", grad_middle_low, w_out, preferred_element_type=jnp.float32
    ).astype(jnp.bfloat16)
    same_doc = seg_ids[:, :, None] == seg_ids[:, None, :]
    shape_three = (batch, length, model_width)
    grad_query, grad_key, grad_value = attend_backward(
        query_rows.reshape(shape_three),
        key_rows.reshape(shape_three),
        value_rows.reshape(shape_three),
        same_doc,
        log_total,
        grad_attended.reshape(shape_three),
        head_count,
        score_scale,
    )
    grad_query_bias = jnp.sum(grad_query, 0)
    grad_value_bias = jnp.sum(grad_value, 0)
    grad_joined = jnp.concatenate([grad_query, grad_key, grad_value], 1).astype(jnp.bfloat16)
    grad_qkv = jnp.einsum("rd,rc->dc", normed, grad_joined, preferred_element_type=jnp.float32).astype(jnp.bfloat16)
    grad_normed = jnp.einsum("rc,dc->rd", grad_joined, w_qkv, preferred_element_type=jnp.float32)
    grad_in_norm, grad_gain_one, grad_shift_one = norm_back(
        stream, widen(gain_one), widen(shift_one), grad_normed
    )
    grads = (
        grad_gain_one,
        grad_shift_one,
        grad_qkv,
        grad_query_bias,
        grad_value_bias,
        grad_w_out,
        grad_out_bias,
    )
    return (grad_middle + grad_in_norm, grads)


def block_backward(grad_out, params, seg_ids, head_count, saved):
    grad_middle, feed_grads = back_feed(grad_out, params, saved)
    grad_in, attend_grads = back_attend(grad_middle, params, seg_ids, head_count, saved)
    return (grad_in, attend_grads + feed_grads)


MESH = pl.DeviceIdType.MESH
VMEM_BYTES = 60 * 2**20


class Place:
    def __init__(self):
        me = lax.axis_index("fsdp")
        self.c = c = lax.rem(me, 2)
        x = lax.rem(me // 2, 2)
        y = lax.rem(me // 4, 2)
        self.z0 = lax.rem(me // 8, 2)
        self.z1 = lax.rem(me // 16, 2)
        self.stride1 = 1 + c
        self.stride2 = 2 - c
        self.bit1 = x * (1 - c) + y * c
        self.bit2 = y * (1 - c) + x * c
        self.here = 2 * y + x
        self.core = me + 1 - 2 * c
        self.first = me + 2 * self.stride1 * (1 - 2 * self.bit1)
        self.second = me + 2 * self.stride2 * (1 - 2 * self.bit2)
        self.near = me + 8 * (1 - 2 * self.z0)
        self.far = me + 16 * (1 - 2 * self.z1)

    def along_second(self, bit1, j):
        return bit1 * self.stride1 + j * self.stride2

    def barrier(self):
        barrier = pltpu.get_barrier_semaphore()
        for partner in (self.core, self.first, self.second, self.near, self.far):
            pl.semaphore_signal(barrier, inc=1, device_id=(partner,), device_id_type=MESH)
        pl.semaphore_wait(barrier, 5)


def padded(rows):
    return -(-rows // 16) * 16


def gather_kernel(shapes, *refs):
    count = len(shapes)
    shards, vec_ref = refs[:count], refs[count]
    wholes, vec_out = refs[count + 1 : 2 * count + 1], refs[2 * count + 1]
    scratch = refs[2 * count + 2 :]
    sent, got, tiles = scratch[:count], scratch[count : 2 * count], scratch[2 * count : 3 * count]
    send_sem, recv_sem, local_sem = scratch[3 * count :]
    at = Place()
    at.barrier()
    started = []

    def send(src, dst, m, k, partner):
        copy = pltpu.make_async_remote_copy(
            src_ref=src,
            dst_ref=dst,
            send_sem=send_sem.at[m, k],
            recv_sem=recv_sem.at[m, k],
            device_id=(partner,),
            device_id_type=MESH,
        )
        copy.start()
        started.append(copy)
        return copy

    def view(m, z1, z0, yx):
        if m == count:
            return vec_out.at[z1, z0, yx, at.c]
        rows, columns = shapes[m]
        half = columns // 2
        lanes = pl.ds(pl.multiple_of(at.c * half, 128), half)
        if yx is None:
            return wholes[m].at[z1, z0, :, lanes]
        return wholes[m].at[z1, z0, pl.ds(pl.multiple_of(yx * 2 * rows, 16), 2 * rows), lanes]

    def my_half(m, mine):
        half = shapes[m][1] // 2
        low, high = shards[m][:, :half].astype(jnp.float32), shards[m][:, half:].astype(jnp.float32)
        return jnp.where(at.c == 0, low, high) if mine else jnp.where(at.c == 0, high, low)

    every = slice(None)
    flights = {}

    def stage(m, k):
        if k == 0:
            if m == count:
                return
            rows, columns = shapes[m]
            value = my_half(m, False)
            extra = padded(rows) - rows
            if extra:
                value = jnp.concatenate([value, jnp.zeros((extra, columns // 2), jnp.float32)], 0)
            sent[m][...] = value.astype(jnp.bfloat16)
            flights[m, 0] = [send(sent[m], got[m], m, 0, at.core)]
        elif k == 1:
            if m == count:
                local = pltpu.make_async_copy(vec_ref, view(m, at.z1, at.z0, at.here), local_sem.at[m])
                local.start()
                flights[m, 1] = [send(vec_ref, view(m, at.z1, at.z0, at.here), m, 1, at.far)]
            else:
                rows = shapes[m][0]
                flights[m, 0][0].wait_recv()
                other = got[m][...].astype(jnp.float32)[:rows]
                mine = my_half(m, True)
                both = jnp.concatenate(
                    [jnp.where(at.c == 0, mine, other), jnp.where(at.c == 0, other, mine)], 0
                )
                tiles[m][...] = both.astype(jnp.bfloat16)
                local = pltpu.make_async_copy(tiles[m], view(m, at.z1, at.z0, at.here), local_sem.at[m])
                local.start()
                flights[m, 1] = [send(tiles[m], view(m, at.z1, at.z0, at.here), m, 1, at.far)]
            flights[m, "local"] = local
        elif k == 2:
            flights[m, "local"].wait()
            flights[m, 1][0].wait_recv()
            part = view(m, every, at.z0, at.here)
            flights[m, 2] = [send(part, part, m, 2, at.near)]
        elif k == 3:
            flights[m, 2][0].wait_recv()
            part = view(m, every, every, at.here)
            flights[m, 3] = [send(part, part, m, 3, at.second)]
        elif k == 4:
            flights[m, 3][0].wait_recv()
            flights[m, 4] = []
            for j in range(2):
                part = view(m, every, every, at.along_second(at.bit1, j))
                flights[m, 4].append(send(part, part, m, 4 + j, at.first))
        elif k == 5:
            for copy in flights[m, 4]:
                copy.wait_recv()
            part = vec_out.at[:, :, :, at.c] if m == count else view(m, every, every, None)
            flights[m, 5] = [send(part, part, m, 6, at.core)]
        else:
            flights[m, 5][0].wait_recv()

    order = [count] + list(range(count))
    for step in range(len(order) + 6):
        for k in range(6, -1, -1):
            if 0 <= step - k < len(order):
                stage(order[step - k], k)
    for copy in started:
        copy.wait_send()


def gather_all(shards, vec):
    shapes = [shard.shape for shard in shards]
    count = len(shapes)
    any_space = pl.BlockSpec(memory_space=pl.ANY)
    vmem = pl.BlockSpec(memory_space=pltpu.VMEM)
    out_shape = [jax.ShapeDtypeStruct((2, 2, 8 * r, c), jnp.bfloat16) for r, c in shapes]
    out_shape.append(jax.ShapeDtypeStruct((2, 2, 4, 2, 8, 128), jnp.float32))
    scratch = [pltpu.VMEM((padded(r), c // 2), jnp.bfloat16) for r, c in shapes] * 2
    scratch += [pltpu.VMEM((2 * r, c // 2), jnp.bfloat16) for r, c in shapes]
    scratch += [
        pltpu.SemaphoreType.DMA((count + 1, 7)),
        pltpu.SemaphoreType.DMA((count + 1, 7)),
        pltpu.SemaphoreType.DMA((count + 1,)),
    ]

    def body(*refs):
        gather_kernel(shapes, *refs)

    return pl.pallas_call(
        body,
        out_shape=out_shape,
        in_specs=[vmem] * (count + 1),
        out_specs=[any_space] * (count + 1),
        scratch_shapes=scratch,
        compiler_params=pltpu.CompilerParams(
            collective_id=0, has_side_effects=True, vmem_limit_bytes=VMEM_BYTES
        ),
        name="gather_params",
    )(*shards, vec)


def add_rows(dst, src, rows):
    def body(i, carry):
        part = pl.ds(pl.multiple_of(i * 16, 16), 16)
        dst[part, :] = (dst[part, :].astype(jnp.float32) + src[part, :].astype(jnp.float32)).astype(dst.dtype)
        return carry

    lax.fori_loop(0, rows // 16, body, 0)


def scatter_kernel(shapes, *refs):
    count = len(shapes)
    grads, vec_ref = refs[:count], refs[count]
    outs, vec_out = refs[count + 1 : 2 * count + 1], refs[2 * count + 1]
    scratch = list(refs[2 * count + 2 :])
    groups = [scratch[i * count : (i + 1) * count] for i in range(8)]
    acc, got0, got1, got2, got3, got4, final, got5 = groups
    vec_acc, vgot0, vgot1, vgot2, vgot3, vgot4, send_sem, recv_sem, local_sem = scratch[8 * count :]
    at = Place()
    at.barrier()
    started = []

    def send(src, dst, m, k, partner):
        copy = pltpu.make_async_remote_copy(
            src_ref=src,
            dst_ref=dst,
            send_sem=send_sem.at[m, k],
            recv_sem=recv_sem.at[m, k],
            device_id=(partner,),
            device_id_type=MESH,
        )
        copy.start()
        started.append(copy)
        return copy

    def lanes(m, core):
        half = shapes[m][1] // 2
        return pl.ds(pl.multiple_of(core * half, 128), half)

    def block(m, z1, z0, yx):
        if m == count:
            return vec_acc.at[z1, z0, yx]
        rows = 2 * shapes[m][0]
        return acc[m].at[z1, z0, pl.ds(pl.multiple_of(yx * rows, 16), rows)]

    every = slice(None)
    flights = {}
    got = {
        1: lambda m: vgot1 if m == count else got1[m],
        2: lambda m: vgot2 if m == count else got2[m],
        3: lambda m: vgot3 if m == count else got3[m],
        4: lambda m: vgot4 if m == count else got4[m],
    }

    def add(m, dst, src):
        if m == count:
            dst[...] += src[...]
        else:
            add_rows(dst, src, dst.shape[0])

    def finish(m, k):
        for copy in flights[m, k]:
            copy.wait_recv()
        if k == 0:
            flights[m, "local"].wait()
            if m == count:
                vec_acc[...] += vgot0[...]
            else:
                for z1 in range(2):
                    for z0 in range(2):
                        add_rows(acc[m].at[z1, z0], got0[m].at[z1, z0], 8 * shapes[m][0])
        elif k == 1:
            for j in range(2):
                for z1 in range(2):
                    for z0 in range(2):
                        add(m, block(m, z1, z0, at.along_second(at.bit1, j)), got[1](m).at[j, z1, z0])
        elif k == 2:
            for z1 in range(2):
                for z0 in range(2):
                    add(m, block(m, z1, z0, at.here), got[2](m).at[z1, z0])
        elif k == 3:
            for z1 in range(2):
                add(m, block(m, z1, at.z0, at.here), got[3](m).at[z1])
        elif k == 4:
            mine = block(m, at.z1, at.z0, at.here)
            if m == count:
                vec_out[...] = mine[...] + vgot4[...]
            else:
                rows = shapes[m][0]
                total = mine[...].astype(jnp.float32) + got4[m][...].astype(jnp.float32)
                final[m][0] = total[:rows]
                final[m][1] = total[rows:]
        elif m < count:
            half = shapes[m][1] // 2
            for core in range(2):

                @pl.when(at.c == core)
                def _():
                    outs[m][:, core * half : (core + 1) * half] = final[m][core]
                    outs[m][:, (1 - core) * half : (2 - core) * half] = got5[m][...]

    def start(m, k):
        if k == 0:
            if m == count:
                local = pltpu.make_async_copy(vec_ref.at[:, :, :, at.c], vec_acc, local_sem.at[m])
                local.start()
                flights[m, 0] = [send(vec_ref.at[:, :, :, 1 - at.c], vgot0, m, 0, at.core)]
            else:
                flights[m, 0] = [send(grads[m].at[:, :, :, lanes(m, 1 - at.c)], got0[m], m, 0, at.core)]
                local = pltpu.make_async_copy(grads[m].at[:, :, :, lanes(m, at.c)], acc[m], local_sem.at[m])
                local.start()
            flights[m, "local"] = local
        elif k == 1:
            flights[m, 1] = [
                send(
                    block(m, every, every, at.along_second(1 - at.bit1, j)),
                    got[1](m).at[j],
                    m,
                    1 + j,
                    at.first,
                )
                for j in range(2)
            ]
        elif k == 2:
            away = at.along_second(at.bit1, 1 - at.bit2)
            flights[m, 2] = [send(block(m, every, every, away), got[2](m), m, 3, at.second)]
        elif k == 3:
            flights[m, 3] = [send(block(m, every, 1 - at.z0, at.here), got[3](m), m, 4, at.near)]
        elif k == 4:
            flights[m, 4] = [send(block(m, 1 - at.z1, at.z0, at.here), got[4](m), m, 5, at.far)]
        else:
            flights[m, 5] = [] if m == count else [send(final[m].at[1 - at.c], got5[m], m, 6, at.core)]

    order = list(range(count)) + [count]
    for step in range(len(order) + 6):
        for k in range(6, -1, -1):
            if 0 <= step - k < len(order):
                m = order[step - k]
                if k > 0:
                    finish(m, k - 1)
                if k < 6:
                    start(m, k)
    for copy in started:
        copy.wait_send()


def scatter_all(grads, vec):
    shapes = [(g.shape[2] // 8, g.shape[3]) for g in grads]
    count = len(shapes)
    any_space = pl.BlockSpec(memory_space=pl.ANY)
    vmem = pl.BlockSpec(memory_space=pltpu.VMEM)
    bf16, f32 = jnp.bfloat16, jnp.float32
    scratch = [pltpu.VMEM((2, 2, 8 * r, c // 2), bf16) for r, c in shapes] * 2
    scratch += [pltpu.VMEM((2, 2, 2, 2 * r, c // 2), bf16) for r, c in shapes]
    scratch += [pltpu.VMEM((2, 2, 2 * r, c // 2), bf16) for r, c in shapes]
    scratch += [pltpu.VMEM((2, 2 * r, c // 2), bf16) for r, c in shapes]
    scratch += [pltpu.VMEM((2 * r, c // 2), bf16) for r, c in shapes]
    scratch += [pltpu.VMEM((2, r, c // 2), f32) for r, c in shapes]
    scratch += [pltpu.VMEM((r, c // 2), f32) for r, c in shapes]
    scratch += [
        pltpu.VMEM((2, 2, 4, 8, 128), f32),
        pltpu.VMEM((2, 2, 4, 8, 128), f32),
        pltpu.VMEM((2, 2, 2, 8, 128), f32),
        pltpu.VMEM((2, 2, 8, 128), f32),
        pltpu.VMEM((2, 8, 128), f32),
        pltpu.VMEM((8, 128), f32),
        pltpu.SemaphoreType.DMA((count + 1, 7)),
        pltpu.SemaphoreType.DMA((count + 1, 7)),
        pltpu.SemaphoreType.DMA((count + 1,)),
    ]
    out_shape = [jax.ShapeDtypeStruct((r, c), f32) for r, c in shapes]
    out_shape.append(jax.ShapeDtypeStruct((8, 128), f32))

    def body(*refs):
        scatter_kernel(shapes, *refs)

    return pl.pallas_call(
        body,
        out_shape=out_shape,
        in_specs=[any_space] * (count + 1),
        out_specs=[vmem] * (count + 1),
        scratch_shapes=scratch,
        compiler_params=pltpu.CompilerParams(
            collective_id=1, has_side_effects=True, vmem_limit_bytes=VMEM_BYTES
        ),
        name="scatter_grads",
    )(*grads, vec)


def on_links(matrices, vectors):
    values = sum(v.shape[0] for v in vectors)
    return (
        lax.axis_size("fsdp") == 32
        and values <= 1024
        and all(m.shape[0] % 8 == 0 and m.shape[1] % 256 == 0 for m in matrices)
    )


def split_vectors(joined, sizes):
    pieces, start = [], 0
    for size in sizes:
        pieces.append(joined[:, start : start + size].reshape(-1))
        start += size
    return pieces


def gather_params(matrices, vectors):
    sizes = [v.shape[0] for v in vectors]
    joined = jnp.concatenate(vectors).astype(jnp.float32)
    if on_links(matrices, vectors):
        tile = jnp.pad(joined, (0, 1024 - joined.shape[0])).reshape(8, 128)
        *whole, whole_vec = gather_all(matrices, tile)
        whole = [w.reshape(-1, w.shape[3]) for w in whole]
        return whole, split_vectors(whole_vec.reshape(32, 1024), sizes)
    whole = [lax.all_gather(m, "fsdp", axis=0, tiled=True) for m in matrices]
    return whole, split_vectors(lax.all_gather(joined, "fsdp", axis=0), sizes)


def scatter_grads(grads, vector_grads):
    devices = lax.axis_size("fsdp")
    sizes = [v.shape[0] // devices for v in vector_grads]
    joined = jnp.concatenate([v.reshape(devices, -1) for v in vector_grads], 1)
    blocks = [jax.ShapeDtypeStruct((g.shape[0] // devices, g.shape[1]), g.dtype) for g in grads]
    parts = [jax.ShapeDtypeStruct((size,), joined.dtype) for size in sizes]
    if on_links(blocks, parts):
        tiles = jnp.pad(joined, ((0, 0), (0, 1024 - joined.shape[1]))).reshape(2, 2, 4, 2, 8, 128)
        *sums, vec = scatter_all([g.reshape(2, 2, -1, g.shape[1]) for g in grads], tiles)
        vec = vec.reshape(1, 1024)
    else:
        sums = [
            lax.psum_scatter(g.astype(jnp.float32), "fsdp", scatter_dimension=0, tiled=True) for g in grads
        ]
        vec = lax.psum_scatter(joined, "fsdp", scatter_dimension=0, tiled=True)
    return sums, split_vectors(vec, sizes)


def on_device(
    patches,
    visible_index,
    segments,
    cotangent,
    enc_norm1_gain,
    enc_norm1_bias,
    enc_qkv,
    enc_query_bias,
    enc_value_bias,
    enc_out,
    enc_out_bias,
    enc_norm2_gain,
    enc_norm2_bias,
    enc_up,
    enc_up_bias,
    enc_down,
    enc_down_bias,
    embed_weight,
    embed_bias,
    mask_token,
    dec_norm1_gain,
    dec_norm1_bias,
    dec_qkv,
    dec_query_bias,
    dec_value_bias,
    dec_out,
    dec_out_bias,
    dec_norm2_gain,
    dec_norm2_bias,
    dec_up,
    dec_up_bias,
    dec_down,
    dec_down_bias,
):
    seq_count = segments.shape[0] // ROW
    seg_ids = segments.reshape(seq_count, ROW)
    vis_slots = visible_index.reshape(seq_count, VIS)
    enc_seg = jnp.take_along_axis(seg_ids, vis_slots, 1)
    seq_index = jnp.arange(seq_count, dtype=jnp.int32)[:, None]
    matrices = (enc_qkv, enc_out, enc_up, enc_down, embed_weight, dec_qkv, dec_out, dec_up, dec_down)
    vectors = (
        enc_norm1_gain,
        enc_norm1_bias,
        enc_query_bias,
        enc_value_bias,
        enc_out_bias,
        enc_norm2_gain,
        enc_norm2_bias,
        enc_up_bias,
        enc_down_bias,
        embed_bias,
        mask_token,
        dec_norm1_gain,
        dec_norm1_bias,
        dec_query_bias,
        dec_value_bias,
        dec_out_bias,
        dec_norm2_gain,
        dec_norm2_bias,
        dec_up_bias,
        dec_down_bias,
    )
    whole, whole_vec = gather_params(matrices, vectors)
    (ng1, nb1, qb, vb, ob, ng2, nb2, ub, db, eb, mask, dng1, dnb1, dqb, dvb, dob, dng2, dnb2, dub, ddb) = whole_vec
    enc_full = (ng1, nb1, whole[0], qb, vb, whole[1], ob, ng2, nb2, whole[2], ub, whole[3], db)
    dec_full = (dng1, dnb1, whole[5], dqb, dvb, whole[6], dob, dng2, dnb2, whole[7], dub, whole[8], ddb)
    hidden, enc_saved = block_forward(widen(patches), enc_full, enc_seg, HEADS)
    hidden_low = hidden.astype(jnp.bfloat16)
    embedded = jnp.dot(hidden_low, whole[4], preferred_element_type=jnp.float32) + eb
    embedded = embedded.reshape(seq_count, VIS, DD)
    dec_in = (
        jnp.broadcast_to(mask, (seq_count, ROW, DD)).at[seq_index, vis_slots].set(embedded)
    )
    dec_in = dec_in.reshape(seq_count * ROW, DD)
    decoded, dec_saved = block_forward(dec_in, dec_full, seg_ids, DHEADS)
    grad_dec_in, dec_grads = block_backward(
        widen(cotangent), dec_full, seg_ids, DHEADS, dec_saved
    )
    grad_dec_in = grad_dec_in.reshape(seq_count, ROW, DD)
    shown_slots = jnp.zeros((seq_count, ROW), jnp.float32).at[seq_index, vis_slots].set(1.0)
    grad_mask = jnp.sum((1.0 - shown_slots)[:, :, None] * grad_dec_in, (0, 1))
    grad_embedded = grad_dec_in[seq_index, vis_slots].reshape(seq_count * VIS, DD)
    grad_embed_b = jnp.sum(grad_embedded, 0)
    grad_embedded_low = grad_embedded.astype(jnp.bfloat16)
    grad_embed_w = jnp.einsum(
        "rd,re->de", hidden_low, grad_embedded_low, preferred_element_type=jnp.float32
    ).astype(jnp.bfloat16)
    grad_hidden = jnp.einsum(
        "re,de->rd", grad_embedded_low, whole[4], preferred_element_type=jnp.float32
    )
    grad_patches, enc_grads = block_backward(grad_hidden, enc_full, enc_seg, HEADS, enc_saved)
    e, d = enc_grads, dec_grads
    matrix_sums, vector_sums = scatter_grads(
        (e[2], e[5], e[9], e[11], grad_embed_w, d[2], d[5], d[9], d[11]),
        (e[0], e[1], e[3], e[4], e[6], e[7], e[8], e[10], e[12], grad_embed_b, grad_mask)
        + (d[0], d[1], d[3], d[4], d[6], d[7], d[8], d[10], d[12]),
    )
    m, v = matrix_sums, vector_sums
    return (
        (decoded.astype(jnp.bfloat16), grad_patches)
        + (v[0], v[1], m[0], v[2], v[3], m[1], v[4], v[5], v[6], m[2], v[7], m[3], v[8])
        + (m[4], v[9], v[10])
        + (v[11], v[12], m[5], v[13], v[14], m[6], v[15], v[16], v[17], m[7], v[18], m[8], v[19])
    )


def solution(mesh):
    return jax.shard_map(
        on_device,
        mesh=mesh,
        in_specs=(
            P("fsdp", None),
            P("fsdp"),
            P("fsdp"),
            P("fsdp", None),
            P("fsdp"),
            P("fsdp"),
            P("fsdp", None),
            P("fsdp"),
            P("fsdp"),
            P("fsdp", None),
            P("fsdp"),
            P("fsdp"),
            P("fsdp"),
            P("fsdp", None),
            P("fsdp"),
            P("fsdp", None),
            P("fsdp"),
            P("fsdp", None),
            P("fsdp"),
            P("fsdp"),
            P("fsdp"),
            P("fsdp"),
            P("fsdp", None),
            P("fsdp"),
            P("fsdp"),
            P("fsdp", None),
            P("fsdp"),
            P("fsdp"),
            P("fsdp"),
            P("fsdp", None),
            P("fsdp"),
            P("fsdp", None),
            P("fsdp"),
        ),
        out_specs=(
            P("fsdp", None),
            P("fsdp", None),
            P("fsdp"),
            P("fsdp"),
            P("fsdp", None),
            P("fsdp"),
            P("fsdp"),
            P("fsdp", None),
            P("fsdp"),
            P("fsdp"),
            P("fsdp"),
            P("fsdp", None),
            P("fsdp"),
            P("fsdp", None),
            P("fsdp"),
            P("fsdp", None),
            P("fsdp"),
            P("fsdp"),
            P("fsdp"),
            P("fsdp"),
            P("fsdp", None),
            P("fsdp"),
            P("fsdp"),
            P("fsdp", None),
            P("fsdp"),
            P("fsdp"),
            P("fsdp"),
            P("fsdp", None),
            P("fsdp"),
            P("fsdp", None),
            P("fsdp"),
        ),
        check_vma=False,
    )
```

```python
import types
from typing import Any, NamedTuple

import jax
import jax.numpy as jnp
from jax import lax
from jax.experimental import pallas as pl
from jax.experimental.pallas import tpu as pltpu
from jax.sharding import PartitionSpec as P

AXIS = "fsdp"
MESH = pl.DeviceIdType.MESH
VMEM_BYTES = 63 * 2**20
F32, BF16 = jnp.float32, jnp.bfloat16
EPSILON = 1e-06
HEADS, DHEADS = 12, 16
LOG2E = 1.4426950408889634
APART = -(2.0**100)
ROOT_HALF = 0.7071067811865476
ROOT_TWO_PI = 0.3989422804014327
VEC_ROWS = 24
PIECES = 5
DEC_PATIENCE, ENC_PATIENCE = 3, 4
ENC_UP_ROW, DEC_UP_ROW = 18, 19
DD = 512
ROW = 529
VIS = 384


class Arguments(NamedTuple):
    patches: Any
    visible_index: Any
    segments: Any
    cotangent: Any
    enc_norm1_gain: Any
    enc_norm1_bias: Any
    enc_qkv: Any
    enc_query_bias: Any
    enc_value_bias: Any
    enc_out: Any
    enc_out_bias: Any
    enc_norm2_gain: Any
    enc_norm2_bias: Any
    enc_up: Any
    enc_up_bias: Any
    enc_down: Any
    enc_down_bias: Any
    embed_weight: Any
    embed_bias: Any
    mask_token: Any
    dec_norm1_gain: Any
    dec_norm1_bias: Any
    dec_qkv: Any
    dec_query_bias: Any
    dec_value_bias: Any
    dec_out: Any
    dec_out_bias: Any
    dec_norm2_gain: Any
    dec_norm2_bias: Any
    dec_up: Any
    dec_up_bias: Any
    dec_down: Any
    dec_down_bias: Any


def matrices_of(a):
    return (
        a.enc_qkv,
        a.enc_out,
        a.enc_up,
        a.enc_down,
        a.embed_weight,
        a.dec_qkv,
        a.dec_out,
        a.dec_up,
        a.dec_down,
    )


def vectors_of(a):
    return (
        a.enc_norm1_gain,
        a.enc_norm1_bias,
        a.enc_query_bias,
        a.enc_value_bias,
        a.enc_out_bias,
        a.enc_norm2_gain,
        a.enc_norm2_bias,
        a.enc_down_bias,
        a.embed_bias,
        a.mask_token,
        a.dec_norm1_gain,
        a.dec_norm1_bias,
        a.dec_query_bias,
        a.dec_value_bias,
        a.dec_out_bias,
        a.dec_norm2_gain,
        a.dec_norm2_bias,
        a.dec_down_bias,
        a.enc_up_bias,
        a.dec_up_bias,
    )


def encoder_of(a):
    return (
        a.enc_norm1_gain,
        a.enc_norm1_bias,
        a.enc_qkv,
        a.enc_query_bias,
        a.enc_value_bias,
        a.enc_out,
        a.enc_out_bias,
        a.enc_norm2_gain,
        a.enc_norm2_bias,
        a.enc_up,
        a.enc_up_bias,
        a.enc_down,
        a.enc_down_bias,
    )


def decoder_of(a):
    return (
        a.dec_norm1_gain,
        a.dec_norm1_bias,
        a.dec_qkv,
        a.dec_query_bias,
        a.dec_value_bias,
        a.dec_out,
        a.dec_out_bias,
        a.dec_norm2_gain,
        a.dec_norm2_bias,
        a.dec_up,
        a.dec_up_bias,
        a.dec_down,
        a.dec_down_bias,
    )


def in_order(matrices, vectors):
    places = Arguments(*range(len(Arguments._fields)))
    found = dict(zip(matrices_of(places) + vectors_of(places), tuple(matrices) + tuple(vectors)))
    return tuple(found[place] for place in sorted(found))


def dot(a, b):
    return jnp.dot(a, b, preferred_element_type=F32)


def dot_nt(a, b):
    return lax.dot_general(a, b, (((1,), (1,)), ((), ())), preferred_element_type=F32)


def at_tile(j, size):
    return pl.ds(pl.multiple_of(j * size, size), size)


def loop(count, body):
    def step(i, carry):
        body(i)
        return carry

    lax.fori_loop(0, count, step, 0)


class Place:
    def __init__(self):
        me = lax.axis_index(AXIS)
        self.c = c = lax.rem(me, 2)
        x = lax.rem(me // 2, 2)
        y = lax.rem(me // 4, 2)
        self.z = lax.rem(me // 8, 4)
        self.stride1 = 1 + c
        self.stride2 = 2 - c
        self.bit1 = x * (1 - c) + y * c
        self.bit2 = y * (1 - c) + x * c
        self.here = 2 * y + x
        self.core = me + 1 - 2 * c
        self.first = me + 2 * self.stride1 * (1 - 2 * self.bit1)
        self.second = me + 2 * self.stride2 * (1 - 2 * self.bit2)
        self.zs = [lax.rem(self.z + i, 4) for i in range(4)]
        self.columns = [me + 8 * (z - self.z) for z in self.zs]

    def yx(self, flip1, flip2):
        bit1 = 1 - self.bit1 if flip1 else self.bit1
        bit2 = 1 - self.bit2 if flip2 else self.bit2
        return bit1 * self.stride1 + bit2 * self.stride2

    def barrier(self):
        barrier = pltpu.get_barrier_semaphore()
        partners = [self.core, self.first, self.second] + self.columns[1:]
        for partner in partners:
            pl.semaphore_signal(barrier, inc=1, device_id=(partner,), device_id_type=MESH)
        pl.semaphore_wait(barrier, len(partners))


def padded(rows):
    return -(-rows // 16) * 16


def chunks_of(shapes):
    out = []
    for m, (rows, columns) in enumerate(shapes):
        half = columns // 2
        if 32 * rows * columns * 2 <= 3 * 2**20:
            out.append((m, 0, 2 * rows, 0, half))
        elif rows % 16 == 0:
            out.append((m, 0, rows, 0, half))
            out.append((m, rows, rows, 0, half))
        else:
            low = half // 256 * 128
            out.append((m, 0, 2 * rows, 0, half - low))
            out.append((m, 0, 2 * rows, half - low, low))
    return out


class Gather:
    def __init__(self, at, shapes, shards, wholes, vec_tile, vec_whole, sent, got, send_sem, recv_sem):
        self.at, self.shapes, self.shards, self.wholes = at, shapes, shards, wholes
        self.vec_tile, self.vec_whole = vec_tile, vec_whole
        self.sent, self.got = sent, got
        self.send_sem, self.recv_sem = send_sem, recv_sem
        self.chunks = [None] + chunks_of(shapes)
        self.started = []
        self.flights = {}

    def send(self, src, dst, chunk, slot, partner):
        copy = pltpu.make_async_remote_copy(
            src_ref=src,
            dst_ref=dst,
            send_sem=self.send_sem.at[chunk, slot],
            recv_sem=self.recv_sem.at[chunk, slot],
            device_id=(partner,),
            device_id_type=MESH,
        )
        copy.start()
        self.started.append(copy)
        return copy

    def view(self, chunk, z, yx):
        if chunk == 0:
            return self.vec_whole.at[z, yx, self.at.c]
        m, row, rows, lane, lanes = self.chunks[chunk]
        chip_rows, half = 2 * self.shapes[m][0], self.shapes[m][1] // 2
        start = pl.multiple_of(yx * chip_rows + row, 16)
        first = pl.multiple_of(self.at.c * half + lane, 128)
        return self.wholes[m].at[z, pl.ds(start, rows), pl.ds(first, lanes)]

    def my_half(self, m, mine):
        half = self.shapes[m][1] // 2
        low, high = self.shards[m][:, :half].astype(F32), self.shards[m][:, half:].astype(F32)
        return jnp.where(self.at.c == 0, low, high) if mine else jnp.where(self.at.c == 0, high, low)

    def swap(self, m):
        rows, columns = self.shapes[m]
        value = self.my_half(m, False)
        extra = padded(rows) - rows
        if extra:
            value = jnp.concatenate([value, jnp.zeros((extra, columns // 2), F32)], 0)
        self.sent[m][...] = value.astype(BF16)
        self.flights["swap", m] = self.send(self.sent[m], self.got[m], len(self.chunks) + m, 0, self.at.core)

    def place(self, m):
        at, (rows, columns) = self.at, self.shapes[m]
        self.flights["swap", m].wait_recv()
        other = self.got[m][...].astype(F32)[:rows]
        mine = self.my_half(m, True)
        both = jnp.concatenate([jnp.where(at.c == 0, mine, other), jnp.where(at.c == 0, other, mine)], 0)
        half = columns // 2
        lanes = pl.ds(pl.multiple_of(at.c * half, 128), half)
        row = pl.ds(pl.multiple_of(at.here * 2 * rows, 16), 2 * rows)
        self.wholes[m][at.z, row, lanes] = both.astype(BF16)

    def stage(self, chunk, k):
        at, flights = self.at, self.flights
        every = slice(None)
        if k == 0:
            if chunk == 0:
                self.vec_whole[at.z, at.here, at.c] = self.vec_tile[...]
            elif self.chunks[chunk][1] == 0 and self.chunks[chunk][3] == 0:
                self.place(self.chunks[chunk][0])
            own = self.view(chunk, at.z, at.here)
            flights[chunk, 0] = [self.send(own, own, chunk, i, at.columns[i]) for i in range(1, 4)]
        elif k == 1:
            for copy in flights[chunk, 0]:
                copy.wait_recv()
            part = self.view(chunk, every, at.here)
            flights[chunk, 1] = [
                self.send(part, part, chunk, 4, at.second),
                self.send(part, part, chunk, 5, at.first),
            ]
            flights[chunk, "core"] = [self.send(part, part, chunk, 7, at.core)]
        elif k == 2:
            flights[chunk, 1][0].wait_recv()
            part = self.view(chunk, every, at.yx(False, True))
            flights[chunk, 2] = self.send(part, part, chunk, 6, at.first)
            flights[chunk, "core"].append(self.send(part, part, chunk, 8, at.core))
            flights[chunk, 1][1].wait_recv()
            part = self.view(chunk, every, at.yx(True, False))
            flights[chunk, "core"].append(self.send(part, part, chunk, 9, at.core))
        elif k == 3:
            flights[chunk, 2].wait_recv()
            part = self.view(chunk, every, at.yx(True, True))
            flights[chunk, "core"].append(self.send(part, part, chunk, 10, at.core))
        else:
            for copy in flights[chunk, "core"]:
                copy.wait_recv()

    def steps(self):
        for m in range(len(self.shapes)):
            self.swap(m)
        yield None
        count = len(self.chunks)
        lags = (0, 2, 3, 4, 5)
        for step in range(count + lags[-1]):
            done = None
            for k, lag in enumerate(lags):
                if 0 <= step - lag < count:
                    self.stage(step - lag, k)
                    if k == 4:
                        done = step - lag
            yield done

    def finish(self):
        for copy in self.started:
            copy.wait_send()


def spread(tiles, width, out_width):
    lane = lax.broadcasted_iota(jnp.int32, tiles[0].shape, 1)
    whole = [jnp.zeros(tiles[0].shape, F32) for _ in range(out_width // 128)]
    for d, tile in enumerate(tiles):
        t, shift = divmod(d * width, 128)
        rolled = pltpu.roll(tile, shift, 1) if shift else tile
        over = shift + width - 128
        if over <= 0:
            whole[t] = whole[t] + rolled
        else:
            whole[t] = whole[t] + jnp.where(lane >= shift, rolled, 0.0)
            whole[t + 1] = whole[t + 1] + jnp.where(lane < over, rolled, 0.0)
    return jnp.concatenate(whole, 1)


def normed_rows(rows, gain, shift):
    centred = rows - jnp.mean(rows, -1, keepdims=True)
    variance = jnp.mean(centred * centred, -1, keepdims=True)
    return centred * lax.rsqrt(variance + EPSILON) * gain + shift


def norm_into(read, gain, shift, out, out_t, length, width):
    chunk = 96 if length % 96 == 0 else 68 * 8 // 17
    loop(
        length // chunk,
        lambda i: out.__setitem__(
            (at_tile(i, chunk), slice(None)), normed_rows(read(at_tile(i, chunk)), gain(), shift()).astype(BF16)
        ),
    )
    turn(out, out_t, width)


def turn(src, dst, width):
    def body(j):
        dst[at_tile(j, 128), :] = src[:, at_tile(j, 128)].T

    loop(width // 128, body)


def turn_back(src, dst, width):
    def body(j):
        dst[:, at_tile(j, 128)] = src[at_tile(j, 128), :].T

    loop(width // 128, body)


def column_tile(whole, j, size):
    tile = whole[:, :, at_tile(j, size)]
    return tile.reshape(tile.shape[0] * tile.shape[1], size)


def forward_block(b, read, length, width, heads, vec, up_bias, whole, finish):
    head = width // heads
    per = 128 // head
    scale = head ** (-0.5) * LOG2E
    size = 256

    def row(index, j=None):
        if j is None:
            return b.vec[index : index + 1, :]
        return b.vec[index : index + 1, at_tile(j, size)]

    norm_into(read, lambda: row(vec.gain1), lambda: row(vec.bias1), b.h, b.hT, length, width)
    yield "qkv"
    tiles = width // size

    def project(third, key, out, out_t):
        def body(j):
            value = dot(b.h[...], column_tile(whole.qkv, third * tiles + j, size))
            if key is not None:
                value = value + row(key, j)
            value = value.astype(BF16)
            out[:, at_tile(j, size)] = value
            out_t[at_tile(j, size), :] = value.T

        loop(tiles, body)

    project(0, vec.bq, b.q, b.qT)
    yield None
    project(1, None, b.k, b.kT)
    yield None
    project(2, vec.bv, b.v, b.vT)
    yield None

    def attend(h):
        group = at_tile(h // per, 128)
        lane = lax.broadcasted_iota(jnp.int32, (length, 128), 1) // head
        keys = jnp.where(lane == lax.rem(h, per), b.k[:, group], jnp.zeros((), BF16))
        scores = dot(keys, b.qT[group, :]) * scale + b.apart[...]
        top = jnp.max(scores, 0, keepdims=True)
        expo = jnp.exp2(scores - top)
        total = jnp.sum(expo, 0, keepdims=True)
        probs = (expo * (1.0 / total)).astype(BF16)
        mine = at_tile(h, head)
        b.oT[mine, :] = dot(b.vT[mine, :], probs).astype(BF16)
        b.lse[h] = top + jnp.log2(total)

    parts = 4
    for part in range(parts):
        loop(heads // parts, lambda i, part=part: attend(i + part * (heads // parts)))
        yield None
    turn_back(b.oT, b.h, width)
    yield "out"

    def middle(j):
        b.v1[:, at_tile(j, size)] = (
            read(slice(None), at_tile(j, size)) + dot(b.h[...], column_tile(whole.out, j, size)) + row(vec.bo, j)
        )

    loop(tiles, middle)
    norm_into(
        lambda rows: b.v1[rows, :], lambda: row(vec.gain2), lambda: row(vec.bias2), b.h, b.h2T, length, width
    )
    yield "up"

    def lift(j):
        u = dot(b.h[...], column_tile(whole.up, j, size)) + up_bias[:, at_tile(j, size)]
        share = 0.5 + 0.5 * lax.erf(u * ROOT_HALF)
        slope = share + u * (jnp.exp2(u * u * (-0.5 * LOG2E)) * ROOT_TWO_PI)
        a = (u * share).astype(BF16)
        b.a[:, at_tile(j, size)] = a
        b.aT[at_tile(j, size), :] = a.T
        b.slope[:, at_tile(j, size)] = slope.astype(BF16)

    ups = b.a.shape[1] // size
    for part in range(4):
        loop(ups // 4, lambda i, part=part: lift(i + part * (ups // 4)))
        yield None
    yield "down"

    def drop(j):
        finish(
            j,
            b.v1[:, at_tile(j, size)] + dot(b.a[...], column_tile(whole.down, j, size)) + row(vec.bd, j),
        )

    loop(tiles, drop)
    yield None


class VecRows(NamedTuple):
    gain1: int
    bias1: int
    bq: int
    bv: int
    bo: int
    gain2: int
    bias2: int
    bd: int


ENC_VEC, DEC_VEC = VecRows(*range(8)), VecRows(*range(2, 10))


class Weights(NamedTuple):
    qkv: Any
    out: Any
    up: Any
    down: Any


class Own(NamedTuple):
    h: Any
    a: Any
    apart: Any


class Saved(NamedTuple):
    hT: Any
    q: Any
    k: Any
    v: Any
    qT: Any
    kT: Any
    vT: Any
    lse: Any
    oT: Any
    v1: Any
    h2T: Any
    aT: Any
    slope: Any


class Read(NamedTuple):
    slope: Any
    aT: Any
    h2T: Any
    v1: Any
    oT: Any
    q: Any
    k: Any
    v: Any
    qT: Any
    kT: Any
    lse: Any
    apart: Any
    hT: Any


class Back(NamedTuple):
    g: Any
    gz: Any
    gu: Any
    acc: Any
    go: Any
    goT: Any
    dqT: Any
    dk: Any
    dv: Any
    gq0: Any
    gq1: Any
    gq2: Any


class VecBufs(NamedTuple):
    tiles: Any
    got0: Any
    got1: Any
    got2: Any
    got3: Any
    sum: Any


def fill(space, kind, refs):
    vars(space).update(zip(kind._fields, refs))
    return space


def fields(kind):
    return len(kind._fields)


def block_buffers(length, width, ff, heads):
    wide, tall = ((length, width), BF16), ((width, length), BF16)
    own = Own(wide, ((length, ff), BF16), ((length, length), F32))
    saved = Saved(
        tall,
        wide,
        wide,
        wide,
        tall,
        tall,
        tall,
        ((heads, 1, length), F32),
        tall,
        ((length, width), F32),
        tall,
        ((ff, length), BF16),
        ((length, ff), BF16),
    )
    return own, saved


def forward_kernel(cfg, refs):
    shapes, sizes, length, slots, padded_slots = cfg
    count = len(shapes)
    it = iter(refs)

    def take(n):
        return [next(it) for _ in range(n)]

    shards = take(count)
    vectors = take(len(sizes))
    patches, index_ref, seg_ref = take(3)
    wholes_out = take(count)
    enc_vec_out, dec_vec_out = take(2)
    enc_saved_out = take(fields(Saved))
    dec_saved_out = take(fields(Saved))
    hid_t_out, dec_in_out, enc_apart_out, dec_apart_out, shown_out, shown_t_out, decoded_out = take(7)
    wholes = take(count)
    sent, got = take(count), take(count)
    vec_tile, vec_whole = take(2)
    enc, dec = types.SimpleNamespace(), types.SimpleNamespace()
    for block in (enc, dec):
        fill(block, Own, take(fields(Own)))
        fill(block, Saved, take(fields(Saved)))
    enc.vec, dec.vec, enc_up, dec_up, hid_t, dec_in, shown, shown_t = take(8)
    send_sem, recv_sem, out_sem = take(3)

    at = Place()
    at.barrier()
    gather = Gather(at, shapes, shards, wholes, vec_tile, vec_whole, sent, got, send_sem, recv_sem)
    outgoing = []

    def put(src, dst):
        copy = pltpu.make_async_copy(src, dst, out_sem.at[len(outgoing)])
        copy.start()
        outgoing.append(copy)

    vec_tile[...] = jnp.zeros((VEC_ROWS, 128), F32)
    for k, ref in enumerate(vectors):
        vec_tile[k : k + 1, : sizes[k]] = ref[...].astype(F32)

    def compute():
        index_row = index_ref[...]
        slot = lax.broadcasted_iota(jnp.int32, (padded_slots, length), 0)
        hit = slot == index_row
        shown[...] = jnp.where(hit, 1.0, 0.0).astype(BF16)
        seg_row = seg_ref[...].astype(F32)
        seg_col = jnp.broadcast_to(seg_row, (128, padded_slots)).T[:, :1]
        enc_seg_row = jnp.sum(jnp.where(hit, seg_col, 0.0), 0, keepdims=True)
        enc_seg_col = jnp.broadcast_to(enc_seg_row, (128, length)).T[:, :1]
        enc.apart[...] = jnp.where(enc_seg_col == enc_seg_row, 0.0, APART)
        yield None
        dec.apart[...] = jnp.where(seg_col == seg_row, 0.0, APART)
        yield "vec"
        pieces = [vec_whole[z, yx, c] for z in range(4) for yx in range(4) for c in range(2)]
        enc.vec[...] = spread([p[:8] for p in pieces], sizes[0], enc.vec.shape[1])
        dec.vec[...] = spread([p[8:] for p in pieces], sizes[8], dec.vec.shape[1])
        keep = lax.broadcasted_iota(jnp.int32, (8, 128), 0)
        up = [jnp.where(keep == ENC_UP_ROW - 16, p[16:], 0.0) for p in pieces]
        enc_up[...] = jnp.sum(spread(up, sizes[ENC_UP_ROW], enc_up.shape[1]), 0, keepdims=True)
        up = [jnp.where(keep == DEC_UP_ROW - 16, p[16:], 0.0) for p in pieces]
        dec_up[...] = jnp.sum(spread(up, sizes[DEC_UP_ROW], dec_up.shape[1]), 0, keepdims=True)
        put(enc.vec, enc_vec_out)
        put(dec.vec, dec_vec_out)
        put(enc.apart, enc_apart_out)
        put(dec.apart, dec_apart_out)
        put(shown, shown_out)
        turn(shown, shown_t, length)
        put(shown_t, shown_t_out)
        yield None

        def read_patches(rows, lanes=slice(None)):
            return patches[rows, lanes].astype(F32)

        def keep_hidden(j, value):
            low = value.astype(BF16)
            enc.h[:, at_tile(j, 256)] = low
            hid_t[at_tile(j, 256), :] = low.T

        names = Weights._fields
        width = patches.shape[1]
        for need in forward_block(
            enc, read_patches, length, width, HEADS, ENC_VEC, enc_up, Weights(*wholes[:4]), keep_hidden
        ):
            yield None if need is None else names.index(need)
        for key, out in zip(Saved._fields, enc_saved_out):
            put(getattr(enc, key), out)
        put(hid_t, hid_t_out)
        yield 4
        dec_width = dec.vec.shape[1]
        marks = shown[...]
        slot_col = lax.broadcasted_iota(jnp.int32, (padded_slots, 1), 0)
        empty = jnp.where(slot_col < slots, 1.0, 0.0) - jnp.sum(marks.astype(F32), 1, keepdims=True)

        def embed(j):
            value = dot(enc.h[...], column_tile(wholes[4], j, 256)) + dec.vec[0:1, at_tile(j, 256)]
            high = value.astype(BF16)
            low = (value - high.astype(F32)).astype(BF16)
            dec_in[:, at_tile(j, 256)] = (
                dot(marks, high) + dot(marks, low) + empty * dec.vec[1:2, at_tile(j, 256)]
            )

        loop(dec_width // 256, embed)
        put(dec_in, dec_in_out)
        yield None

        def read_in(rows, lanes=slice(None)):
            return dec_in[rows, lanes]

        def keep_decoded(j, value):
            decoded_out[:, at_tile(j, 256)] = value[:slots].astype(BF16)

        for need in forward_block(
            dec, read_in, padded_slots, dec_width, DHEADS, DEC_VEC, dec_up, Weights(*wholes[5:]), keep_decoded
        ):
            yield None if need is None else 5 + names.index(need)
        for key, out in zip(Saved._fields, dec_saved_out):
            put(getattr(dec, key), out)

    last = {"vec": 0}
    for chunk, part in enumerate(gather.chunks):
        if part is not None:
            last[part[0]] = chunk
    ready = -1
    work = compute()
    need = next(work)
    ended = False
    copied = set()
    for done in gather.steps():
        if done is not None:
            ready = done
            for m in range(count):
                if last[m] <= ready and m not in copied:
                    copied.add(m)
                    put(wholes[m], wholes_out[m])
        budget = PIECES
        while not ended and budget > 0 and (need is None or last[need] <= ready):
            try:
                need = next(work)
            except StopIteration:
                ended = True
            budget -= 1
    while not ended:
        try:
            need = next(work)
        except StopIteration:
            ended = True
    gather.finish()
    for copy in outgoing:
        copy.wait()


def forward_all(shards, vectors, patches, index, segments, row):
    shapes = [s.shape for s in shards]
    sizes = [v.shape[0] for v in vectors]
    count = len(shapes)
    length, width = patches.shape
    slots = -(-row // 32) * 32
    dec_width = 32 * sizes[8]
    ff, dec_ff = 32 * sizes[ENC_UP_ROW], 32 * sizes[DEC_UP_ROW]
    enc_own, enc_saved = block_buffers(length, width, ff, HEADS)
    dec_own, dec_saved = block_buffers(slots, dec_width, dec_ff, DHEADS)
    whole_shapes = [((4, 8 * r, c), BF16) for r, c in shapes]
    vec_shapes = [((8, width), F32), ((16, dec_width), F32)]
    extra = [((width, length), BF16), ((slots, dec_width), F32)]
    apart = [((length, length), F32), ((slots, slots), F32)]
    outs = whole_shapes + vec_shapes + list(enc_saved) + list(dec_saved) + extra + apart
    outs += [((slots, length), BF16), ((length, slots), BF16)]
    any_space = pl.BlockSpec(memory_space=pl.ANY)
    vmem = pl.BlockSpec(memory_space=pltpu.VMEM)
    out_specs = [any_space] * len(outs) + [vmem]
    out_shape = [jax.ShapeDtypeStruct(*o) for o in outs] + [jax.ShapeDtypeStruct((row, dec_width), BF16)]
    chunk_count = 1 + len(chunks_of(shapes)) + count
    scratch = whole_shapes + [((padded(r), c // 2), BF16) for r, c in shapes] * 2
    scratch += [((VEC_ROWS, 128), F32), ((4, 4, 2, VEC_ROWS, 128), F32)]
    scratch += list(enc_own) + list(enc_saved)
    scratch += list(dec_own) + list(dec_saved)
    scratch += vec_shapes + [((1, ff), F32), ((1, dec_ff), F32)] + extra + outs[-2:]
    scratch = [pltpu.VMEM(*s) for s in scratch]
    scratch += [
        pltpu.SemaphoreType.DMA((chunk_count, 11)),
        pltpu.SemaphoreType.DMA((chunk_count, 11)),
        pltpu.SemaphoreType.DMA((len(outs),)),
    ]
    cfg = (shapes, sizes, length, row, slots)

    def body(*refs):
        forward_kernel(cfg, refs)

    seg_row = jnp.pad(segments.reshape(1, row), ((0, 0), (0, slots - row)), constant_values=2)
    results = pl.pallas_call(
        body,
        out_shape=out_shape,
        in_specs=[vmem] * (count + len(sizes) + 3),
        out_specs=out_specs,
        scratch_shapes=scratch,
        compiler_params=pltpu.CompilerParams(
            collective_id=0, has_side_effects=True, vmem_limit_bytes=VMEM_BYTES
        ),
        name="gather_forward",
    )(*shards, *[v.reshape(1, -1) for v in vectors], patches, index.reshape(1, length), seg_row)
    it = iter(results)
    take = lambda n: [next(it) for _ in range(n)]
    wholes = take(count)
    enc_vec, dec_vec = take(2)
    enc_kept = fill(types.SimpleNamespace(), Saved, take(fields(Saved)))
    dec_kept = fill(types.SimpleNamespace(), Saved, take(fields(Saved)))
    hid_t, dec_in, enc_kept.apart, dec_kept.apart, shown, shown_t, decoded = take(7)
    return wholes, enc_vec, dec_vec, enc_kept, dec_kept, hid_t, dec_in, shown, shown_t, decoded


class Scatter:
    STAGES = 6

    def __init__(self, at, shapes, grads, outs, bufs, vec, send_sem, recv_sem):
        self.at, self.shapes, self.grads, self.outs = at, shapes, grads, outs
        self.got0, self.got1, self.got2, self.got3, self.final, self.got4 = bufs
        self.vec = vec
        self.send_sem, self.recv_sem = send_sem, recv_sem
        self.started = []
        self.parts = []
        self.begun = 0
        self.order = 0

    def send(self, src, dst, p, slot, partner):
        copy = pltpu.make_async_remote_copy(
            src_ref=src,
            dst_ref=dst,
            send_sem=self.send_sem.at[p, slot],
            recv_sem=self.recv_sem.at[p, slot],
            device_id=(partner,),
            device_id_type=MESH,
        )
        copy.start()
        self.started.append(copy)
        return copy

    def lanes(self, part, core):
        m, lane, lanes = part
        return pl.ds(pl.multiple_of(core * (self.shapes[m][1] // 2) + lane, 128), lanes)

    def block(self, part, z, yx):
        if part is None:
            return self.vec.tiles.at[z, yx, self.at.c]
        rows = 2 * self.shapes[part[0]][0]
        return self.grads[part[0]].at[z, pl.ds(pl.multiple_of(yx * rows, 16), rows), self.lanes(part, self.at.c)]

    def buf(self, key, part, *index):
        if part is None:
            return self.vec[1 + key].at[index] if index else self.vec[1 + key]
        m, lane, lanes = part
        bufs = (self.got0, self.got1, self.got2, self.got3)[key][m]
        rest = (slice(None),) * (len(bufs.shape) - 1 - len(index))
        return bufs.at[index + rest + (pl.ds(lane, lanes),)]

    def add(self, part, dst, src):
        if part is None:
            dst[...] += src[...]
            return
        rows = dst.shape[0]
        step = 48 if rows % 48 == 0 else 32

        def body(i):
            rows_here = at_tile(i, step)
            dst[rows_here, :] = (dst[rows_here, :].astype(F32) + src[rows_here, :].astype(F32)).astype(BF16)

        loop(rows // step, body)

    def advance(self, entry):
        at, every = self.at, slice(None)
        p, part, k, flights = entry.p, entry.part, entry.stage, entry.flights
        for copy in flights:
            copy.wait_recv()
        if k == 0:
            pass
        elif k == 1:
            if part is None:
                own = self.vec.tiles.at[:, :, at.c]
                own[...] += self.vec.got0[...]
            else:
                own = self.grads[part[0]].at[:, :, self.lanes(part, at.c)]
                for z in range(4):
                    self.add(part, own.at[z], self.buf(0, part, z))
        elif k == 2:
            for j in range(2):
                for z in range(4):
                    self.add(part, self.block(part, z, at.bit1 * at.stride1 + j * at.stride2), self.buf(1, part, j, z))
        elif k == 3:
            for z in range(4):
                self.add(part, self.block(part, z, at.here), self.buf(2, part, z))
        elif k == 4:
            total = self.block(part, at.z, at.here)[...].astype(F32)
            for i in range(3):
                total = total + self.buf(3, part, i)[...].astype(F32)
            if part is None:
                self.vec.sum[...] = total
            else:
                m, lane, lanes = part
                rows = self.shapes[m][0]
                self.final[m][0, :, lane : lane + lanes] = total[:rows]
                self.final[m][1, :, lane : lane + lanes] = total[rows:]
        elif part is not None:
            m, lane, lanes = part
            half = self.shapes[m][1] // 2
            here = pl.ds(pl.multiple_of(at.c * half + lane, 128), lanes)
            there = pl.ds(pl.multiple_of((1 - at.c) * half + lane, 128), lanes)
            self.outs[m][:, here] = self.final[m][at.c, :, lane : lane + lanes]
            self.outs[m][:, there] = self.got4[m][:, lane : lane + lanes]
        if k == 0:
            if part is None:
                src, dst = self.vec.tiles.at[:, :, 1 - at.c], self.vec.got0
            else:
                src, dst = self.grads[part[0]].at[:, :, self.lanes(part, 1 - at.c)], self.buf(0, part)
            flights = [self.send(src, dst, p, 0, at.core)]
        elif k == 1:
            away = (1 - at.bit1) * at.stride1
            flights = [
                self.send(
                    self.block(part, every, away + j * at.stride2), self.buf(1, part, j), p, 1 + j, at.first
                )
                for j in range(2)
            ]
        elif k == 2:
            flights = [self.send(self.block(part, every, at.yx(False, True)), self.buf(2, part), p, 3, at.second)]
        elif k == 3:
            flights = [
                self.send(self.block(part, at.zs[i], at.here), self.buf(3, part, i - 1), p, 3 + i, at.columns[i])
                for i in range(1, 4)
            ]
        elif k == 4 and part is not None:
            m, lane, lanes = part
            src = self.final[m].at[1 - at.c, :, pl.ds(lane, lanes)]
            flights = [self.send(src, self.got4[m].at[:, pl.ds(lane, lanes)], p, 7, at.core)]
        else:
            flights = []
        self.order += 1
        vars(entry).update(stage=k + 1, flights=flights, tick=self.begun, order=self.order)

    def emit(self, *parts):
        for part in parts:
            entry = types.SimpleNamespace(p=len(self.parts), part=part, stage=0, flights=[])
            self.parts.append(entry)
            self.advance(entry)

    def flying(self):
        return sorted((e for e in self.parts if e.stage < self.STAGES), key=lambda e: e.order)

    def tick(self, patience):
        self.begun += 1
        for entry in self.flying():
            if self.begun - entry.tick >= patience:
                self.advance(entry)

    def finish(self):
        while self.flying():
            self.advance(self.flying()[0])
        for copy in self.started:
            copy.wait_send()


def scatter_shapes(shapes):
    scratch = [((4, 8 * r, c // 2), BF16) for r, c in shapes]
    scratch += [((2, 4, 2 * r, c // 2), BF16) for r, c in shapes]
    scratch += [((4, 2 * r, c // 2), BF16) for r, c in shapes]
    scratch += [((3, 2 * r, c // 2), BF16) for r, c in shapes]
    scratch += [((2, r, c // 2), F32) for r, c in shapes]
    scratch += [((r, c // 2), F32) for r, c in shapes]
    return scratch


def lane_parts(shapes, m):
    half = shapes[m][1] // 2
    if 32 * shapes[m][0] * shapes[m][1] * 2 <= 3 * 2**20:
        return [(m, 0, half)]
    low = half // 256 * 128
    return [(m, 0, half - low), (m, half - low, low)]


def collect(whole, width, d):
    lane = lax.broadcasted_iota(jnp.int32, (whole.shape[0], 128), 1)
    t, shift = divmod(d * width, 128)
    tile = whole[:, t * 128 : (t + 1) * 128]
    if shift:
        tile = pltpu.roll(tile, 128 - shift, 1)
    if shift + width > 128:
        after = pltpu.roll(whole[:, (t + 1) * 128 : (t + 2) * 128], 128 - shift, 1)
        tile = jnp.where(lane < 128 - shift, tile, after)
    return jnp.where(lane < width, tile, 0.0)


def norm_back(x, gain, grad):
    centred = x - jnp.mean(x, -1, keepdims=True)
    rate = lax.rsqrt(jnp.mean(centred * centred, -1, keepdims=True) + EPSILON)
    unit = centred * rate
    inner = grad * gain
    back = rate * (inner - jnp.mean(inner, -1, keepdims=True) - unit * jnp.mean(inner * unit, -1, keepdims=True))
    return back, grad * unit


def back_buffers(length, width, ff):
    wide, tall = ((length, width), BF16), ((width, length), BF16)
    wide32, tall32 = ((length, width), F32), ((width, length), F32)
    return Back(
        wide32, wide, ((length, ff), BF16), wide32, wide, tall, tall32, wide32, wide32, wide, wide, wide
    )


def row_chunk(length):
    return 96 if length % 96 == 0 else 32


def backward_block(b, need, read, length, width, heads, vec, up_grad, whole, emit):
    head = width // heads
    per = 128 // head
    scale = head ** (-0.5)
    size = 256
    chunk = row_chunk(length)
    ff = b.gu.shape[1]

    def keep(index, value, j=None):
        if j is None:
            b.dvec[index : index + 1, :] = value
        else:
            b.dvec[index : index + 1, at_tile(j, size)] = value

    def low(j):
        value = b.g[:, at_tile(j, size)]
        keep(vec.bd, jnp.sum(value, 0, keepdims=True), j)
        b.gz[:, at_tile(j, size)] = value.astype(BF16)

    loop(width // size, low)
    need("down", "slope", "aT")
    blocks = ff // 4 // size

    def feed(j):
        place = (j // blocks, at_tile(lax.rem(j, blocks), size), slice(None))
        grad = dot_nt(b.gz[...], whole.down[place]) * b.slope[:, at_tile(j, size)].astype(F32)
        up_grad[:, at_tile(j, size)] = jnp.sum(grad, 0, keepdims=True)
        b.gu[:, at_tile(j, size)] = grad.astype(BF16)
        whole.down[place] = dot(b.aT[at_tile(j, size), :], b.gz[...]).astype(BF16)

    count = ff // size
    for part in range(4):
        loop(count // 4, lambda i, part=part: feed(i + part * (count // 4)))
        if part < 3:
            yield
    emit("down")
    yield
    need("up", "h2T")

    def lift(j, first):
        columns = at_tile(j, width)
        tile = whole.up[:, :, columns]
        part = dot_nt(b.gu[:, columns], tile.reshape(width, width))
        b.acc[...] = part if first else b.acc[...] + part

        def grad(i):
            lanes = pl.ds(pl.multiple_of(j * width + i * size, size), size)
            value = dot(b.h2T[...], b.gu[:, lanes]).astype(BF16)
            whole.up[:, :, lanes] = value.reshape(4, width // 4, size)

        loop(width // size, grad)

    lift(0, True)
    yield
    for j in range(1, ff // width):
        lift(j, False)
        if j < ff // width - 1:
            yield
    emit("up")
    yield
    need("v1", "out", "oT")
    zero = jnp.zeros((1, width), F32)

    def norm_two(i, sums):
        rows = at_tile(i, chunk)
        grad = b.acc[rows, :]
        back, terms = norm_back(b.v1[rows, :], b.vec[vec.gain2 : vec.gain2 + 1, :], grad)
        total = b.g[rows, :] + back
        b.g[rows, :] = total
        b.gz[rows, :] = total.astype(BF16)
        return (
            sums[0] + jnp.sum(terms, 0, keepdims=True),
            sums[1] + jnp.sum(grad, 0, keepdims=True),
            sums[2] + jnp.sum(total, 0, keepdims=True),
        )

    gain_sum, shift_sum, out_sum = lax.fori_loop(0, length // chunk, norm_two, (zero, zero, zero))
    keep(vec.gain2, gain_sum)
    keep(vec.bias2, shift_sum)
    keep(vec.bo, out_sum)
    span = width // 2
    for i in range(2):
        tile = whole.out[2 * i : 2 * i + 2].reshape(span, width)
        b.go[:, i * span : (i + 1) * span] = dot_nt(b.gz[...], tile).astype(BF16)

    def out_grad(j):
        value = dot(b.oT[...], b.gz[:, at_tile(j, size)]).astype(BF16)
        whole.out[:, :, at_tile(j, size)] = value.reshape(4, width // 4, size)

    loop(width // size, out_grad)
    emit("out")
    turn(b.go, b.goT, width)
    yield
    need("q", "k", "v", "qT", "kT", "lse", "apart")
    b.dk[...] = jnp.zeros((length, width), F32)
    b.dv[...] = jnp.zeros((length, width), F32)

    def attend(h):
        group = at_tile(h // per, 128)
        mine = at_tile(h, head)
        lane = lax.broadcasted_iota(jnp.int32, (length, 128), 1) // head == lax.rem(h, per)

        def only(ref):
            return jnp.where(lane, ref[:, group], jnp.zeros((), BF16))

        scores = dot(only(b.k), b.qT[group, :]) * (scale * LOG2E) + b.apart[...]
        probs = jnp.exp2(scores - b.lse[h])
        b.dv[:, group] += dot(probs.astype(BF16), only(b.go))
        back = dot(only(b.v), b.goT[group, :])
        centre = jnp.sum(probs * back, 0, keepdims=True)
        grad = (probs * (back - centre) * scale).astype(BF16)
        b.dk[:, group] += dot(grad, only(b.q))
        b.dqT[mine, :] = dot(b.kT[mine, :], grad)

    parts = 4
    for part in range(parts):
        loop(heads // parts, lambda i, part=part: attend(i + part * (heads // parts)))
        yield
    need("qkv", "hT")

    def query_grad(j):
        lanes = at_tile(j, 128)
        value = b.dqT[lanes, :].T
        b.dvec[vec.bq : vec.bq + 1, lanes] = jnp.sum(value, 0, keepdims=True)
        b.gq0[:, lanes] = value.astype(BF16)

    def rest_grad(j):
        lanes = at_tile(j, 128)
        value = b.dv[:, lanes]
        b.dvec[vec.bv : vec.bv + 1, lanes] = jnp.sum(value, 0, keepdims=True)
        b.gq2[:, lanes] = value.astype(BF16)
        b.gq1[:, lanes] = b.dk[:, lanes].astype(BF16)

    loop(width // 128, query_grad)
    loop(width // 128, rest_grad)
    for third in range(3):
        gq = (b.gq0, b.gq1, b.gq2)[third]
        tile = whole.qkv[:, :, third * width : (third + 1) * width].reshape(width, width)
        part = dot_nt(gq[...], tile)
        b.acc[...] = part if third == 0 else b.acc[...] + part

        def grad(i, gq=gq, third=third):
            value = dot(b.hT[...], gq[:, at_tile(i, size)]).astype(BF16)
            whole.qkv[:, :, pl.ds(pl.multiple_of(third * width + i * size, size), size)] = value.reshape(
                4, width // 4, size
            )

        loop(width // size, grad)
    emit("qkv")
    yield
    need("x")

    def norm_one(i, sums):
        rows = at_tile(i, chunk)
        grad = b.acc[rows, :]
        back, terms = norm_back(read(rows), b.vec[vec.gain1 : vec.gain1 + 1, :], grad)
        b.g[rows, :] = b.g[rows, :] + back
        return (sums[0] + jnp.sum(terms, 0, keepdims=True), sums[1] + jnp.sum(grad, 0, keepdims=True))

    gain_sum, shift_sum = lax.fori_loop(0, length // chunk, norm_one, (zero, zero))
    keep(vec.gain1, gain_sum)
    keep(vec.bias1, shift_sum)
    yield


class Inputs:
    def __init__(self, sem):
        self.sem, self.count, self.flights = sem, 0, {}

    def fetch(self, name, src, dst):
        copy = pltpu.make_async_copy(src, dst, self.sem.at[self.count])
        copy.start()
        self.count += 1
        self.flights[name] = copy

    def need(self, *names):
        for name in names:
            if name in self.flights:
                self.flights.pop(name).wait()

    def finish(self):
        self.need(*list(self.flights))


def fetch_block(inputs, weights, saved, whole, b):
    for key, src, dst in (
        ("down", weights.down, whole.down),
        ("slope", saved.slope, b.slope),
        ("aT", saved.aT, b.aT),
        ("up", weights.up, whole.up),
        ("h2T", saved.h2T, b.h2T),
        ("v1", saved.v1, b.v1),
        ("out", weights.out, whole.out),
        ("oT", saved.oT, b.oT),
        ("q", saved.q, b.q),
        ("k", saved.k, b.k),
        ("v", saved.v, b.v),
        ("qT", saved.qT, b.qT),
        ("kT", saved.kT, b.kT),
        ("lse", saved.lse, b.lse),
        ("apart", saved.apart, b.apart),
        ("qkv", weights.qkv, whole.qkv),
        ("hT", saved.hT, b.hT),
    ):
        inputs.fetch(key, src, dst)


def decoder_back_kernel(cfg, refs):
    shapes, slots, padded_slots, width, length = cfg
    it = iter(refs)

    def take(n):
        return [next(it) for _ in range(n)]

    cotangent, dec_vec = take(2)
    weights, embed_in = Weights(*take(4)), next(it)
    saved = Read(*take(fields(Read)))
    dec_in, shown, shown_t, hid_t = take(4)
    outs = take(3)
    qkv_out, embed_out, hidden_out, dvec_out, up_out = take(5)
    whole, embed_whole = Weights(*take(4)), next(it)
    b = fill(types.SimpleNamespace(), Read, take(fields(Read)))
    here_in, here_shown, here_shown_t, here_hid_t = take(4)
    fill(b, Back, take(fields(Back)))
    b.dvec, up_grad, grad_hidden = take(3)
    bufs = [take(3) for _ in range(6)]
    send_sem, recv_sem, in_sem, out_sem = take(4)
    b.vec = dec_vec
    inputs = Inputs(in_sem)
    fetch_block(inputs, weights, saved, whole, b)
    inputs.fetch("x", dec_in, here_in)
    inputs.fetch(0, shown, here_shown)
    inputs.fetch(1, shown_t, here_shown_t)
    inputs.fetch(2, hid_t, here_hid_t)
    inputs.fetch(3, embed_in, embed_whole)
    at = Place()
    at.barrier()
    sent = ("out", "up", "down")
    scatter = Scatter(at, shapes, [whole.out, whole.up, whole.down], outs, bufs, None, send_sem, recv_sem)
    b.dvec[...] = jnp.zeros(b.dvec.shape, F32)
    for j in range(width // 128):
        lanes = slice(j * 128, (j + 1) * 128)
        b.g[slots // 16 * 16 :, lanes] = jnp.zeros((padded_slots - slots // 16 * 16, 128), F32)
        b.g[:slots, lanes] = cotangent[:, lanes].astype(F32)

    def emit(name):
        if name in sent:
            m = sent.index(name)
            scatter.emit(*lane_parts(shapes, m))

    def read(rows):
        return here_in[rows, :]

    for _ in backward_block(
        b, inputs.need, read, padded_slots, width, DHEADS, DEC_VEC, up_grad, whole, emit
    ):
        scatter.tick(DEC_PATIENCE)
    outgoing = []

    def put(src, dst):
        copy = pltpu.make_async_copy(src, dst, out_sem.at[len(outgoing)])
        copy.start()
        outgoing.append(copy)

    put(whole.qkv, qkv_out)
    inputs.need(0, 1, 2, 3)
    slot_col = lax.broadcasted_iota(jnp.int32, (padded_slots, 1), 0)
    empty = jnp.where(slot_col < slots, 1.0, 0.0) - jnp.sum(here_shown[...].astype(F32), 1, keepdims=True)

    def embed(j):
        lanes = at_tile(j, 256)
        value = b.g[:, lanes]
        b.dvec[1:2, lanes] = jnp.sum(empty * value, 0, keepdims=True)
        high = value.astype(BF16)
        low = (value - high.astype(F32)).astype(BF16)
        rows = dot(here_shown_t[...], high) + dot(here_shown_t[...], low)
        b.dvec[0:1, lanes] = jnp.sum(rows, 0, keepdims=True)
        b.gz[:length, lanes] = rows.astype(BF16)

    loop(width // 256, embed)
    wide = embed_whole.shape[1] * 4
    for i in range(2):
        tile = embed_whole[2 * i : 2 * i + 2].reshape(wide // 2, width)
        grad_hidden[:, i * (wide // 2) : (i + 1) * (wide // 2)] = dot_nt(b.gz[:length, :], tile)

    def embed_grad(j):
        value = dot(here_hid_t[...], b.gz[:length, at_tile(j, 256)]).astype(BF16)
        embed_whole[:, :, at_tile(j, 256)] = value.reshape(4, wide // 4, 256)

    loop(width // 256, embed_grad)
    put(embed_whole, embed_out)
    put(grad_hidden, hidden_out)
    put(b.dvec, dvec_out)
    put(up_grad, up_out)
    inputs.finish()
    scatter.finish()
    for copy in outgoing:
        copy.wait()


def struct(shape):
    return jax.ShapeDtypeStruct(*shape)


def decoder_back(weights, kept, cotangent, dec_vec, dec_in, shown, shown_t, hid_t, row):
    wide = [(w.shape[1] // 8, w.shape[2]) for w in weights]
    shapes = wide[1:4]
    slots, width = dec_in.shape
    length = shown.shape[1]
    ff = wide[2][1]
    any_space = pl.BlockSpec(memory_space=pl.ANY)
    vmem = pl.BlockSpec(memory_space=pltpu.VMEM)
    back = back_buffers(slots, width, ff)
    whole_shapes = [(w.shape, BF16) for w in weights]
    read = [getattr(kept, key) for key in Read._fields]
    read_shapes = [(a.shape, a.dtype) for a in read]
    other = [(a.shape, a.dtype) for a in (dec_in, shown, shown_t, hid_t)]
    results = [((16, width), F32), ((1, ff), F32), ((length, hid_t.shape[0]), F32)]
    scratch = [pltpu.VMEM(*s) for s in whole_shapes + read_shapes + other + list(back) + results]
    scratch += [pltpu.VMEM(*s) for s in scatter_shapes(shapes)]
    scratch += [
        pltpu.SemaphoreType.DMA((8, 8)),
        pltpu.SemaphoreType.DMA((8, 8)),
        pltpu.SemaphoreType.DMA((24,)),
        pltpu.SemaphoreType.DMA((8,)),
    ]
    outs = [(s, F32) for s in shapes]
    out_shape = [struct(s) for s in outs + [whole_shapes[0], whole_shapes[4], results[2], results[0], results[1]]]
    cfg = (shapes, row, slots, width, length)

    def body(*refs):
        decoder_back_kernel(cfg, refs)

    return pl.pallas_call(
        body,
        out_shape=out_shape,
        in_specs=[vmem] * 2 + [any_space] * (5 + len(read) + 4),
        out_specs=[vmem] * 3 + [any_space] * 5,
        scratch_shapes=scratch,
        compiler_params=pltpu.CompilerParams(
            collective_id=1, has_side_effects=True, vmem_limit_bytes=VMEM_BYTES
        ),
        name="decoder_back",
    )(cotangent, dec_vec, *weights, *read, dec_in, shown, shown_t, hid_t)


def encoder_back_kernel(cfg, refs):
    shapes, sizes, length, width = cfg
    count = len(shapes)
    it = iter(refs)

    def take(n):
        return [next(it) for _ in range(n)]

    enc_vec, dec_dvec, dec_up_grad = take(3)
    weights = Weights(*take(4))
    dec_grads = take(2)
    saved = Read(*take(fields(Read)))
    patches, hidden = take(2)
    outs = take(count)
    vec_outs = take(len(sizes))
    patch_out = next(it)
    whole = Weights(*take(4))
    dec_whole = take(2)
    b = fill(types.SimpleNamespace(), Read, take(fields(Read)))
    x = next(it)
    fill(b, Back, take(fields(Back)))
    b.dvec, up_grad = take(2)
    bufs = [take(count) for _ in range(6)]
    vec = VecBufs(*take(6))
    send_sem, recv_sem, in_sem, out_sem = take(4)
    b.vec = enc_vec
    inputs = Inputs(in_sem)
    inputs.fetch(0, dec_grads[0], dec_whole[0])
    inputs.fetch("g", hidden, b.g)
    inputs.fetch(1, dec_grads[1], dec_whole[1])
    fetch_block(inputs, weights, saved, whole, b)
    inputs.fetch("x", patches, x)
    at = Place()
    at.barrier()
    scatter = Scatter(at, shapes, dec_whole + list(whole), outs, bufs, vec, send_sem, recv_sem)
    for m in range(2):
        inputs.need(m)
        scatter.emit(*lane_parts(shapes, m))

    def emit(name):
        scatter.emit(*lane_parts(shapes, 2 + Weights._fields.index(name)))

    def read(rows):
        return x[rows, :].astype(F32)

    inputs.need("g")
    for _ in backward_block(b, inputs.need, read, length, width, HEADS, ENC_VEC, up_grad, whole, emit):
        scatter.tick(ENC_PATIENCE)
    copy = pltpu.make_async_copy(b.g, patch_out, out_sem.at[0])
    copy.start()
    enc_dvec, dec_dvec = b.dvec[...], dec_dvec[...]
    ups, dec_ups = up_grad[...], dec_up_grad[...]
    for d in range(32):
        tile = vec.tiles.at[d // 8, d // 2 % 4, d % 2]
        tile[0:8] = collect(enc_dvec, sizes[0], d)
        row = lax.broadcasted_iota(jnp.int32, (8, 128), 0)
        up = jnp.broadcast_to(collect(ups, sizes[ENC_UP_ROW], d), (8, 128))
        dec_up = jnp.broadcast_to(collect(dec_ups, sizes[DEC_UP_ROW], d), (8, 128))
        both = collect(dec_dvec, sizes[8], d)
        tile[8:16] = both[:8]
        tile[16:24] = jnp.where(row == ENC_UP_ROW - 16, up, jnp.where(row == DEC_UP_ROW - 16, dec_up, both[8:]))
    scatter.emit(None)
    inputs.finish()
    scatter.finish()
    for k, ref in enumerate(vec_outs):
        ref[...] = vec.sum[k : k + 1, : sizes[k]]
    copy.wait()


def encoder_back(weights, dec_grads, kept, enc_vec, dec_dvec, dec_up_grad, patches, grad_hidden, sizes):
    shapes = [(w.shape[1] // 8, w.shape[2]) for w in list(dec_grads) + list(weights)]
    length, width = patches.shape
    ff = weights[2].shape[2]
    any_space = pl.BlockSpec(memory_space=pl.ANY)
    vmem = pl.BlockSpec(memory_space=pltpu.VMEM)
    back = back_buffers(length, width, ff)
    whole_shapes = [(w.shape, BF16) for w in list(weights) + list(dec_grads)]
    read = [getattr(kept, key) for key in Read._fields]
    read_shapes = [(a.shape, a.dtype) for a in read]
    scratch = whole_shapes + read_shapes + [(patches.shape, BF16)] + list(back)
    scratch += [((8, width), F32), ((1, ff), F32)]
    scratch += scatter_shapes(shapes)
    tile = (VEC_ROWS, 128)
    scratch += [((4, 4, 2) + tile, F32), ((4, 4) + tile, F32), ((2, 4) + tile, F32), ((4,) + tile, F32)]
    scratch += [((3,) + tile, F32), (tile, F32)]
    scratch = [pltpu.VMEM(*s) for s in scratch]
    scratch += [
        pltpu.SemaphoreType.DMA((14, 8)),
        pltpu.SemaphoreType.DMA((14, 8)),
        pltpu.SemaphoreType.DMA((24,)),
        pltpu.SemaphoreType.DMA((1,)),
    ]
    outs = [(s, F32) for s in shapes] + [((1, s), F32) for s in sizes] + [((length, width), F32)]
    cfg = (shapes, sizes, length, width)

    def body(*refs):
        encoder_back_kernel(cfg, refs)

    results = pl.pallas_call(
        body,
        out_shape=[struct(s) for s in outs],
        in_specs=[vmem] * 3 + [any_space] * (4 + 2 + len(read) + 2),
        out_specs=[vmem] * (len(shapes) + len(sizes)) + [any_space],
        scratch_shapes=scratch,
        compiler_params=pltpu.CompilerParams(
            collective_id=2, has_side_effects=True, vmem_limit_bytes=VMEM_BYTES
        ),
        name="encoder_back",
    )(enc_vec, dec_dvec, dec_up_grad, *weights, *dec_grads, *read, patches, grad_hidden)
    count = len(shapes)
    return results[:count], results[count : count + len(sizes)], results[-1]


def settle(arrays):
    count = len(arrays)
    vmem = pl.BlockSpec(memory_space=pltpu.VMEM)

    def body(*refs):
        for src, dst in zip(refs[:count], refs[count:]):
            rows = src.shape[0]
            if rows % 16 == 0 and rows > 128:
                loop(rows // 16, lambda i, src=src, dst=dst: dst.__setitem__(at_tile(i, 16), src[at_tile(i, 16)]))
            else:
                dst[...] = src[...]

    return pl.pallas_call(
        body,
        out_shape=[jax.ShapeDtypeStruct(a.shape, a.dtype) for a in arrays],
        in_specs=[vmem] * count,
        out_specs=[vmem] * count,
        compiler_params=pltpu.CompilerParams(vmem_limit_bytes=VMEM_BYTES),
        name="settle",
    )(*arrays)


def widen(value):
    return value.astype(jnp.float32)


def layer_norm(stream, gain, shift):
    row_mean = jnp.mean(stream, -1, keepdims=True)
    centred = stream - row_mean
    row_var = jnp.mean(centred * centred, -1, keepdims=True)
    return centred * lax.rsqrt(row_var + EPSILON) * gain + shift


def norm_pull(stream, gain, shift, grad_out):
    pull = jax.vjp(layer_norm, stream, gain, shift)[1]
    return pull(grad_out)


def gelu_exact(value):
    return jax.nn.gelu(value, approximate=False)


def split_heads(rows, head_count):
    batch, length, model_width = rows.shape
    return rows.reshape(batch, length, head_count, model_width // head_count)


def masked_scores(query_heads, key_heads, same_doc, score_scale):
    scores = (
        jnp.einsum("bqhd,bkhd->bhqk", query_heads, key_heads, preferred_element_type=jnp.float32)
        * score_scale
    )
    return jnp.where(same_doc[:, None], scores, -1000000000.0)


def attend_forward(query_rows, key_rows, value_rows, same_doc, head_count, score_scale):
    batch, length, model_width = query_rows.shape
    scores = masked_scores(
        split_heads(query_rows, head_count),
        split_heads(key_rows, head_count),
        same_doc,
        score_scale,
    )
    row_max = jnp.max(scores, -1, keepdims=True)
    expo = jnp.exp(scores - row_max)
    row_sum = jnp.sum(expo, -1, keepdims=True)
    att_probs = (expo / row_sum).astype(jnp.bfloat16)
    mixed = jnp.einsum(
        "bhqk,bkhd->bqhd",
        att_probs,
        split_heads(value_rows, head_count),
        preferred_element_type=jnp.float32,
    )
    return (mixed.reshape(batch, length, model_width), row_max + jnp.log(row_sum))


def attend_backward(
    query_rows, key_rows, value_rows, same_doc, log_total, grad_mixed, head_count, score_scale
):
    batch, length, model_width = query_rows.shape
    query_heads = split_heads(query_rows, head_count)
    key_heads = split_heads(key_rows, head_count)
    value_heads = split_heads(value_rows, head_count)
    grad_heads = split_heads(grad_mixed, head_count)
    att_probs = jnp.exp(masked_scores(query_heads, key_heads, same_doc, score_scale) - log_total)
    grad_value = jnp.einsum(
        "bhqk,bqhd->bkhd",
        att_probs.astype(jnp.bfloat16),
        grad_heads,
        preferred_element_type=jnp.float32,
    )
    grad_probs = jnp.einsum(
        "bqhd,bkhd->bhqk", grad_heads, value_heads, preferred_element_type=jnp.float32
    )
    centre = jnp.sum(att_probs * grad_probs, -1, keepdims=True)
    grad_scores = (att_probs * (grad_probs - centre) * score_scale).astype(jnp.bfloat16)
    grad_query = jnp.einsum(
        "bhqk,bkhd->bqhd", grad_scores, key_heads, preferred_element_type=jnp.float32
    )
    grad_key = jnp.einsum(
        "bhqk,bqhd->bkhd", grad_scores, query_heads, preferred_element_type=jnp.float32
    )
    rows = batch * length
    return (
        grad_query.reshape(rows, model_width),
        grad_key.reshape(rows, model_width),
        grad_value.reshape(rows, model_width),
    )


def block_forward(stream, params, seg_ids, head_count):
    (
        gain_one,
        shift_one,
        w_qkv,
        query_bias,
        value_bias,
        w_out,
        out_bias,
        gain_two,
        shift_two,
        w_up,
        up_bias,
        w_down,
        down_bias,
    ) = params
    row_count, model_width = stream.shape
    batch, length = seg_ids.shape
    score_scale = (model_width // head_count) ** (-0.5)
    normed = layer_norm(stream, widen(gain_one), widen(shift_one)).astype(jnp.bfloat16)
    joined = jnp.dot(normed, w_qkv, preferred_element_type=jnp.float32)
    query_rows = (joined[:, :model_width] + widen(query_bias)).astype(jnp.bfloat16)
    key_rows = joined[:, model_width : 2 * model_width].astype(jnp.bfloat16)
    value_rows = (joined[:, 2 * model_width :] + widen(value_bias)).astype(jnp.bfloat16)
    same_doc = seg_ids[:, :, None] == seg_ids[:, None, :]
    shape_three = (batch, length, model_width)
    mixed, log_total = attend_forward(
        query_rows.reshape(shape_three),
        key_rows.reshape(shape_three),
        value_rows.reshape(shape_three),
        same_doc,
        head_count,
        score_scale,
    )
    attended = mixed.reshape(row_count, model_width).astype(jnp.bfloat16)
    middle = stream + jnp.dot(attended, w_out, preferred_element_type=jnp.float32) + widen(out_bias)
    normed_two = layer_norm(middle, widen(gain_two), widen(shift_two)).astype(jnp.bfloat16)
    hidden_up = jnp.dot(normed_two, w_up, preferred_element_type=jnp.float32) + widen(up_bias)
    activated = gelu_exact(hidden_up).astype(jnp.bfloat16)
    result = (
        middle + jnp.dot(activated, w_down, preferred_element_type=jnp.float32) + widen(down_bias)
    )
    saved = (
        stream,
        middle,
        normed,
        query_rows,
        key_rows,
        value_rows,
        log_total,
        attended,
        normed_two,
        hidden_up,
        activated,
    )
    return (result, saved)


def back_feed(grad_out, params, saved):
    (
        gain_one,
        shift_one,
        w_qkv,
        query_bias,
        value_bias,
        w_out,
        out_bias,
        gain_two,
        shift_two,
        w_up,
        up_bias,
        w_down,
        down_bias,
    ) = params
    (
        stream,
        middle,
        normed,
        query_rows,
        key_rows,
        value_rows,
        log_total,
        attended,
        normed_two,
        hidden_up,
        activated,
    ) = saved
    grad_low = grad_out.astype(jnp.bfloat16)
    grad_down_bias = jnp.sum(grad_out, 0)
    grad_down = jnp.einsum("rf,rw->fw", activated, grad_low, preferred_element_type=jnp.float32)
    grad_act = jnp.einsum("rw,fw->rf", grad_low, w_down, preferred_element_type=jnp.float32)
    grad_hidden = jax.vjp(gelu_exact, hidden_up)[1](grad_act)[0]
    grad_hidden_low = grad_hidden.astype(jnp.bfloat16)
    grad_up_bias = jnp.sum(grad_hidden, 0)
    grad_up = jnp.einsum(
        "rd,rf->df", normed_two, grad_hidden_low, preferred_element_type=jnp.float32
    )
    grad_normed_two = jnp.einsum(
        "rf,df->rd", grad_hidden_low, w_up, preferred_element_type=jnp.float32
    )
    grad_mid_norm, grad_gain_two, grad_shift_two = norm_pull(
        middle, widen(gain_two), widen(shift_two), grad_normed_two
    )
    grad_middle = grad_out + grad_mid_norm
    return (
        grad_middle,
        (grad_gain_two, grad_shift_two, grad_up, grad_up_bias, grad_down, grad_down_bias),
    )


def back_attend(grad_middle, params, seg_ids, head_count, saved):
    (
        gain_one,
        shift_one,
        w_qkv,
        query_bias,
        value_bias,
        w_out,
        out_bias,
        gain_two,
        shift_two,
        w_up,
        up_bias,
        w_down,
        down_bias,
    ) = params
    (
        stream,
        middle,
        normed,
        query_rows,
        key_rows,
        value_rows,
        log_total,
        attended,
        normed_two,
        hidden_up,
        activated,
    ) = saved
    row_count, model_width = stream.shape
    batch, length = seg_ids.shape
    score_scale = (model_width // head_count) ** (-0.5)
    grad_middle_low = grad_middle.astype(jnp.bfloat16)
    grad_out_bias = jnp.sum(grad_middle, 0)
    grad_w_out = jnp.einsum(
        "rv,rw->vw", attended, grad_middle_low, preferred_element_type=jnp.float32
    )
    grad_attended = jnp.einsum(
        "rw,vw->rv", grad_middle_low, w_out, preferred_element_type=jnp.float32
    ).astype(jnp.bfloat16)
    same_doc = seg_ids[:, :, None] == seg_ids[:, None, :]
    shape_three = (batch, length, model_width)
    grad_query, grad_key, grad_value = attend_backward(
        query_rows.reshape(shape_three),
        key_rows.reshape(shape_three),
        value_rows.reshape(shape_three),
        same_doc,
        log_total,
        grad_attended.reshape(shape_three),
        head_count,
        score_scale,
    )
    grad_query_bias = jnp.sum(grad_query, 0)
    grad_value_bias = jnp.sum(grad_value, 0)
    grad_joined = jnp.concatenate([grad_query, grad_key, grad_value], 1).astype(jnp.bfloat16)
    grad_qkv = jnp.einsum("rd,rc->dc", normed, grad_joined, preferred_element_type=jnp.float32)
    grad_normed = jnp.einsum("rc,dc->rd", grad_joined, w_qkv, preferred_element_type=jnp.float32)
    grad_in_norm, grad_gain_one, grad_shift_one = norm_pull(
        stream, widen(gain_one), widen(shift_one), grad_normed
    )
    grads = (
        grad_gain_one,
        grad_shift_one,
        grad_qkv,
        grad_query_bias,
        grad_value_bias,
        grad_w_out,
        grad_out_bias,
    )
    return (grad_middle + grad_in_norm, grads)


def block_backward(grad_out, params, seg_ids, head_count, saved):
    grad_middle, feed_grads = back_feed(grad_out, params, saved)
    grad_in, attend_grads = back_attend(grad_middle, params, seg_ids, head_count, saved)
    return (grad_in, attend_grads + feed_grads)


def by_collectives(a):
    seq_count = a.segments.shape[0] // ROW
    seg_ids = a.segments.reshape(seq_count, ROW)
    vis_slots = a.visible_index.reshape(seq_count, VIS)
    enc_seg = jnp.take_along_axis(seg_ids, vis_slots, 1)
    seq_index = jnp.arange(seq_count, dtype=jnp.int32)[:, None]
    matrices = [lax.all_gather(m, AXIS, axis=0, tiled=True) for m in matrices_of(a)]
    joined = lax.all_gather(jnp.concatenate(vectors_of(a)), AXIS, axis=0)
    sizes = [v.shape[0] for v in vectors_of(a)]
    vectors, start = [], 0
    for size in sizes:
        vectors.append(joined[:, start : start + size].reshape(-1))
        start += size
    whole = Arguments(a.patches, a.visible_index, a.segments, a.cotangent, *in_order(matrices, vectors))
    hidden, enc_saved = block_forward(widen(a.patches), encoder_of(whole), enc_seg, HEADS)
    hidden_low = hidden.astype(jnp.bfloat16)
    embedded = jnp.dot(hidden_low, whole.embed_weight, preferred_element_type=jnp.float32) + widen(
        whole.embed_bias
    )
    embedded = embedded.reshape(seq_count, VIS, DD)
    dec_in = (
        jnp.broadcast_to(widen(whole.mask_token), (seq_count, ROW, DD))
        .at[seq_index, vis_slots]
        .set(embedded)
    )
    dec_in = dec_in.reshape(seq_count * ROW, DD)
    decoded, dec_saved = block_forward(dec_in, decoder_of(whole), seg_ids, DHEADS)
    grad_dec_in, dec_grads = block_backward(
        widen(a.cotangent), decoder_of(whole), seg_ids, DHEADS, dec_saved
    )
    grad_dec_in = grad_dec_in.reshape(seq_count, ROW, DD)
    shown_slots = jnp.zeros((seq_count, ROW), jnp.float32).at[seq_index, vis_slots].set(1.0)
    grad_mask = jnp.sum((1.0 - shown_slots)[:, :, None] * grad_dec_in, (0, 1))
    grad_embedded = grad_dec_in[seq_index, vis_slots].reshape(seq_count * VIS, DD)
    grad_embed_b = jnp.sum(grad_embedded, 0)
    grad_embedded_low = grad_embedded.astype(jnp.bfloat16)
    grad_embed_w = jnp.einsum(
        "rd,re->de", hidden_low, grad_embedded_low, preferred_element_type=jnp.float32
    )
    grad_hidden = jnp.einsum(
        "re,de->rd", grad_embedded_low, whole.embed_weight, preferred_element_type=jnp.float32
    )
    grad_patches, enc_grads = block_backward(grad_hidden, encoder_of(whole), enc_seg, HEADS, enc_saved)
    grads = Arguments(None, None, None, None, *enc_grads, grad_embed_w, grad_embed_b, grad_mask, *dec_grads)
    sums = [lax.psum_scatter(m, AXIS, scatter_dimension=0, tiled=True) for m in matrices_of(grads)]
    joined = jnp.concatenate([v.reshape(-1, size) for v, size in zip(vectors_of(grads), sizes)], 1)
    joined = lax.psum_scatter(joined, AXIS, scatter_dimension=0, tiled=True).reshape(-1)
    vector_sums, start = [], 0
    for size in sizes:
        vector_sums.append(joined[start : start + size])
        start += size
    return (decoded.astype(jnp.bfloat16), grad_patches) + in_order(sums, vector_sums)


def fits(a):
    return (
        lax.axis_size(AXIS) == 32
        and a.segments.shape[0] == ROW
        and a.patches.shape[0] == VIS
        and all(m.shape[0] % 8 == 0 and m.shape[1] % 256 == 0 for m in matrices_of(a))
        and all(v.shape[0] <= 128 for v in vectors_of(a))
    )


def by_kernels(a):
    vectors = vectors_of(a)
    sizes = [v.shape[0] for v in vectors]
    wholes, enc_vec, dec_vec, enc_kept, dec_kept, hid_t, dec_in, shown, shown_t, decoded = forward_all(
        matrices_of(a), vectors, a.patches, a.visible_index, a.segments, ROW
    )
    *dec_sums, qkv, embed, grad_hidden, dec_dvec, dec_up = decoder_back(
        wholes[5:] + [wholes[4]], dec_kept, a.cotangent, dec_vec, dec_in, shown, shown_t, hid_t, ROW
    )
    (dec_qkv, embed, *enc_sums), vec_sums, grad_patches = encoder_back(
        wholes[:4], [qkv, embed], enc_kept, enc_vec, dec_dvec, dec_up, a.patches, grad_hidden, sizes
    )
    sums = in_order(list(enc_sums) + [embed, dec_qkv] + list(dec_sums), vec_sums)
    results = settle((decoded, grad_patches) + sums)
    shapes = (None,) * 4 + tuple(v.shape for v in a[4:])
    return tuple(results[:2]) + tuple(r.reshape(-1) if len(s) == 1 else r for r, s in zip(results[2:], shapes[4:]))


def on_device(*arguments):
    a = Arguments(*arguments)
    return by_kernels(a) if fits(a) else by_collectives(a)


def solution(mesh):
    count = len(Arguments._fields)
    vectors = vectors_of(Arguments(*range(count)))
    specs = [P(AXIS) if i in (1, 2) or i in vectors else P(AXIS, None) for i in range(count)]
    return jax.shard_map(
        on_device,
        mesh=mesh,
        in_specs=tuple(specs),
        out_specs=tuple([P(AXIS, None)] * 2 + specs[4:]),
        check_vma=False,
    )
```

```python
import types
from typing import Any, NamedTuple

import jax
import jax.numpy as jnp
from jax import lax
from jax.experimental import pallas as pl
from jax.experimental.pallas import tpu as pltpu
from jax.sharding import PartitionSpec as P

AXIS = "fsdp"
MESH = pl.DeviceIdType.MESH
VMEM_BYTES = 63 * 2**20
F32, BF16 = jnp.float32, jnp.bfloat16
EPSILON = 1e-06
HEADS, DHEADS = 12, 16
LOG2E = 1.4426950408889634
APART = -(2.0**100)
ROOT_HALF = 0.7071067811865476
ROOT_TWO_PI = 0.3989422804014327
VEC_ROWS = 24
PIECES = 5
LAGS = (0, 1, 2, 3, 4)
GATHER_ORDER = (4, 6, 1, 0, 2, 3, 5, 7, 8)
DEC_PATIENCE, ENC_PATIENCE = 3, 4
ENC_UP_ROW, DEC_UP_ROW = 18, 19
DD = 512
ROW = 529
VIS = 384


class Arguments(NamedTuple):
    patches: Any
    visible_index: Any
    segments: Any
    cotangent: Any
    enc_norm1_gain: Any
    enc_norm1_bias: Any
    enc_qkv: Any
    enc_query_bias: Any
    enc_value_bias: Any
    enc_out: Any
    enc_out_bias: Any
    enc_norm2_gain: Any
    enc_norm2_bias: Any
    enc_up: Any
    enc_up_bias: Any
    enc_down: Any
    enc_down_bias: Any
    embed_weight: Any
    embed_bias: Any
    mask_token: Any
    dec_norm1_gain: Any
    dec_norm1_bias: Any
    dec_qkv: Any
    dec_query_bias: Any
    dec_value_bias: Any
    dec_out: Any
    dec_out_bias: Any
    dec_norm2_gain: Any
    dec_norm2_bias: Any
    dec_up: Any
    dec_up_bias: Any
    dec_down: Any
    dec_down_bias: Any


def matrices_of(a):
    return (
        a.enc_qkv,
        a.enc_out,
        a.enc_up,
        a.enc_down,
        a.embed_weight,
        a.dec_qkv,
        a.dec_out,
        a.dec_up,
        a.dec_down,
    )


def vectors_of(a):
    return (
        a.enc_norm1_gain,
        a.enc_norm1_bias,
        a.enc_query_bias,
        a.enc_value_bias,
        a.enc_out_bias,
        a.enc_norm2_gain,
        a.enc_norm2_bias,
        a.enc_down_bias,
        a.embed_bias,
        a.mask_token,
        a.dec_norm1_gain,
        a.dec_norm1_bias,
        a.dec_query_bias,
        a.dec_value_bias,
        a.dec_out_bias,
        a.dec_norm2_gain,
        a.dec_norm2_bias,
        a.dec_down_bias,
        a.enc_up_bias,
        a.dec_up_bias,
    )


def encoder_of(a):
    return (
        a.enc_norm1_gain,
        a.enc_norm1_bias,
        a.enc_qkv,
        a.enc_query_bias,
        a.enc_value_bias,
        a.enc_out,
        a.enc_out_bias,
        a.enc_norm2_gain,
        a.enc_norm2_bias,
        a.enc_up,
        a.enc_up_bias,
        a.enc_down,
        a.enc_down_bias,
    )


def decoder_of(a):
    return (
        a.dec_norm1_gain,
        a.dec_norm1_bias,
        a.dec_qkv,
        a.dec_query_bias,
        a.dec_value_bias,
        a.dec_out,
        a.dec_out_bias,
        a.dec_norm2_gain,
        a.dec_norm2_bias,
        a.dec_up,
        a.dec_up_bias,
        a.dec_down,
        a.dec_down_bias,
    )


def in_order(matrices, vectors):
    places = Arguments(*range(len(Arguments._fields)))
    found = dict(zip(matrices_of(places) + vectors_of(places), tuple(matrices) + tuple(vectors)))
    return tuple(found[place] for place in sorted(found))


def dot(a, b):
    return jnp.dot(a, b, preferred_element_type=F32)


def dot_nt(a, b):
    return lax.dot_general(a, b, (((1,), (1,)), ((), ())), preferred_element_type=F32)


def at_tile(j, size):
    return pl.ds(pl.multiple_of(j * size, size), size)


def loop(count, body):
    def step(i, carry):
        body(i)
        return carry

    lax.fori_loop(0, count, step, 0)


class Place:
    def __init__(self):
        me = lax.axis_index(AXIS)
        self.c = c = lax.rem(me, 2)
        x = lax.rem(me // 2, 2)
        y = lax.rem(me // 4, 2)
        self.z = lax.rem(me // 8, 4)
        self.stride1 = 1 + c
        self.stride2 = 2 - c
        self.bit1 = x * (1 - c) + y * c
        self.bit2 = y * (1 - c) + x * c
        self.here = 2 * y + x
        self.core = me + 1 - 2 * c
        self.first = me + 2 * self.stride1 * (1 - 2 * self.bit1)
        self.second = me + 2 * self.stride2 * (1 - 2 * self.bit2)
        self.zs = [lax.rem(self.z + i, 4) for i in range(4)]
        self.columns = [me + 8 * (z - self.z) for z in self.zs]

    def yx(self, flip1, flip2):
        bit1 = 1 - self.bit1 if flip1 else self.bit1
        bit2 = 1 - self.bit2 if flip2 else self.bit2
        return bit1 * self.stride1 + bit2 * self.stride2

    def greet(self):
        for partner in [self.core, self.first, self.second] + self.columns[1:]:
            pl.semaphore_signal(pltpu.get_barrier_semaphore(), inc=1, device_id=(partner,), device_id_type=MESH)

    def meet(self):
        pl.semaphore_wait(pltpu.get_barrier_semaphore(), 6)


def padded(rows):
    return -(-rows // 16) * 16


def chunks_of(shapes):
    out = []
    for m, (rows, columns) in enumerate(shapes):
        half = columns // 2
        if 32 * rows * columns * 2 <= 3 * 2**20 and m != len(shapes) - 1:
            out.append((m, 0, 2 * rows, 0, half))
        elif rows % 16 == 0:
            out.append((m, 0, rows, 0, half))
            out.append((m, rows, rows, 0, half))
        else:
            low = half // 256 * 128
            out.append((m, 0, 2 * rows, 0, half - low))
            out.append((m, 0, 2 * rows, half - low, low))
    return out


class Gather:
    def __init__(self, at, shapes, shards, wholes, vec_tile, vec_whole, sent, got, send_sem, recv_sem):
        self.at, self.shapes, self.shards, self.wholes = at, shapes, shards, wholes
        self.vec_tile, self.vec_whole = vec_tile, vec_whole
        self.sent, self.got = sent, got
        self.send_sem, self.recv_sem = send_sem, recv_sem
        self.chunks = [None] + sorted(chunks_of(shapes), key=lambda part: GATHER_ORDER.index(part[0]))
        self.started = []
        self.flights = {}

    def send(self, src, dst, chunk, slot, partner):
        copy = pltpu.make_async_remote_copy(
            src_ref=src,
            dst_ref=dst,
            send_sem=self.send_sem.at[chunk, slot],
            recv_sem=self.recv_sem.at[chunk, slot],
            device_id=(partner,),
            device_id_type=MESH,
        )
        copy.start()
        self.started.append(copy)
        return copy

    def view(self, chunk, z, yx):
        if chunk == 0:
            return self.vec_whole.at[z, yx, self.at.c]
        m, row, rows, lane, lanes = self.chunks[chunk]
        chip_rows, half = 2 * self.shapes[m][0], self.shapes[m][1] // 2
        start = pl.multiple_of(yx * chip_rows + row, 16)
        first = pl.multiple_of(self.at.c * half + lane, 128)
        return self.wholes[m].at[z, pl.ds(start, rows), pl.ds(first, lanes)]

    def my_half(self, m, mine):
        half = self.shapes[m][1] // 2
        low, high = self.shards[m][:, :half].astype(F32), self.shards[m][:, half:].astype(F32)
        return jnp.where(self.at.c == 0, low, high) if mine else jnp.where(self.at.c == 0, high, low)

    def swap(self, m):
        rows, columns = self.shapes[m]
        value = self.my_half(m, False)
        extra = padded(rows) - rows
        if extra:
            value = jnp.concatenate([value, jnp.zeros((extra, columns // 2), F32)], 0)
        self.sent[m][...] = value.astype(BF16)
        self.flights["swap", m] = self.send(self.sent[m], self.got[m], len(self.chunks) + m, 0, self.at.core)

    def place(self, m):
        at, (rows, columns) = self.at, self.shapes[m]
        self.flights["swap", m].wait_recv()
        other = self.got[m][...].astype(F32)[:rows]
        mine = self.my_half(m, True)
        both = jnp.concatenate([jnp.where(at.c == 0, mine, other), jnp.where(at.c == 0, other, mine)], 0)
        half = columns // 2
        lanes = pl.ds(pl.multiple_of(at.c * half, 128), half)
        row = pl.ds(pl.multiple_of(at.here * 2 * rows, 16), 2 * rows)
        self.wholes[m][at.z, row, lanes] = both.astype(BF16)

    def stage(self, chunk, k):
        at, flights = self.at, self.flights
        every = slice(None)
        if k == 0:
            if chunk == 0:
                self.vec_whole[at.z, at.here, at.c] = self.vec_tile[...]
            elif self.chunks[chunk][1] == 0 and self.chunks[chunk][3] == 0:
                self.place(self.chunks[chunk][0])
            own = self.view(chunk, at.z, at.here)
            flights[chunk, 0] = [self.send(own, own, chunk, i, at.columns[i]) for i in range(1, 4)]
        elif k == 1:
            for copy in flights[chunk, 0]:
                copy.wait_recv()
            part = self.view(chunk, every, at.here)
            flights[chunk, 1] = [
                self.send(part, part, chunk, 4, at.second),
                self.send(part, part, chunk, 5, at.first),
            ]
            flights[chunk, "core"] = [self.send(part, part, chunk, 7, at.core)]
        elif k == 2:
            flights[chunk, 1][0].wait_recv()
            part = self.view(chunk, every, at.yx(False, True))
            flights[chunk, 2] = self.send(part, part, chunk, 6, at.first)
            flights[chunk, "core"].append(self.send(part, part, chunk, 8, at.core))
            flights[chunk, 1][1].wait_recv()
            part = self.view(chunk, every, at.yx(True, False))
            flights[chunk, "core"].append(self.send(part, part, chunk, 9, at.core))
        elif k == 3:
            flights[chunk, 2].wait_recv()
            part = self.view(chunk, every, at.yx(True, True))
            flights[chunk, "core"].append(self.send(part, part, chunk, 10, at.core))
        elif k == 4:
            for copy in flights[chunk, "core"]:
                copy.wait_recv()

    def steps(self):
        swaps = list(GATHER_ORDER)
        for _ in range(2):
            self.swap(swaps.pop(0))
        count = len(self.chunks)
        for step in range(count + LAGS[-1]):
            done = None
            if swaps:
                self.swap(swaps.pop(0))
            for k, lag in enumerate(LAGS):
                if 0 <= step - lag < count:
                    self.stage(step - lag, k)
                    if k == 4:
                        done = step - lag
            yield done

    def finish(self):
        for copy in self.started:
            copy.wait_send()


def spread(tiles, width, out_width):
    lane = lax.broadcasted_iota(jnp.int32, tiles[0].shape, 1)
    whole = [jnp.zeros(tiles[0].shape, F32) for _ in range(out_width // 128)]
    for d, tile in enumerate(tiles):
        t, shift = divmod(d * width, 128)
        rolled = pltpu.roll(tile, shift, 1) if shift else tile
        over = shift + width - 128
        if over <= 0:
            whole[t] = whole[t] + rolled
        else:
            whole[t] = whole[t] + jnp.where(lane >= shift, rolled, 0.0)
            whole[t + 1] = whole[t + 1] + jnp.where(lane < over, rolled, 0.0)
    return jnp.concatenate(whole, 1)


def normed_rows(rows, gain, shift):
    centred = rows - jnp.mean(rows, -1, keepdims=True)
    variance = jnp.mean(centred * centred, -1, keepdims=True)
    return centred * lax.rsqrt(variance + EPSILON) * gain + shift


def norm_into(read, gain, shift, out, out_t, length, width):
    chunk = length // 2
    loop(
        length // chunk,
        lambda i: out.__setitem__(
            (at_tile(i, chunk), slice(None)), normed_rows(read(at_tile(i, chunk)), gain(), shift()).astype(BF16)
        ),
    )
    turn(out, out_t, width)


def turn(src, dst, width):
    def body(j):
        dst[at_tile(j, 128), :] = src[:, at_tile(j, 128)].T

    loop(width // 128, body)


def turn_back(src, dst, width):
    def body(j):
        dst[:, at_tile(j, 128)] = src[at_tile(j, 128), :].T

    loop(width // 128, body)


def column_tile(whole, j, size):
    tile = whole[:, :, at_tile(j, size)]
    return tile.reshape(tile.shape[0] * tile.shape[1], size)


def forward_block(b, read, length, width, heads, vec, up_bias, whole, finish):
    head = width // heads
    per = 128 // head
    scale = head ** (-0.5) * LOG2E
    size = 256

    def row(index, j=None):
        if j is None:
            return b.vec[index : index + 1, :]
        return b.vec[index : index + 1, at_tile(j, size)]

    norm_into(read, lambda: row(vec.gain1), lambda: row(vec.bias1), b.h, b.hT, length, width)
    yield "qkv"
    tiles = width // size

    def project(third, key, out, out_t):
        def body(j):
            value = dot(b.h[...], column_tile(whole.qkv, third * tiles + j, size))
            if key is not None:
                value = value + row(key, j)
            value = value.astype(BF16)
            out[:, at_tile(j, size)] = value
            out_t[at_tile(j, size), :] = value.T

        loop(tiles, body)

    project(0, vec.bq, b.q, b.qT)
    yield None
    project(1, None, b.k, b.kT)
    yield None
    project(2, vec.bv, b.v, b.vT)
    yield None

    def attend(h):
        group = at_tile(h // per, 128)
        lane = lax.broadcasted_iota(jnp.int32, (length, 128), 1) // head
        keys = jnp.where(lane == lax.rem(h, per), b.k[:, group], jnp.zeros((), BF16))
        scores = dot(keys, b.qT[group, :]) * scale + b.apart[...]
        top = jnp.max(scores, 0, keepdims=True)
        expo = jnp.exp2(scores - top)
        total = jnp.sum(expo, 0, keepdims=True)
        probs = (expo * (1.0 / total)).astype(BF16)
        mine = at_tile(h, head)
        b.oT[mine, :] = dot(b.vT[mine, :], probs).astype(BF16)
        b.lse[h] = top + jnp.log2(total)

    parts = 4
    for part in range(parts):
        loop(heads // parts, lambda i, part=part: attend(i + part * (heads // parts)))
        yield None
    turn_back(b.oT, b.h, width)
    yield "out"

    def middle(j):
        b.v1[:, at_tile(j, size)] = (
            read(slice(None), at_tile(j, size)) + dot(b.h[...], column_tile(whole.out, j, size)) + row(vec.bo, j)
        )

    loop(tiles, middle)
    norm_into(
        lambda rows: b.v1[rows, :], lambda: row(vec.gain2), lambda: row(vec.bias2), b.h, b.h2T, length, width
    )
    yield "up"

    def lift(j):
        u = dot(b.h[...], column_tile(whole.up, j, size)) + up_bias[:, at_tile(j, size)]
        share = 0.5 + 0.5 * lax.erf(u * ROOT_HALF)
        slope = share + u * (jnp.exp2(u * u * (-0.5 * LOG2E)) * ROOT_TWO_PI)
        a = (u * share).astype(BF16)
        b.a[:, at_tile(j, size)] = a
        b.aT[at_tile(j, size), :] = a.T
        b.slope[:, at_tile(j, size)] = slope.astype(BF16)

    ups = b.a.shape[1] // size
    for part in range(4):
        loop(ups // 4, lambda i, part=part: lift(i + part * (ups // 4)))
        yield None
    yield "down"

    def drop(j):
        finish(
            j,
            b.v1[:, at_tile(j, size)] + dot(b.a[...], column_tile(whole.down, j, size)) + row(vec.bd, j),
        )

    loop(tiles, drop)
    yield None


class VecRows(NamedTuple):
    gain1: int
    bias1: int
    bq: int
    bv: int
    bo: int
    gain2: int
    bias2: int
    bd: int


ENC_VEC, DEC_VEC = VecRows(*range(8)), VecRows(*range(2, 10))


class Weights(NamedTuple):
    qkv: Any
    out: Any
    up: Any
    down: Any


class Own(NamedTuple):
    h: Any
    a: Any
    apart: Any


class Saved(NamedTuple):
    hT: Any
    q: Any
    k: Any
    v: Any
    qT: Any
    kT: Any
    vT: Any
    lse: Any
    oT: Any
    v1: Any
    h2T: Any
    aT: Any
    slope: Any


class Read(NamedTuple):
    slope: Any
    aT: Any
    h2T: Any
    v1: Any
    oT: Any
    q: Any
    k: Any
    v: Any
    qT: Any
    kT: Any
    lse: Any
    apart: Any
    hT: Any


class Back(NamedTuple):
    g: Any
    gz: Any
    gu: Any
    acc: Any
    go: Any
    goT: Any
    dqT: Any
    dk: Any
    dv: Any
    gq0: Any
    gq1: Any
    gq2: Any


class VecBufs(NamedTuple):
    tiles: Any
    got0: Any
    got1: Any
    got2: Any
    got3: Any
    sum: Any


def fill(space, kind, refs):
    vars(space).update(zip(kind._fields, refs))
    return space


def fields(kind):
    return len(kind._fields)


def block_buffers(length, width, ff, heads):
    wide, tall = ((length, width), BF16), ((width, length), BF16)
    own = Own(wide, ((length, ff), BF16), ((length, length), F32))
    saved = Saved(
        tall,
        wide,
        wide,
        wide,
        tall,
        tall,
        tall,
        ((heads, 1, length), F32),
        tall,
        ((length, width), F32),
        tall,
        ((ff, length), BF16),
        ((length, ff), BF16),
    )
    return own, saved


def forward_kernel(cfg, refs):
    shapes, sizes, length, slots, padded_slots = cfg
    count = len(shapes)
    it = iter(refs)

    def take(n):
        return [next(it) for _ in range(n)]

    shards = take(count)
    vectors = take(len(sizes))
    patches, index_ref, seg_ref = take(3)
    wholes_out = take(count)
    enc_vec_out, dec_vec_out = take(2)
    enc_saved_out = take(fields(Saved))
    dec_saved_out = take(fields(Saved))
    hid_t_out, dec_in_out, enc_apart_out, dec_apart_out, shown_out, shown_t_out, decoded_out = take(7)
    wholes = take(count)
    sent, got = take(count), take(count)
    vec_tile, vec_whole = take(2)
    enc, dec = types.SimpleNamespace(), types.SimpleNamespace()
    for block in (enc, dec):
        fill(block, Own, take(fields(Own)))
        fill(block, Saved, take(fields(Saved)))
    enc.vec, dec.vec, enc_up, dec_up, hid_t, dec_in, shown, shown_t = take(8)
    send_sem, recv_sem, out_sem = take(3)

    at = Place()
    at.greet()
    at.meet()
    gather = Gather(at, shapes, shards, wholes, vec_tile, vec_whole, sent, got, send_sem, recv_sem)
    outgoing = []

    def put(src, dst):
        copy = pltpu.make_async_copy(src, dst, out_sem.at[len(outgoing)])
        copy.start()
        outgoing.append(copy)

    vec_tile[...] = jnp.zeros((VEC_ROWS, 128), F32)
    for k, ref in enumerate(vectors):
        vec_tile[k : k + 1, : sizes[k]] = ref[...].astype(F32)

    def compute():
        index_row = index_ref[...]
        slot = lax.broadcasted_iota(jnp.int32, (padded_slots, length), 0)
        hit = slot == index_row
        shown[...] = jnp.where(hit, 1.0, 0.0).astype(BF16)
        seg_row = seg_ref[...].astype(F32)
        seg_col = jnp.broadcast_to(seg_row, (128, padded_slots)).T[:, :1]
        enc_seg_row = jnp.sum(jnp.where(hit, seg_col, 0.0), 0, keepdims=True)
        enc_seg_col = jnp.broadcast_to(enc_seg_row, (128, length)).T[:, :1]
        enc.apart[...] = jnp.where(enc_seg_col == enc_seg_row, 0.0, APART)
        yield None
        dec.apart[...] = jnp.where(seg_col == seg_row, 0.0, APART)
        yield "vec"
        pieces = [vec_whole[z, yx, c] for z in range(4) for yx in range(4) for c in range(2)]
        enc.vec[...] = spread([p[:8] for p in pieces], sizes[0], enc.vec.shape[1])
        dec.vec[...] = spread([p[8:] for p in pieces], sizes[8], dec.vec.shape[1])
        keep = lax.broadcasted_iota(jnp.int32, (8, 128), 0)
        up = [jnp.where(keep == ENC_UP_ROW - 16, p[16:], 0.0) for p in pieces]
        enc_up[...] = jnp.sum(spread(up, sizes[ENC_UP_ROW], enc_up.shape[1]), 0, keepdims=True)
        up = [jnp.where(keep == DEC_UP_ROW - 16, p[16:], 0.0) for p in pieces]
        dec_up[...] = jnp.sum(spread(up, sizes[DEC_UP_ROW], dec_up.shape[1]), 0, keepdims=True)
        put(enc.vec, enc_vec_out)
        put(dec.vec, dec_vec_out)
        put(enc.apart, enc_apart_out)
        put(dec.apart, dec_apart_out)
        put(shown, shown_out)
        turn(shown, shown_t, length)
        put(shown_t, shown_t_out)
        yield None

        def read_patches(rows, lanes=slice(None)):
            return patches[rows, lanes].astype(F32)

        def keep_hidden(j, value):
            low = value.astype(BF16)
            enc.h[:, at_tile(j, 256)] = low
            hid_t[at_tile(j, 256), :] = low.T

        names = Weights._fields
        width = patches.shape[1]
        for need in forward_block(
            enc, read_patches, length, width, HEADS, ENC_VEC, enc_up, Weights(*wholes[:4]), keep_hidden
        ):
            yield None if need is None else names.index(need)
        for key, out in zip(Saved._fields, enc_saved_out):
            put(getattr(enc, key), out)
        put(hid_t, hid_t_out)
        yield 4
        dec_width = dec.vec.shape[1]
        marks = shown[...]
        slot_col = lax.broadcasted_iota(jnp.int32, (padded_slots, 1), 0)
        empty = jnp.where(slot_col < slots, 1.0, 0.0) - jnp.sum(marks.astype(F32), 1, keepdims=True)

        def embed(j):
            value = dot(enc.h[...], column_tile(wholes[4], j, 256)) + dec.vec[0:1, at_tile(j, 256)]
            high = value.astype(BF16)
            low = (value - high.astype(F32)).astype(BF16)
            dec_in[:, at_tile(j, 256)] = (
                dot(marks, high) + dot(marks, low) + empty * dec.vec[1:2, at_tile(j, 256)]
            )

        loop(dec_width // 256, embed)
        put(dec_in, dec_in_out)
        yield None

        def read_in(rows, lanes=slice(None)):
            return dec_in[rows, lanes]

        def keep_decoded(j, value):
            decoded_out[:, at_tile(j, 256)] = value[:slots].astype(BF16)

        for need in forward_block(
            dec, read_in, padded_slots, dec_width, DHEADS, DEC_VEC, dec_up, Weights(*wholes[5:]), keep_decoded
        ):
            yield None if need is None else 5 + names.index(need)
        for key, out in zip(Saved._fields, dec_saved_out):
            put(getattr(dec, key), out)

    last = {"vec": 0}
    for chunk, part in enumerate(gather.chunks):
        if part is not None:
            last[part[0]] = chunk
    ready = -1
    work = compute()
    need = next(work)
    ended = False
    copied = set()
    for done in gather.steps():
        if done is not None:
            ready = done
            for m in range(count):
                if last[m] <= ready and m not in copied:
                    copied.add(m)
                    put(wholes[m], wholes_out[m])
        budget = PIECES
        while not ended and budget > 0 and (need is None or last[need] <= ready):
            try:
                need = next(work)
            except StopIteration:
                ended = True
            budget -= 1
    while not ended:
        try:
            need = next(work)
        except StopIteration:
            ended = True
    gather.finish()
    for copy in outgoing:
        copy.wait()


def forward_all(shards, vectors, patches, index, segments, row):
    shapes = [s.shape for s in shards]
    sizes = [v.shape[0] for v in vectors]
    count = len(shapes)
    length, width = patches.shape
    slots = -(-row // 32) * 32
    dec_width = 32 * sizes[8]
    ff, dec_ff = 32 * sizes[ENC_UP_ROW], 32 * sizes[DEC_UP_ROW]
    enc_own, enc_saved = block_buffers(length, width, ff, HEADS)
    dec_own, dec_saved = block_buffers(slots, dec_width, dec_ff, DHEADS)
    whole_shapes = [((4, 8 * r, c), BF16) for r, c in shapes]
    vec_shapes = [((8, width), F32), ((16, dec_width), F32)]
    extra = [((width, length), BF16), ((slots, dec_width), F32)]
    apart = [((length, length), F32), ((slots, slots), F32)]
    outs = whole_shapes + vec_shapes + list(enc_saved) + list(dec_saved) + extra + apart
    outs += [((slots, length), BF16), ((length, slots), BF16)]
    any_space = pl.BlockSpec(memory_space=pl.ANY)
    vmem = pl.BlockSpec(memory_space=pltpu.VMEM)
    out_specs = [any_space] * len(outs) + [vmem]
    out_shape = [jax.ShapeDtypeStruct(*o) for o in outs] + [jax.ShapeDtypeStruct((row, dec_width), BF16)]
    chunk_count = 1 + len(chunks_of(shapes)) + count
    scratch = whole_shapes + [((padded(r), c // 2), BF16) for r, c in shapes] * 2
    scratch += [((VEC_ROWS, 128), F32), ((4, 4, 2, VEC_ROWS, 128), F32)]
    scratch += list(enc_own) + list(enc_saved)
    scratch += list(dec_own) + list(dec_saved)
    scratch += vec_shapes + [((1, ff), F32), ((1, dec_ff), F32)] + extra + outs[-2:]
    scratch = [pltpu.VMEM(*s) for s in scratch]
    scratch += [
        pltpu.SemaphoreType.DMA((chunk_count, 11)),
        pltpu.SemaphoreType.DMA((chunk_count, 11)),
        pltpu.SemaphoreType.DMA((len(outs),)),
    ]
    cfg = (shapes, sizes, length, row, slots)

    def body(*refs):
        forward_kernel(cfg, refs)

    seg_row = jnp.pad(segments.reshape(1, row), ((0, 0), (0, slots - row)), constant_values=2)
    results = pl.pallas_call(
        body,
        out_shape=out_shape,
        in_specs=[vmem] * (count + len(sizes) + 3),
        out_specs=out_specs,
        scratch_shapes=scratch,
        compiler_params=pltpu.CompilerParams(
            collective_id=0, has_side_effects=True, vmem_limit_bytes=VMEM_BYTES
        ),
        name="gather_forward",
    )(*shards, *[v.reshape(1, -1) for v in vectors], patches, index.reshape(1, length), seg_row)
    it = iter(results)
    take = lambda n: [next(it) for _ in range(n)]
    wholes = take(count)
    enc_vec, dec_vec = take(2)
    enc_kept = fill(types.SimpleNamespace(), Saved, take(fields(Saved)))
    dec_kept = fill(types.SimpleNamespace(), Saved, take(fields(Saved)))
    hid_t, dec_in, enc_kept.apart, dec_kept.apart, shown, shown_t, decoded = take(7)
    return wholes, enc_vec, dec_vec, enc_kept, dec_kept, hid_t, dec_in, shown, shown_t, decoded


class Scatter:
    def __init__(self, at, shapes, grads, outs, bufs, vec, send_sem, recv_sem):
        self.at, self.shapes, self.grads, self.outs = at, shapes, grads, outs
        self.bufs, self.vec = bufs, vec
        self.send_sem, self.recv_sem = send_sem, recv_sem
        self.started = []
        self.parts = []
        self.begun = 0
        self.order = 0

    def send(self, src, dst, p, slot, partner):
        copy = pltpu.make_async_remote_copy(
            src_ref=src,
            dst_ref=dst,
            send_sem=self.send_sem.at[p, slot],
            recv_sem=self.recv_sem.at[p, slot],
            device_id=(partner,),
            device_id_type=MESH,
        )
        copy.start()
        self.started.append(copy)
        return copy

    def lanes(self, part, core):
        m, lane, lanes = part
        return pl.ds(pl.multiple_of(core * (self.shapes[m][1] // 2) + lane, 128), lanes)

    def block(self, part, z, yx):
        if part is None:
            return self.vec.tiles.at[z, yx, self.at.c]
        rows = 2 * self.shapes[part[0]][0]
        return self.grads[part[0]].at[z, pl.ds(pl.multiple_of(yx * rows, 16), rows), self.lanes(part, self.at.c)]

    def plane(self, part, z):
        return self.grads[part[0]].at[z, :, self.lanes(part, self.at.c)]

    def add(self, part, dst, src):
        if part is None:
            dst[...] += src[...]
            return
        rows = dst.shape[0]
        step = 48 if rows % 48 == 0 else 32

        def body(i):
            rows_here = at_tile(i, step)
            dst[rows_here, :] = dst[rows_here, :] + src[rows_here, :]

        loop(rows // step, body)

    def advance(self, entry):
        for copy in entry.flights:
            copy.wait_recv()
        if entry.part is None:
            self.finish_vec(entry.stage)
            flights = self.start_vec(entry.p, entry.stage)
        else:
            self.finish_stage(entry.part, entry.stage, entry.bufs)
            flights = self.start_stage(entry.p, entry.part, entry.stage, entry.bufs)
        self.order += 1
        vars(entry).update(stage=entry.stage + 1, flights=flights, tick=self.begun, order=self.order)

    def finish_vec(self, k):
        at, vec = self.at, self.vec
        if k == 1:
            own = vec.tiles.at[:, :, at.c]
            own[...] += vec.got0[...]
        elif k == 2:
            for j in range(2):
                for z in range(4):
                    self.block(None, z, at.bit1 * at.stride1 + j * at.stride2)[...] += vec.got1[j, z]
        elif k == 3:
            for z in range(4):
                self.block(None, z, at.here)[...] += vec.got2[z]
        elif k == 4:
            vec.sum[...] = self.block(None, at.z, at.here)[...] + vec.got3[0] + vec.got3[1] + vec.got3[2]

    def start_vec(self, p, k):
        at, vec, every = self.at, self.vec, slice(None)
        if k == 0:
            return [self.send(vec.tiles.at[:, :, 1 - at.c], vec.got0, p, 0, at.core)]
        if k == 1:
            away = (1 - at.bit1) * at.stride1
            return [
                self.send(self.block(None, every, away + j * at.stride2), vec.got1.at[j], p, 1 + j, at.first)
                for j in range(2)
            ]
        if k == 2:
            return [self.send(self.block(None, every, at.yx(False, True)), vec.got2, p, 3, at.second)]
        if k == 3:
            return [
                self.send(self.block(None, at.zs[i], at.here), vec.got3.at[i - 1], p, 3 + i, at.columns[i])
                for i in range(1, 4)
            ]
        return []

    def finish_stage(self, part, k, bufs):
        at = self.at
        got0, got1, got2, got3, final, got4 = bufs
        m, lane, lanes = part
        if k == 1:
            for z in range(4):
                self.add(part, self.plane(part, z), got0.at[z])
        elif k == 2:
            for j in range(2):
                for z in range(4):
                    self.add(part, self.block(part, z, at.bit1 * at.stride1 + j * at.stride2), got1.at[j, z])
        elif k == 3:
            for z in range(4):
                self.add(part, self.block(part, z, at.here), got2.at[z])
        elif k == 4:
            total = self.block(part, at.z, at.here)[...].astype(F32)
            for i in range(3):
                total = total + got3[i].astype(F32)
            rows = self.shapes[m][0]
            final[0] = total[:rows]
            final[1] = total[rows:]
        elif k == 5:
            half = self.shapes[m][1] // 2
            here = pl.ds(pl.multiple_of(at.c * half + lane, 128), lanes)
            there = pl.ds(pl.multiple_of((1 - at.c) * half + lane, 128), lanes)
            self.outs[m][:, here] = final[at.c]
            self.outs[m][:, there] = got4[...]

    def start_stage(self, p, part, k, bufs):
        at, every = self.at, slice(None)
        got0, got1, got2, got3, final, got4 = bufs
        m, lane, lanes = part
        away = (1 - at.bit1) * at.stride1
        if k == 0:
            return [self.send(self.grads[m].at[:, :, self.lanes(part, 1 - at.c)], got0, p, 0, at.core)]
        if k == 1:
            return [
                self.send(self.block(part, every, away + j * at.stride2), got1.at[j], p, 1 + j, at.first)
                for j in range(2)
            ]
        if k == 2:
            return [self.send(self.block(part, every, at.yx(False, True)), got2, p, 3, at.second)]
        if k == 3:
            return [
                self.send(self.block(part, at.zs[i], at.here), got3.at[i - 1], p, 3 + i, at.columns[i])
                for i in range(1, 4)
            ]
        if k == 4:
            return [self.send(final.at[1 - at.c], got4, p, 7, at.core)]
        return []

    def emit(self, *names):
        for m in names:
            for part in [None] if m is None else lane_parts(self.shapes, m):
                bufs = None if part is None else self.bufs[len(self.parts)]
                entry = types.SimpleNamespace(p=len(self.parts), part=part, stage=0, flights=[], bufs=bufs)
                self.parts.append(entry)
                self.advance(entry)

    def flying(self):
        return sorted((e for e in self.parts if e.stage < 6), key=lambda e: e.order)

    def tick(self, patience):
        self.begun += 1
        for entry in self.flying():
            if self.begun - entry.tick >= patience:
                self.advance(entry)

    def finish(self):
        while self.flying():
            self.advance(self.flying()[0])
        for copy in self.started:
            copy.wait_send()


def lane_parts(shapes, m):
    half = shapes[m][1] // 2
    if 32 * shapes[m][0] * shapes[m][1] * 2 <= 3 * 2**20:
        return [(m, 0, half)]
    low = half // 256 * 128
    return [(m, 0, half - low), (m, half - low, low)]


def scatter_shapes(shapes, order):
    scratch = []
    for name in order:
        for m, _, lanes in lane_parts(shapes, name):
            r = shapes[m][0]
            scratch.append(((4, 8 * r, lanes), BF16))
            scratch.append(((2, 4, 2 * r, lanes), BF16))
            scratch.append(((4, 2 * r, lanes), BF16))
            scratch.append(((3, 2 * r, lanes), BF16))
            scratch.append(((2, r, lanes), F32))
            scratch.append(((r, lanes), F32))
    return scratch


def collect(whole, width, d):
    lane = lax.broadcasted_iota(jnp.int32, (whole.shape[0], 128), 1)
    t, shift = divmod(d * width, 128)
    tile = whole[:, t * 128 : (t + 1) * 128]
    if shift:
        tile = pltpu.roll(tile, 128 - shift, 1)
    if shift + width > 128:
        after = pltpu.roll(whole[:, (t + 1) * 128 : (t + 2) * 128], 128 - shift, 1)
        tile = jnp.where(lane < 128 - shift, tile, after)
    return jnp.where(lane < width, tile, 0.0)


def norm_back(x, gain, grad):
    centred = x - jnp.mean(x, -1, keepdims=True)
    rate = lax.rsqrt(jnp.mean(centred * centred, -1, keepdims=True) + EPSILON)
    unit = centred * rate
    inner = grad * gain
    back = rate * (inner - jnp.mean(inner, -1, keepdims=True) - unit * jnp.mean(inner * unit, -1, keepdims=True))
    return back, grad * unit


def back_buffers(length, width, ff):
    wide, tall = ((length, width), BF16), ((width, length), BF16)
    wide32, tall32 = ((length, width), F32), ((width, length), F32)
    return Back(
        wide32, wide, ((length, ff), BF16), wide32, wide, tall, tall32, wide32, wide32, wide, wide, wide
    )


def row_chunk(length):
    return length // 2


def backward_block(b, need, read, length, width, heads, vec, up_grad, whole, emit):
    head = width // heads
    per = 128 // head
    scale = head ** (-0.5)
    size = 256
    chunk = row_chunk(length)
    ff = b.gu.shape[1]

    def keep(index, value, j=None):
        if j is None:
            b.dvec[index : index + 1, :] = value
        else:
            b.dvec[index : index + 1, at_tile(j, size)] = value

    def low(j):
        value = b.g[:, at_tile(j, size)]
        keep(vec.bd, jnp.sum(value, 0, keepdims=True), j)
        b.gz[:, at_tile(j, size)] = value.astype(BF16)

    loop(width // size, low)
    blocks = ff // 4 // size

    def feed(j):
        place = (j // blocks, at_tile(lax.rem(j, blocks), size), slice(None))
        grad = dot_nt(b.gz[...], whole.down[place]) * b.slope[:, at_tile(j, size)].astype(F32)
        up_grad[:, at_tile(j, size)] = jnp.sum(grad, 0, keepdims=True)
        b.gu[:, at_tile(j, size)] = grad.astype(BF16)
        whole.down[place] = dot(b.aT[at_tile(j, size), :], b.gz[...]).astype(BF16)

    count = ff // size
    for part in range(4):
        need(("down", part), ("slope", part), ("aT", part))
        loop(count // 4, lambda i, part=part: feed(i + part * (count // 4)))
        if part < 3:
            yield
    emit("down")
    yield
    need("up", "h2T")

    def lift(j, first):
        columns = at_tile(j, width)
        tile = whole.up[:, :, columns]
        part = dot_nt(b.gu[:, columns], tile.reshape(width, width))
        b.acc[...] = part if first else b.acc[...] + part

        def grad(i):
            lanes = pl.ds(pl.multiple_of(j * width + i * size, size), size)
            value = dot(b.h2T[...], b.gu[:, lanes]).astype(BF16)
            whole.up[:, :, lanes] = value.reshape(4, width // 4, size)

        loop(width // size, grad)

    lift(0, True)
    yield
    for j in range(1, ff // width):
        lift(j, False)
        if j < ff // width - 1:
            yield
    emit("up")
    yield
    need("v1", "out", "oT")
    zero = jnp.zeros((1, width), F32)

    def norm_two(i, sums):
        rows = at_tile(i, chunk)
        grad = b.acc[rows, :]
        back, terms = norm_back(b.v1[rows, :], b.vec[vec.gain2 : vec.gain2 + 1, :], grad)
        total = b.g[rows, :] + back
        b.g[rows, :] = total
        b.gz[rows, :] = total.astype(BF16)
        return (
            sums[0] + jnp.sum(terms, 0, keepdims=True),
            sums[1] + jnp.sum(grad, 0, keepdims=True),
            sums[2] + jnp.sum(total, 0, keepdims=True),
        )

    gain_sum, shift_sum, out_sum = lax.fori_loop(0, length // chunk, norm_two, (zero, zero, zero))
    keep(vec.gain2, gain_sum)
    keep(vec.bias2, shift_sum)
    keep(vec.bo, out_sum)
    span = width // 2
    for i in range(2):
        tile = whole.out[2 * i : 2 * i + 2].reshape(span, width)
        b.go[:, i * span : (i + 1) * span] = dot_nt(b.gz[...], tile).astype(BF16)

    def out_grad(j):
        value = dot(b.oT[...], b.gz[:, at_tile(j, size)]).astype(BF16)
        whole.out[:, :, at_tile(j, size)] = value.reshape(4, width // 4, size)

    loop(width // size, out_grad)
    emit("out")
    turn(b.go, b.goT, width)
    yield
    need("q", "k", "v", "qT", "kT", "lse", "apart")
    b.dk[...] = jnp.zeros((length, width), F32)
    b.dv[...] = jnp.zeros((length, width), F32)

    def attend(h):
        group = at_tile(h // per, 128)
        mine = at_tile(h, head)
        lane = lax.broadcasted_iota(jnp.int32, (length, 128), 1) // head == lax.rem(h, per)

        def only(ref):
            return jnp.where(lane, ref[:, group], jnp.zeros((), BF16))

        scores = dot(only(b.k), b.qT[group, :]) * (scale * LOG2E) + b.apart[...]
        probs = jnp.exp2(scores - b.lse[h])
        b.dv[:, group] += dot(probs.astype(BF16), only(b.go))
        back = dot(only(b.v), b.goT[group, :])
        centre = jnp.sum(probs * back, 0, keepdims=True)
        grad = (probs * (back - centre) * scale).astype(BF16)
        b.dk[:, group] += dot(grad, only(b.q))
        b.dqT[mine, :] = dot(b.kT[mine, :], grad)

    parts = 4
    for part in range(parts):
        loop(heads // parts, lambda i, part=part: attend(i + part * (heads // parts)))
        yield
    need("qkv", "hT")

    def query_grad(j):
        lanes = at_tile(j, 128)
        value = b.dqT[lanes, :].T
        b.dvec[vec.bq : vec.bq + 1, lanes] = jnp.sum(value, 0, keepdims=True)
        b.gq0[:, lanes] = value.astype(BF16)

    def rest_grad(j):
        lanes = at_tile(j, 128)
        value = b.dv[:, lanes]
        b.dvec[vec.bv : vec.bv + 1, lanes] = jnp.sum(value, 0, keepdims=True)
        b.gq2[:, lanes] = value.astype(BF16)
        b.gq1[:, lanes] = b.dk[:, lanes].astype(BF16)

    loop(width // 128, query_grad)
    loop(width // 128, rest_grad)
    for third in range(3):
        gq = (b.gq0, b.gq1, b.gq2)[third]
        tile = whole.qkv[:, :, third * width : (third + 1) * width].reshape(width, width)
        part = dot_nt(gq[...], tile)
        b.acc[...] = part if third == 0 else b.acc[...] + part

        def grad(i, gq=gq, third=third):
            value = dot(b.hT[...], gq[:, at_tile(i, size)]).astype(BF16)
            whole.qkv[:, :, pl.ds(pl.multiple_of(third * width + i * size, size), size)] = value.reshape(
                4, width // 4, size
            )

        loop(width // size, grad)
    emit("qkv")
    yield
    need("x")

    def norm_one(i, sums):
        rows = at_tile(i, chunk)
        grad = b.acc[rows, :]
        back, terms = norm_back(read(rows), b.vec[vec.gain1 : vec.gain1 + 1, :], grad)
        b.g[rows, :] = b.g[rows, :] + back
        return (sums[0] + jnp.sum(terms, 0, keepdims=True), sums[1] + jnp.sum(grad, 0, keepdims=True))

    gain_sum, shift_sum = lax.fori_loop(0, length // chunk, norm_one, (zero, zero))
    keep(vec.gain1, gain_sum)
    keep(vec.bias1, shift_sum)
    yield


class Inputs:
    def __init__(self, sem):
        self.sem, self.count, self.flights = sem, 0, {}

    def fetch(self, name, src, dst):
        copy = pltpu.make_async_copy(src, dst, self.sem.at[self.count])
        copy.start()
        self.count += 1
        self.flights[name] = copy

    def need(self, *names):
        for name in names:
            if name in self.flights:
                self.flights.pop(name).wait()

    def finish(self):
        self.need(*list(self.flights))


def fetch_block(inputs, weights, saved, whole, b):
    quarter = b.slope.shape[1] // 4
    for i in range(4):
        part = pl.ds(i * quarter, quarter)
        inputs.fetch(("down", i), weights.down.at[i], whole.down.at[i])
        inputs.fetch(("slope", i), saved.slope.at[:, part], b.slope.at[:, part])
        inputs.fetch(("aT", i), saved.aT.at[part], b.aT.at[part])
    for key, src, dst in (
        ("up", weights.up, whole.up),
        ("h2T", saved.h2T, b.h2T),
        ("v1", saved.v1, b.v1),
        ("out", weights.out, whole.out),
        ("oT", saved.oT, b.oT),
        ("q", saved.q, b.q),
        ("k", saved.k, b.k),
        ("v", saved.v, b.v),
        ("qT", saved.qT, b.qT),
        ("kT", saved.kT, b.kT),
        ("lse", saved.lse, b.lse),
        ("apart", saved.apart, b.apart),
        ("qkv", weights.qkv, whole.qkv),
        ("hT", saved.hT, b.hT),
    ):
        inputs.fetch(key, src, dst)


def decoder_back_kernel(cfg, refs):
    shapes, slots, padded_slots, width, length, parts = cfg
    it = iter(refs)

    def take(n):
        return [next(it) for _ in range(n)]

    cotangent, dec_vec = take(2)
    weights, embed_in = Weights(*take(4)), next(it)
    saved = Read(*take(fields(Read)))
    dec_in, shown, shown_t, hid_t = take(4)
    outs = take(3)
    qkv_out, embed_out, hidden_out, dvec_out, up_out = take(5)
    whole, embed_whole = Weights(*take(4)), next(it)
    b = fill(types.SimpleNamespace(), Read, take(fields(Read)))
    here_in, here_shown, here_shown_t, here_hid_t = take(4)
    fill(b, Back, take(fields(Back)))
    b.dvec, up_grad, grad_hidden = take(3)
    bufs = [take(6) for _ in range(parts)]
    send_sem, recv_sem, in_sem, out_sem = take(4)
    b.vec = dec_vec
    inputs = Inputs(in_sem)
    fetch_block(inputs, weights, saved, whole, b)
    inputs.fetch("x", dec_in, here_in)
    inputs.fetch(0, shown, here_shown)
    inputs.fetch(1, shown_t, here_shown_t)
    inputs.fetch(2, hid_t, here_hid_t)
    inputs.fetch(3, embed_in, embed_whole)
    at = Place()
    at.greet()
    sent = ("out", "up", "down")
    scatter = Scatter(at, shapes, [whole.out, whole.up, whole.down], outs, bufs, None, send_sem, recv_sem)
    b.dvec[...] = jnp.zeros(b.dvec.shape, F32)
    for j in range(width // 128):
        lanes = slice(j * 128, (j + 1) * 128)
        b.g[slots // 16 * 16 :, lanes] = jnp.zeros((padded_slots - slots // 16 * 16, 128), F32)
        b.g[:slots, lanes] = cotangent[:, lanes].astype(F32)

    def emit(name):
        if name == "down":
            at.meet()
        if name in sent:
            scatter.emit(sent.index(name))

    def read(rows):
        return here_in[rows, :]

    for _ in backward_block(
        b, inputs.need, read, padded_slots, width, DHEADS, DEC_VEC, up_grad, whole, emit
    ):
        scatter.tick(DEC_PATIENCE)
    outgoing = []

    def put(src, dst):
        copy = pltpu.make_async_copy(src, dst, out_sem.at[len(outgoing)])
        copy.start()
        outgoing.append(copy)

    put(whole.qkv, qkv_out)
    inputs.need(0, 1, 2, 3)
    slot_col = lax.broadcasted_iota(jnp.int32, (padded_slots, 1), 0)
    empty = jnp.where(slot_col < slots, 1.0, 0.0) - jnp.sum(here_shown[...].astype(F32), 1, keepdims=True)

    def embed(j):
        lanes = at_tile(j, 256)
        value = b.g[:, lanes]
        b.dvec[1:2, lanes] = jnp.sum(empty * value, 0, keepdims=True)
        high = value.astype(BF16)
        low = (value - high.astype(F32)).astype(BF16)
        rows = dot(here_shown_t[...], high) + dot(here_shown_t[...], low)
        b.dvec[0:1, lanes] = jnp.sum(rows, 0, keepdims=True)
        b.gz[:length, lanes] = rows.astype(BF16)

    loop(width // 256, embed)
    wide = embed_whole.shape[1] * 4
    for i in range(2):
        tile = embed_whole[2 * i : 2 * i + 2].reshape(wide // 2, width)
        grad_hidden[:, i * (wide // 2) : (i + 1) * (wide // 2)] = dot_nt(b.gz[:length, :], tile)

    def embed_grad(j):
        value = dot(here_hid_t[...], b.gz[:length, at_tile(j, 256)]).astype(BF16)
        embed_whole[:, :, at_tile(j, 256)] = value.reshape(4, wide // 4, 256)

    loop(width // 256, embed_grad)
    put(embed_whole, embed_out)
    put(grad_hidden, hidden_out)
    put(b.dvec, dvec_out)
    put(up_grad, up_out)
    inputs.finish()
    scatter.finish()
    for copy in outgoing:
        copy.wait()


def struct(shape):
    return jax.ShapeDtypeStruct(*shape)


def decoder_back(weights, kept, cotangent, dec_vec, dec_in, shown, shown_t, hid_t, row):
    wide = [(w.shape[1] // 8, w.shape[2]) for w in weights]
    shapes = wide[1:4]
    slots, width = dec_in.shape
    length = shown.shape[1]
    ff = wide[2][1]
    any_space = pl.BlockSpec(memory_space=pl.ANY)
    vmem = pl.BlockSpec(memory_space=pltpu.VMEM)
    back = back_buffers(slots, width, ff)
    whole_shapes = [(w.shape, BF16) for w in weights]
    read = [getattr(kept, key) for key in Read._fields]
    read_shapes = [(a.shape, a.dtype) for a in read]
    other = [(a.shape, a.dtype) for a in (dec_in, shown, shown_t, hid_t)]
    results = [((16, width), F32), ((1, ff), F32), ((length, hid_t.shape[0]), F32)]
    scratch = [pltpu.VMEM(*s) for s in whole_shapes + read_shapes + other + list(back) + results]
    sums = scatter_shapes(shapes, (2, 1, 0))
    scratch += [pltpu.VMEM(*s) for s in sums]
    scratch += [
        pltpu.SemaphoreType.DMA((8, 8)),
        pltpu.SemaphoreType.DMA((8, 8)),
        pltpu.SemaphoreType.DMA((32,)),
        pltpu.SemaphoreType.DMA((8,)),
    ]
    outs = [(s, F32) for s in shapes]
    out_shape = [struct(s) for s in outs + [whole_shapes[0], whole_shapes[4], results[2], results[0], results[1]]]
    cfg = (shapes, row, slots, width, length, len(sums) // 6)

    def body(*refs):
        decoder_back_kernel(cfg, refs)

    return pl.pallas_call(
        body,
        out_shape=out_shape,
        in_specs=[vmem] * 2 + [any_space] * (5 + len(read) + 4),
        out_specs=[vmem] * 3 + [any_space] * 5,
        scratch_shapes=scratch,
        compiler_params=pltpu.CompilerParams(
            collective_id=1, has_side_effects=True, vmem_limit_bytes=VMEM_BYTES
        ),
        name="decoder_back",
    )(cotangent, dec_vec, *weights, *read, dec_in, shown, shown_t, hid_t)


def encoder_back_kernel(cfg, refs):
    shapes, sizes, length, width, parts = cfg
    count = len(shapes)
    it = iter(refs)

    def take(n):
        return [next(it) for _ in range(n)]

    enc_vec, dec_dvec, dec_up_grad = take(3)
    weights = Weights(*take(4))
    dec_grads = take(2)
    saved = Read(*take(fields(Read)))
    patches, hidden = take(2)
    outs = take(count)
    vec_outs = take(len(sizes))
    patch_out = next(it)
    whole = Weights(*take(4))
    dec_whole = take(2)
    b = fill(types.SimpleNamespace(), Read, take(fields(Read)))
    x = next(it)
    fill(b, Back, take(fields(Back)))
    b.dvec, up_grad = take(2)
    bufs = [take(6) for _ in range(parts)]
    vec = VecBufs(*take(6))
    send_sem, recv_sem, in_sem, out_sem = take(4)
    b.vec = enc_vec
    inputs = Inputs(in_sem)
    inputs.fetch(0, dec_grads[0], dec_whole[0])
    inputs.fetch("g", hidden, b.g)
    inputs.fetch(1, dec_grads[1], dec_whole[1])
    fetch_block(inputs, weights, saved, whole, b)
    inputs.fetch("x", patches, x)
    at = Place()
    at.greet()
    at.meet()
    scatter = Scatter(at, shapes, dec_whole + list(whole), outs, bufs, vec, send_sem, recv_sem)
    for m in range(2):
        inputs.need(m)
        scatter.emit(m)

    def emit(name):
        scatter.emit(2 + Weights._fields.index(name))

    def read(rows):
        return x[rows, :].astype(F32)

    inputs.need("g")
    for _ in backward_block(b, inputs.need, read, length, width, HEADS, ENC_VEC, up_grad, whole, emit):
        scatter.tick(ENC_PATIENCE)
    copy = pltpu.make_async_copy(b.g, patch_out, out_sem.at[0])
    copy.start()
    enc_dvec, dec_dvec = b.dvec[...], dec_dvec[...]
    ups, dec_ups = up_grad[...], dec_up_grad[...]
    for d in range(32):
        tile = vec.tiles.at[d // 8, d // 2 % 4, d % 2]
        tile[0:8] = collect(enc_dvec, sizes[0], d)
        row = lax.broadcasted_iota(jnp.int32, (8, 128), 0)
        up = jnp.broadcast_to(collect(ups, sizes[ENC_UP_ROW], d), (8, 128))
        dec_up = jnp.broadcast_to(collect(dec_ups, sizes[DEC_UP_ROW], d), (8, 128))
        both = collect(dec_dvec, sizes[8], d)
        tile[8:16] = both[:8]
        tile[16:24] = jnp.where(row == ENC_UP_ROW - 16, up, jnp.where(row == DEC_UP_ROW - 16, dec_up, both[8:]))
    scatter.emit(None)
    inputs.finish()
    scatter.finish()
    for k, ref in enumerate(vec_outs):
        ref[...] = vec.sum[k : k + 1, : sizes[k]]
    copy.wait()


def encoder_back(weights, dec_grads, kept, enc_vec, dec_dvec, dec_up_grad, patches, grad_hidden, sizes):
    shapes = [(w.shape[1] // 8, w.shape[2]) for w in list(dec_grads) + list(weights)]
    length, width = patches.shape
    ff = weights[2].shape[2]
    any_space = pl.BlockSpec(memory_space=pl.ANY)
    vmem = pl.BlockSpec(memory_space=pltpu.VMEM)
    back = back_buffers(length, width, ff)
    whole_shapes = [(w.shape, BF16) for w in list(weights) + list(dec_grads)]
    read = [getattr(kept, key) for key in Read._fields]
    read_shapes = [(a.shape, a.dtype) for a in read]
    scratch = whole_shapes + read_shapes + [(patches.shape, BF16)] + list(back)
    scratch += [((8, width), F32), ((1, ff), F32)]
    sums = scatter_shapes(shapes, (0, 1, 5, 4, 3, 2))
    scratch += sums
    tile = (VEC_ROWS, 128)
    scratch += [((4, 4, 2) + tile, F32), ((4, 4) + tile, F32), ((2, 4) + tile, F32), ((4,) + tile, F32)]
    scratch += [((3,) + tile, F32), (tile, F32)]
    scratch = [pltpu.VMEM(*s) for s in scratch]
    scratch += [
        pltpu.SemaphoreType.DMA((14, 8)),
        pltpu.SemaphoreType.DMA((14, 8)),
        pltpu.SemaphoreType.DMA((32,)),
        pltpu.SemaphoreType.DMA((1,)),
    ]
    outs = [(s, F32) for s in shapes] + [((1, s), F32) for s in sizes] + [((length, width), F32)]
    cfg = (shapes, sizes, length, width, len(sums) // 6)

    def body(*refs):
        encoder_back_kernel(cfg, refs)

    results = pl.pallas_call(
        body,
        out_shape=[struct(s) for s in outs],
        in_specs=[vmem] * 3 + [any_space] * (4 + 2 + len(read) + 2),
        out_specs=[vmem] * (len(shapes) + len(sizes)) + [any_space],
        scratch_shapes=scratch,
        compiler_params=pltpu.CompilerParams(
            collective_id=2, has_side_effects=True, vmem_limit_bytes=VMEM_BYTES
        ),
        name="encoder_back",
    )(enc_vec, dec_dvec, dec_up_grad, *weights, *dec_grads, *read, patches, grad_hidden)
    count = len(shapes)
    return results[:count], results[count : count + len(sizes)], results[-1]


def settle(arrays):
    count = len(arrays)
    vmem = pl.BlockSpec(memory_space=pltpu.VMEM)

    def body(*refs):
        for src, dst in zip(refs[:count], refs[count:]):
            rows = src.shape[0]
            if rows % 16 == 0 and rows > 128:
                loop(rows // 16, lambda i, src=src, dst=dst: dst.__setitem__(at_tile(i, 16), src[at_tile(i, 16)]))
            else:
                dst[...] = src[...]

    return pl.pallas_call(
        body,
        out_shape=[jax.ShapeDtypeStruct(a.shape, a.dtype) for a in arrays],
        in_specs=[vmem] * count,
        out_specs=[vmem] * count,
        compiler_params=pltpu.CompilerParams(vmem_limit_bytes=VMEM_BYTES),
        name="settle",
    )(*arrays)


def widen(value):
    return value.astype(jnp.float32)


def layer_norm(stream, gain, shift):
    row_mean = jnp.mean(stream, -1, keepdims=True)
    centred = stream - row_mean
    row_var = jnp.mean(centred * centred, -1, keepdims=True)
    return centred * lax.rsqrt(row_var + EPSILON) * gain + shift


def norm_pull(stream, gain, shift, grad_out):
    pull = jax.vjp(layer_norm, stream, gain, shift)[1]
    return pull(grad_out)


def gelu_exact(value):
    return jax.nn.gelu(value, approximate=False)


def split_heads(rows, head_count):
    batch, length, model_width = rows.shape
    return rows.reshape(batch, length, head_count, model_width // head_count)


def masked_scores(query_heads, key_heads, same_doc, score_scale):
    scores = (
        jnp.einsum("bqhd,bkhd->bhqk", query_heads, key_heads, preferred_element_type=jnp.float32)
        * score_scale
    )
    return jnp.where(same_doc[:, None], scores, -1000000000.0)


def attend_forward(query_rows, key_rows, value_rows, same_doc, head_count, score_scale):
    batch, length, model_width = query_rows.shape
    scores = masked_scores(
        split_heads(query_rows, head_count),
        split_heads(key_rows, head_count),
        same_doc,
        score_scale,
    )
    row_max = jnp.max(scores, -1, keepdims=True)
    expo = jnp.exp(scores - row_max)
    row_sum = jnp.sum(expo, -1, keepdims=True)
    att_probs = (expo / row_sum).astype(jnp.bfloat16)
    mixed = jnp.einsum(
        "bhqk,bkhd->bqhd",
        att_probs,
        split_heads(value_rows, head_count),
        preferred_element_type=jnp.float32,
    )
    return (mixed.reshape(batch, length, model_width), row_max + jnp.log(row_sum))


def attend_backward(
    query_rows, key_rows, value_rows, same_doc, log_total, grad_mixed, head_count, score_scale
):
    batch, length, model_width = query_rows.shape
    query_heads = split_heads(query_rows, head_count)
    key_heads = split_heads(key_rows, head_count)
    value_heads = split_heads(value_rows, head_count)
    grad_heads = split_heads(grad_mixed, head_count)
    att_probs = jnp.exp(masked_scores(query_heads, key_heads, same_doc, score_scale) - log_total)
    grad_value = jnp.einsum(
        "bhqk,bqhd->bkhd",
        att_probs.astype(jnp.bfloat16),
        grad_heads,
        preferred_element_type=jnp.float32,
    )
    grad_probs = jnp.einsum(
        "bqhd,bkhd->bhqk", grad_heads, value_heads, preferred_element_type=jnp.float32
    )
    centre = jnp.sum(att_probs * grad_probs, -1, keepdims=True)
    grad_scores = (att_probs * (grad_probs - centre) * score_scale).astype(jnp.bfloat16)
    grad_query = jnp.einsum(
        "bhqk,bkhd->bqhd", grad_scores, key_heads, preferred_element_type=jnp.float32
    )
    grad_key = jnp.einsum(
        "bhqk,bqhd->bkhd", grad_scores, query_heads, preferred_element_type=jnp.float32
    )
    rows = batch * length
    return (
        grad_query.reshape(rows, model_width),
        grad_key.reshape(rows, model_width),
        grad_value.reshape(rows, model_width),
    )


def block_forward(stream, params, seg_ids, head_count):
    (
        gain_one,
        shift_one,
        w_qkv,
        query_bias,
        value_bias,
        w_out,
        out_bias,
        gain_two,
        shift_two,
        w_up,
        up_bias,
        w_down,
        down_bias,
    ) = params
    row_count, model_width = stream.shape
    batch, length = seg_ids.shape
    score_scale = (model_width // head_count) ** (-0.5)
    normed = layer_norm(stream, widen(gain_one), widen(shift_one)).astype(jnp.bfloat16)
    joined = jnp.dot(normed, w_qkv, preferred_element_type=jnp.float32)
    query_rows = (joined[:, :model_width] + widen(query_bias)).astype(jnp.bfloat16)
    key_rows = joined[:, model_width : 2 * model_width].astype(jnp.bfloat16)
    value_rows = (joined[:, 2 * model_width :] + widen(value_bias)).astype(jnp.bfloat16)
    same_doc = seg_ids[:, :, None] == seg_ids[:, None, :]
    shape_three = (batch, length, model_width)
    mixed, log_total = attend_forward(
        query_rows.reshape(shape_three),
        key_rows.reshape(shape_three),
        value_rows.reshape(shape_three),
        same_doc,
        head_count,
        score_scale,
    )
    attended = mixed.reshape(row_count, model_width).astype(jnp.bfloat16)
    middle = stream + jnp.dot(attended, w_out, preferred_element_type=jnp.float32) + widen(out_bias)
    normed_two = layer_norm(middle, widen(gain_two), widen(shift_two)).astype(jnp.bfloat16)
    hidden_up = jnp.dot(normed_two, w_up, preferred_element_type=jnp.float32) + widen(up_bias)
    activated = gelu_exact(hidden_up).astype(jnp.bfloat16)
    result = (
        middle + jnp.dot(activated, w_down, preferred_element_type=jnp.float32) + widen(down_bias)
    )
    saved = (
        stream,
        middle,
        normed,
        query_rows,
        key_rows,
        value_rows,
        log_total,
        attended,
        normed_two,
        hidden_up,
        activated,
    )
    return (result, saved)


def back_feed(grad_out, params, saved):
    (
        gain_one,
        shift_one,
        w_qkv,
        query_bias,
        value_bias,
        w_out,
        out_bias,
        gain_two,
        shift_two,
        w_up,
        up_bias,
        w_down,
        down_bias,
    ) = params
    (
        stream,
        middle,
        normed,
        query_rows,
        key_rows,
        value_rows,
        log_total,
        attended,
        normed_two,
        hidden_up,
        activated,
    ) = saved
    grad_low = grad_out.astype(jnp.bfloat16)
    grad_down_bias = jnp.sum(grad_out, 0)
    grad_down = jnp.einsum("rf,rw->fw", activated, grad_low, preferred_element_type=jnp.float32)
    grad_act = jnp.einsum("rw,fw->rf", grad_low, w_down, preferred_element_type=jnp.float32)
    grad_hidden = jax.vjp(gelu_exact, hidden_up)[1](grad_act)[0]
    grad_hidden_low = grad_hidden.astype(jnp.bfloat16)
    grad_up_bias = jnp.sum(grad_hidden, 0)
    grad_up = jnp.einsum(
        "rd,rf->df", normed_two, grad_hidden_low, preferred_element_type=jnp.float32
    )
    grad_normed_two = jnp.einsum(
        "rf,df->rd", grad_hidden_low, w_up, preferred_element_type=jnp.float32
    )
    grad_mid_norm, grad_gain_two, grad_shift_two = norm_pull(
        middle, widen(gain_two), widen(shift_two), grad_normed_two
    )
    grad_middle = grad_out + grad_mid_norm
    return (
        grad_middle,
        (grad_gain_two, grad_shift_two, grad_up, grad_up_bias, grad_down, grad_down_bias),
    )


def back_attend(grad_middle, params, seg_ids, head_count, saved):
    (
        gain_one,
        shift_one,
        w_qkv,
        query_bias,
        value_bias,
        w_out,
        out_bias,
        gain_two,
        shift_two,
        w_up,
        up_bias,
        w_down,
        down_bias,
    ) = params
    (
        stream,
        middle,
        normed,
        query_rows,
        key_rows,
        value_rows,
        log_total,
        attended,
        normed_two,
        hidden_up,
        activated,
    ) = saved
    row_count, model_width = stream.shape
    batch, length = seg_ids.shape
    score_scale = (model_width // head_count) ** (-0.5)
    grad_middle_low = grad_middle.astype(jnp.bfloat16)
    grad_out_bias = jnp.sum(grad_middle, 0)
    grad_w_out = jnp.einsum(
        "rv,rw->vw", attended, grad_middle_low, preferred_element_type=jnp.float32
    )
    grad_attended = jnp.einsum(
        "rw,vw->rv", grad_middle_low, w_out, preferred_element_type=jnp.float32
    ).astype(jnp.bfloat16)
    same_doc = seg_ids[:, :, None] == seg_ids[:, None, :]
    shape_three = (batch, length, model_width)
    grad_query, grad_key, grad_value = attend_backward(
        query_rows.reshape(shape_three),
        key_rows.reshape(shape_three),
        value_rows.reshape(shape_three),
        same_doc,
        log_total,
        grad_attended.reshape(shape_three),
        head_count,
        score_scale,
    )
    grad_query_bias = jnp.sum(grad_query, 0)
    grad_value_bias = jnp.sum(grad_value, 0)
    grad_joined = jnp.concatenate([grad_query, grad_key, grad_value], 1).astype(jnp.bfloat16)
    grad_qkv = jnp.einsum("rd,rc->dc", normed, grad_joined, preferred_element_type=jnp.float32)
    grad_normed = jnp.einsum("rc,dc->rd", grad_joined, w_qkv, preferred_element_type=jnp.float32)
    grad_in_norm, grad_gain_one, grad_shift_one = norm_pull(
        stream, widen(gain_one), widen(shift_one), grad_normed
    )
    grads = (
        grad_gain_one,
        grad_shift_one,
        grad_qkv,
        grad_query_bias,
        grad_value_bias,
        grad_w_out,
        grad_out_bias,
    )
    return (grad_middle + grad_in_norm, grads)


def block_backward(grad_out, params, seg_ids, head_count, saved):
    grad_middle, feed_grads = back_feed(grad_out, params, saved)
    grad_in, attend_grads = back_attend(grad_middle, params, seg_ids, head_count, saved)
    return (grad_in, attend_grads + feed_grads)


def by_collectives(a):
    seq_count = a.segments.shape[0] // ROW
    seg_ids = a.segments.reshape(seq_count, ROW)
    vis_slots = a.visible_index.reshape(seq_count, VIS)
    enc_seg = jnp.take_along_axis(seg_ids, vis_slots, 1)
    seq_index = jnp.arange(seq_count, dtype=jnp.int32)[:, None]
    matrices = [lax.all_gather(m, AXIS, axis=0, tiled=True) for m in matrices_of(a)]
    joined = lax.all_gather(jnp.concatenate(vectors_of(a)), AXIS, axis=0)
    sizes = [v.shape[0] for v in vectors_of(a)]
    vectors, start = [], 0
    for size in sizes:
        vectors.append(joined[:, start : start + size].reshape(-1))
        start += size
    whole = Arguments(a.patches, a.visible_index, a.segments, a.cotangent, *in_order(matrices, vectors))
    hidden, enc_saved = block_forward(widen(a.patches), encoder_of(whole), enc_seg, HEADS)
    hidden_low = hidden.astype(jnp.bfloat16)
    embedded = jnp.dot(hidden_low, whole.embed_weight, preferred_element_type=jnp.float32) + widen(
        whole.embed_bias
    )
    embedded = embedded.reshape(seq_count, VIS, DD)
    dec_in = (
        jnp.broadcast_to(widen(whole.mask_token), (seq_count, ROW, DD))
        .at[seq_index, vis_slots]
        .set(embedded)
    )
    dec_in = dec_in.reshape(seq_count * ROW, DD)
    decoded, dec_saved = block_forward(dec_in, decoder_of(whole), seg_ids, DHEADS)
    grad_dec_in, dec_grads = block_backward(
        widen(a.cotangent), decoder_of(whole), seg_ids, DHEADS, dec_saved
    )
    grad_dec_in = grad_dec_in.reshape(seq_count, ROW, DD)
    shown_slots = jnp.zeros((seq_count, ROW), jnp.float32).at[seq_index, vis_slots].set(1.0)
    grad_mask = jnp.sum((1.0 - shown_slots)[:, :, None] * grad_dec_in, (0, 1))
    grad_embedded = grad_dec_in[seq_index, vis_slots].reshape(seq_count * VIS, DD)
    grad_embed_b = jnp.sum(grad_embedded, 0)
    grad_embedded_low = grad_embedded.astype(jnp.bfloat16)
    grad_embed_w = jnp.einsum(
        "rd,re->de", hidden_low, grad_embedded_low, preferred_element_type=jnp.float32
    )
    grad_hidden = jnp.einsum(
        "re,de->rd", grad_embedded_low, whole.embed_weight, preferred_element_type=jnp.float32
    )
    grad_patches, enc_grads = block_backward(grad_hidden, encoder_of(whole), enc_seg, HEADS, enc_saved)
    grads = Arguments(None, None, None, None, *enc_grads, grad_embed_w, grad_embed_b, grad_mask, *dec_grads)
    sums = [lax.psum_scatter(m, AXIS, scatter_dimension=0, tiled=True) for m in matrices_of(grads)]
    joined = jnp.concatenate([v.reshape(-1, size) for v, size in zip(vectors_of(grads), sizes)], 1)
    joined = lax.psum_scatter(joined, AXIS, scatter_dimension=0, tiled=True).reshape(-1)
    vector_sums, start = [], 0
    for size in sizes:
        vector_sums.append(joined[start : start + size])
        start += size
    return (decoded.astype(jnp.bfloat16), grad_patches) + in_order(sums, vector_sums)


def fits(a):
    return (
        lax.axis_size(AXIS) == 32
        and a.segments.shape[0] == ROW
        and a.patches.shape[0] == VIS
        and all(m.shape[0] % 8 == 0 and m.shape[1] % 256 == 0 for m in matrices_of(a))
        and all(v.shape[0] <= 128 for v in vectors_of(a))
    )


def by_kernels(a):
    vectors = vectors_of(a)
    sizes = [v.shape[0] for v in vectors]
    wholes, enc_vec, dec_vec, enc_kept, dec_kept, hid_t, dec_in, shown, shown_t, decoded = forward_all(
        matrices_of(a), vectors, a.patches, a.visible_index, a.segments, ROW
    )
    *dec_sums, qkv, embed, grad_hidden, dec_dvec, dec_up = decoder_back(
        wholes[5:] + [wholes[4]], dec_kept, a.cotangent, dec_vec, dec_in, shown, shown_t, hid_t, ROW
    )
    (dec_qkv, embed, *enc_sums), vec_sums, grad_patches = encoder_back(
        wholes[:4], [qkv, embed], enc_kept, enc_vec, dec_dvec, dec_up, a.patches, grad_hidden, sizes
    )
    sums = in_order(list(enc_sums) + [embed, dec_qkv] + list(dec_sums), vec_sums)
    results = settle((decoded, grad_patches) + sums)
    shapes = (None,) * 4 + tuple(v.shape for v in a[4:])
    return tuple(results[:2]) + tuple(r.reshape(-1) if len(s) == 1 else r for r, s in zip(results[2:], shapes[4:]))


def on_device(*arguments):
    a = Arguments(*arguments)
    return by_kernels(a) if fits(a) else by_collectives(a)


def solution(mesh):
    count = len(Arguments._fields)
    vectors = vectors_of(Arguments(*range(count)))
    specs = [P(AXIS) if i in (1, 2) or i in vectors else P(AXIS, None) for i in range(count)]
    return jax.shard_map(
        on_device,
        mesh=mesh,
        in_specs=tuple(specs),
        out_specs=tuple([P(AXIS, None)] * 2 + specs[4:]),
        check_vma=False,
    )
```

```python
import types
from typing import Any, NamedTuple

import jax
import jax.numpy as jnp
from jax import lax
from jax.experimental import pallas as pl
from jax.experimental.pallas import tpu as pltpu
from jax.sharding import PartitionSpec as P

AXIS = "fsdp"
MESH = pl.DeviceIdType.MESH
VMEM_BYTES = 63 * 2**20
F32, BF16 = jnp.float32, jnp.bfloat16
EPSILON = 1e-06
HEADS, DHEADS = 12, 16
LOG2E = 1.4426950408889634
APART = -(2.0**100)
ROOT_HALF = 0.7071067811865476
ROOT_TWO_PI = 0.3989422804014327
VEC_ROWS = 24
PIECES = 4
LAGS = (0, 1, 2, 3, 4)
GATHER_ORDER = (4, 6, 1, 0, 2, 3, 5, 7, 8)
DEC_PATIENCE, ENC_PATIENCE = 4, 4
ENC_UP_ROW, DEC_UP_ROW = 18, 19
DD = 512
ROW = 529
VIS = 384


class Arguments(NamedTuple):
    patches: Any
    visible_index: Any
    segments: Any
    cotangent: Any
    enc_norm1_gain: Any
    enc_norm1_bias: Any
    enc_qkv: Any
    enc_query_bias: Any
    enc_value_bias: Any
    enc_out: Any
    enc_out_bias: Any
    enc_norm2_gain: Any
    enc_norm2_bias: Any
    enc_up: Any
    enc_up_bias: Any
    enc_down: Any
    enc_down_bias: Any
    embed_weight: Any
    embed_bias: Any
    mask_token: Any
    dec_norm1_gain: Any
    dec_norm1_bias: Any
    dec_qkv: Any
    dec_query_bias: Any
    dec_value_bias: Any
    dec_out: Any
    dec_out_bias: Any
    dec_norm2_gain: Any
    dec_norm2_bias: Any
    dec_up: Any
    dec_up_bias: Any
    dec_down: Any
    dec_down_bias: Any


def matrices_of(a):
    return (
        a.enc_qkv,
        a.enc_out,
        a.enc_up,
        a.enc_down,
        a.embed_weight,
        a.dec_qkv,
        a.dec_out,
        a.dec_up,
        a.dec_down,
    )


def vectors_of(a):
    return (
        a.enc_norm1_gain,
        a.enc_norm1_bias,
        a.enc_query_bias,
        a.enc_value_bias,
        a.enc_out_bias,
        a.enc_norm2_gain,
        a.enc_norm2_bias,
        a.enc_down_bias,
        a.embed_bias,
        a.mask_token,
        a.dec_norm1_gain,
        a.dec_norm1_bias,
        a.dec_query_bias,
        a.dec_value_bias,
        a.dec_out_bias,
        a.dec_norm2_gain,
        a.dec_norm2_bias,
        a.dec_down_bias,
        a.enc_up_bias,
        a.dec_up_bias,
    )


def encoder_of(a):
    return (
        a.enc_norm1_gain,
        a.enc_norm1_bias,
        a.enc_qkv,
        a.enc_query_bias,
        a.enc_value_bias,
        a.enc_out,
        a.enc_out_bias,
        a.enc_norm2_gain,
        a.enc_norm2_bias,
        a.enc_up,
        a.enc_up_bias,
        a.enc_down,
        a.enc_down_bias,
    )


def decoder_of(a):
    return (
        a.dec_norm1_gain,
        a.dec_norm1_bias,
        a.dec_qkv,
        a.dec_query_bias,
        a.dec_value_bias,
        a.dec_out,
        a.dec_out_bias,
        a.dec_norm2_gain,
        a.dec_norm2_bias,
        a.dec_up,
        a.dec_up_bias,
        a.dec_down,
        a.dec_down_bias,
    )


def in_order(matrices, vectors):
    places = Arguments(*range(len(Arguments._fields)))
    found = dict(zip(matrices_of(places) + vectors_of(places), tuple(matrices) + tuple(vectors)))
    return tuple(found[place] for place in sorted(found))


def dot(a, b):
    return jnp.dot(a, b, preferred_element_type=F32)


def dot_nt(a, b):
    return lax.dot_general(a, b, (((1,), (1,)), ((), ())), preferred_element_type=F32)


def at_tile(j, size):
    return pl.ds(pl.multiple_of(j * size, size), size)


def loop(count, body):
    def step(i, carry):
        body(i)
        return carry

    lax.fori_loop(0, count, step, 0)


class Place:
    def __init__(self):
        me = lax.axis_index(AXIS)
        self.c = c = lax.rem(me, 2)
        x = lax.rem(me // 2, 2)
        y = lax.rem(me // 4, 2)
        self.z = lax.rem(me // 8, 4)
        self.stride1 = 1 + c
        self.stride2 = 2 - c
        self.bit1 = x * (1 - c) + y * c
        self.bit2 = y * (1 - c) + x * c
        self.here = 2 * y + x
        self.core = me + 1 - 2 * c
        self.first = me + 2 * self.stride1 * (1 - 2 * self.bit1)
        self.second = me + 2 * self.stride2 * (1 - 2 * self.bit2)
        self.zs = [lax.rem(self.z + i, 4) for i in range(4)]
        self.columns = [me + 8 * (z - self.z) for z in self.zs]

    def yx(self, flip1, flip2):
        bit1 = 1 - self.bit1 if flip1 else self.bit1
        bit2 = 1 - self.bit2 if flip2 else self.bit2
        return bit1 * self.stride1 + bit2 * self.stride2

    def greet(self):
        for partner in [self.core, self.first, self.second] + self.columns[1:]:
            pl.semaphore_signal(pltpu.get_barrier_semaphore(), inc=1, device_id=(partner,), device_id_type=MESH)

    def meet(self):
        pl.semaphore_wait(pltpu.get_barrier_semaphore(), 6)


def padded(rows):
    return -(-rows // 16) * 16


def chunks_of(shapes):
    out = []
    for m, (rows, columns) in enumerate(shapes):
        half = columns // 2
        if 32 * rows * columns * 2 <= 2 * 2**20 and m != len(shapes) - 1:
            out.append((m, 0, 2 * rows, 0, half))
        elif rows % 16 == 0:
            out.append((m, 0, rows, 0, half))
            out.append((m, rows, rows, 0, half))
        else:
            low = half // 256 * 128
            out.append((m, 0, 2 * rows, 0, half - low))
            out.append((m, 0, 2 * rows, half - low, low))
    return out


class Gather:
    def __init__(self, at, shapes, shards, wholes, vec_tile, vec_whole, sent, got, send_sem, recv_sem):
        self.at, self.shapes, self.shards, self.wholes = at, shapes, shards, wholes
        self.vec_tile, self.vec_whole = vec_tile, vec_whole
        self.sent, self.got = sent, got
        self.send_sem, self.recv_sem = send_sem, recv_sem
        self.chunks = [None] + sorted(chunks_of(shapes), key=lambda part: GATHER_ORDER.index(part[0]))
        self.started = []
        self.flights = {}

    def send(self, src, dst, chunk, slot, partner):
        copy = pltpu.make_async_remote_copy(
            src_ref=src,
            dst_ref=dst,
            send_sem=self.send_sem.at[chunk, slot],
            recv_sem=self.recv_sem.at[chunk, slot],
            device_id=(partner,),
            device_id_type=MESH,
        )
        copy.start()
        self.started.append(copy)
        return copy

    def view(self, chunk, z, yx):
        if chunk == 0:
            return self.vec_whole.at[z, yx, self.at.c]
        m, row, rows, lane, lanes = self.chunks[chunk]
        chip_rows, half = 2 * self.shapes[m][0], self.shapes[m][1] // 2
        start = pl.multiple_of(yx * chip_rows + row, 16)
        first = pl.multiple_of(self.at.c * half + lane, 128)
        return self.wholes[m].at[z, pl.ds(start, rows), pl.ds(first, lanes)]

    def my_half(self, m, mine):
        half = self.shapes[m][1] // 2
        low, high = self.shards[m][:, :half].astype(F32), self.shards[m][:, half:].astype(F32)
        return jnp.where(self.at.c == 0, low, high) if mine else jnp.where(self.at.c == 0, high, low)

    def swap(self, m):
        rows, columns = self.shapes[m]
        value = self.my_half(m, False)
        extra = padded(rows) - rows
        if extra:
            value = jnp.concatenate([value, jnp.zeros((extra, columns // 2), F32)], 0)
        self.sent[m][...] = value.astype(BF16)
        self.flights["swap", m] = self.send(self.sent[m], self.got[m], len(self.chunks) + m, 0, self.at.core)

    def place(self, m):
        at, (rows, columns) = self.at, self.shapes[m]
        self.flights["swap", m].wait_recv()
        other = self.got[m][...].astype(F32)[:rows]
        mine = self.my_half(m, True)
        both = jnp.concatenate([jnp.where(at.c == 0, mine, other), jnp.where(at.c == 0, other, mine)], 0)
        half = columns // 2
        lanes = pl.ds(pl.multiple_of(at.c * half, 128), half)
        row = pl.ds(pl.multiple_of(at.here * 2 * rows, 16), 2 * rows)
        self.wholes[m][at.z, row, lanes] = both.astype(BF16)

    def stage(self, chunk, k):
        at, flights = self.at, self.flights
        every = slice(None)
        if k == 0:
            if chunk == 0:
                self.vec_whole[at.z, at.here, at.c] = self.vec_tile[...]
            elif self.chunks[chunk][1] == 0 and self.chunks[chunk][3] == 0:
                self.place(self.chunks[chunk][0])
            own = self.view(chunk, at.z, at.here)
            flights[chunk, 0] = [self.send(own, own, chunk, i, at.columns[i]) for i in range(1, 4)]
        elif k == 1:
            for copy in flights[chunk, 0]:
                copy.wait_recv()
            part = self.view(chunk, every, at.here)
            flights[chunk, 1] = [
                self.send(part, part, chunk, 4, at.second),
                self.send(part, part, chunk, 5, at.first),
            ]
            flights[chunk, "core"] = [self.send(part, part, chunk, 7, at.core)]
        elif k == 2:
            flights[chunk, 1][0].wait_recv()
            part = self.view(chunk, every, at.yx(False, True))
            flights[chunk, 2] = self.send(part, part, chunk, 6, at.first)
            flights[chunk, "core"].append(self.send(part, part, chunk, 8, at.core))
            flights[chunk, 1][1].wait_recv()
            part = self.view(chunk, every, at.yx(True, False))
            flights[chunk, "core"].append(self.send(part, part, chunk, 9, at.core))
        elif k == 3:
            flights[chunk, 2].wait_recv()
            part = self.view(chunk, every, at.yx(True, True))
            flights[chunk, "core"].append(self.send(part, part, chunk, 10, at.core))
        elif k == 4:
            for copy in flights[chunk, "core"]:
                copy.wait_recv()

    def steps(self):
        swaps = list(GATHER_ORDER)
        for _ in range(2):
            self.swap(swaps.pop(0))
        count = len(self.chunks)
        for step in range(count + LAGS[-1]):
            done = None
            if swaps:
                self.swap(swaps.pop(0))
            for k, lag in enumerate(LAGS):
                if 0 <= step - lag < count:
                    self.stage(step - lag, k)
                    if k == 4:
                        done = step - lag
            yield done

    def finish(self):
        for copy in self.started:
            copy.wait_send()


def spread(tiles, width, out_width):
    lane = lax.broadcasted_iota(jnp.int32, tiles[0].shape, 1)
    whole = [jnp.zeros(tiles[0].shape, F32) for _ in range(out_width // 128)]
    for d, tile in enumerate(tiles):
        t, shift = divmod(d * width, 128)
        rolled = pltpu.roll(tile, shift, 1) if shift else tile
        over = shift + width - 128
        if over <= 0:
            whole[t] = whole[t] + rolled
        else:
            whole[t] = whole[t] + jnp.where(lane >= shift, rolled, 0.0)
            whole[t + 1] = whole[t + 1] + jnp.where(lane < over, rolled, 0.0)
    return jnp.concatenate(whole, 1)


def normed_rows(rows, gain, shift):
    centred = rows - jnp.mean(rows, -1, keepdims=True)
    variance = jnp.mean(centred * centred, -1, keepdims=True)
    return centred * lax.rsqrt(variance + EPSILON) * gain + shift


def norm_into(read, gain, shift, out, out_t, length, width):
    chunk = length // 2
    loop(
        length // chunk,
        lambda i: out.__setitem__(
            (at_tile(i, chunk), slice(None)), normed_rows(read(at_tile(i, chunk)), gain(), shift()).astype(BF16)
        ),
    )
    turn(out, out_t, width)


def turn(src, dst, width):
    def body(j):
        dst[at_tile(j, 128), :] = src[:, at_tile(j, 128)].T

    loop(width // 128, body)


def turn_back(src, dst, width):
    def body(j):
        dst[:, at_tile(j, 128)] = src[at_tile(j, 128), :].T

    loop(width // 128, body)


def column_tile(whole, j, size):
    tile = whole[:, :, at_tile(j, size)]
    return tile.reshape(tile.shape[0] * tile.shape[1], size)


def forward_block(b, read, length, width, heads, vec, up_bias, whole, finish):
    head = width // heads
    per = 128 // head
    scale = head ** (-0.5) * LOG2E
    size = 256

    def row(index, j=None):
        if j is None:
            return b.vec[index : index + 1, :]
        return b.vec[index : index + 1, at_tile(j, size)]

    norm_into(read, lambda: row(vec.gain1), lambda: row(vec.bias1), b.h, b.hT, length, width)
    yield "qkv"
    tiles = width // size

    def project(third, key, out, out_t):
        def body(j):
            value = dot(b.h[...], column_tile(whole.qkv, third * tiles + j, size))
            if key is not None:
                value = value + row(key, j)
            value = value.astype(BF16)
            out[:, at_tile(j, size)] = value
            out_t[at_tile(j, size), :] = value.T

        loop(tiles, body)

    project(0, vec.bq, b.q, b.qT)
    yield None
    project(1, None, b.k, b.kT)
    yield None
    project(2, vec.bv, b.v, b.vT)
    yield None

    def attend(h):
        group = at_tile(h // per, 128)
        lane = lax.broadcasted_iota(jnp.int32, (length, 128), 1) // head
        keys = jnp.where(lane == lax.rem(h, per), b.k[:, group], jnp.zeros((), BF16))
        scores = dot(keys, b.qT[group, :]) * scale + b.apart[...]
        top = jnp.max(scores, 0, keepdims=True)
        expo = jnp.exp2(scores - top)
        total = jnp.sum(expo, 0, keepdims=True)
        probs = (expo * (1.0 / total)).astype(BF16)
        mine = at_tile(h, head)
        b.oT[mine, :] = dot(b.vT[mine, :], probs).astype(BF16)
        b.lse[h] = top + jnp.log2(total)

    parts = 4
    for part in range(parts):
        loop(heads // parts, lambda i, part=part: attend(i + part * (heads // parts)))
        yield None
    turn_back(b.oT, b.h, width)
    yield "out"

    def middle(j):
        b.v1[:, at_tile(j, size)] = (
            read(slice(None), at_tile(j, size)) + dot(b.h[...], column_tile(whole.out, j, size)) + row(vec.bo, j)
        )

    loop(tiles, middle)
    norm_into(
        lambda rows: b.v1[rows, :], lambda: row(vec.gain2), lambda: row(vec.bias2), b.h, b.h2T, length, width
    )
    yield "up"

    def lift(j):
        u = dot(b.h[...], column_tile(whole.up, j, size)) + up_bias[:, at_tile(j, size)]
        share = 0.5 + 0.5 * lax.erf(u * ROOT_HALF)
        slope = share + u * (jnp.exp2(u * u * (-0.5 * LOG2E)) * ROOT_TWO_PI)
        a = (u * share).astype(BF16)
        b.a[:, at_tile(j, size)] = a
        b.aT[at_tile(j, size), :] = a.T
        b.slope[:, at_tile(j, size)] = slope.astype(BF16)

    ups = b.a.shape[1] // size
    for part in range(4):
        loop(ups // 4, lambda i, part=part: lift(i + part * (ups // 4)))
        yield None
    yield "down"

    def drop(j):
        finish(
            j,
            b.v1[:, at_tile(j, size)] + dot(b.a[...], column_tile(whole.down, j, size)) + row(vec.bd, j),
        )

    loop(tiles, drop)
    yield None


class VecRows(NamedTuple):
    gain1: int
    bias1: int
    bq: int
    bv: int
    bo: int
    gain2: int
    bias2: int
    bd: int


ENC_VEC, DEC_VEC = VecRows(*range(8)), VecRows(*range(2, 10))


class Weights(NamedTuple):
    qkv: Any
    out: Any
    up: Any
    down: Any


class Own(NamedTuple):
    h: Any
    a: Any
    apart: Any


class Saved(NamedTuple):
    hT: Any
    q: Any
    k: Any
    v: Any
    qT: Any
    kT: Any
    vT: Any
    lse: Any
    oT: Any
    v1: Any
    h2T: Any
    aT: Any
    slope: Any


class Read(NamedTuple):
    slope: Any
    aT: Any
    h2T: Any
    v1: Any
    oT: Any
    q: Any
    k: Any
    v: Any
    qT: Any
    kT: Any
    lse: Any
    apart: Any
    hT: Any


class Back(NamedTuple):
    g: Any
    gz: Any
    gu: Any
    acc: Any
    go: Any
    goT: Any
    dqT: Any
    dk: Any
    dv: Any
    gq0: Any
    gq1: Any
    gq2: Any


class VecBufs(NamedTuple):
    tiles: Any
    got0: Any
    got1: Any
    got2: Any
    got3: Any
    sum: Any


def fill(space, kind, refs):
    vars(space).update(zip(kind._fields, refs))
    return space


def fields(kind):
    return len(kind._fields)


def block_buffers(length, width, ff, heads):
    wide, tall = ((length, width), BF16), ((width, length), BF16)
    own = Own(wide, ((length, ff), BF16), ((length, length), F32))
    saved = Saved(
        tall,
        wide,
        wide,
        wide,
        tall,
        tall,
        tall,
        ((heads, 1, length), F32),
        tall,
        ((length, width), F32),
        tall,
        ((ff, length), BF16),
        ((length, ff), BF16),
    )
    return own, saved


def forward_kernel(cfg, refs):
    shapes, sizes, length, slots, padded_slots = cfg
    count = len(shapes)
    it = iter(refs)

    def take(n):
        return [next(it) for _ in range(n)]

    shards = take(count)
    vectors = take(len(sizes))
    patches, index_ref, seg_ref = take(3)
    wholes_out = take(count)
    enc_vec_out, dec_vec_out = take(2)
    enc_saved_out = take(fields(Saved))
    dec_saved_out = take(fields(Saved))
    hid_t_out, dec_in_out, enc_apart_out, dec_apart_out, shown_out, shown_t_out, decoded_out = take(7)
    wholes = take(count)
    sent, got = take(count), take(count)
    vec_tile, vec_whole = take(2)
    enc, dec = types.SimpleNamespace(), types.SimpleNamespace()
    for block in (enc, dec):
        fill(block, Own, take(fields(Own)))
        fill(block, Saved, take(fields(Saved)))
    enc.vec, dec.vec, enc_up, dec_up, hid_t, dec_in, shown, shown_t = take(8)
    send_sem, recv_sem, out_sem = take(3)

    at = Place()
    at.greet()
    at.meet()
    gather = Gather(at, shapes, shards, wholes, vec_tile, vec_whole, sent, got, send_sem, recv_sem)
    outgoing = []

    def put(src, dst):
        copy = pltpu.make_async_copy(src, dst, out_sem.at[len(outgoing)])
        copy.start()
        outgoing.append(copy)

    vec_tile[...] = jnp.zeros((VEC_ROWS, 128), F32)
    for k, ref in enumerate(vectors):
        vec_tile[k : k + 1, : sizes[k]] = ref[...].astype(F32)

    def compute():
        index_row = index_ref[...]
        slot = lax.broadcasted_iota(jnp.int32, (padded_slots, length), 0)
        hit = slot == index_row
        shown[...] = jnp.where(hit, 1.0, 0.0).astype(BF16)
        seg_row = seg_ref[...].astype(F32)
        seg_col = jnp.broadcast_to(seg_row, (128, padded_slots)).T[:, :1]
        enc_seg_row = jnp.sum(jnp.where(hit, seg_col, 0.0), 0, keepdims=True)
        enc_seg_col = jnp.broadcast_to(enc_seg_row, (128, length)).T[:, :1]
        enc.apart[...] = jnp.where(enc_seg_col == enc_seg_row, 0.0, APART)
        yield None
        dec.apart[...] = jnp.where(seg_col == seg_row, 0.0, APART)
        yield "vec"
        pieces = [vec_whole[z, yx, c] for z in range(4) for yx in range(4) for c in range(2)]
        enc.vec[...] = spread([p[:8] for p in pieces], sizes[0], enc.vec.shape[1])
        dec.vec[...] = spread([p[8:] for p in pieces], sizes[8], dec.vec.shape[1])
        keep = lax.broadcasted_iota(jnp.int32, (8, 128), 0)
        up = [jnp.where(keep == ENC_UP_ROW - 16, p[16:], 0.0) for p in pieces]
        enc_up[...] = jnp.sum(spread(up, sizes[ENC_UP_ROW], enc_up.shape[1]), 0, keepdims=True)
        up = [jnp.where(keep == DEC_UP_ROW - 16, p[16:], 0.0) for p in pieces]
        dec_up[...] = jnp.sum(spread(up, sizes[DEC_UP_ROW], dec_up.shape[1]), 0, keepdims=True)
        put(enc.vec, enc_vec_out)
        put(dec.vec, dec_vec_out)
        put(enc.apart, enc_apart_out)
        put(dec.apart, dec_apart_out)
        put(shown, shown_out)
        turn(shown, shown_t, length)
        put(shown_t, shown_t_out)
        yield None

        def read_patches(rows, lanes=slice(None)):
            return patches[rows, lanes].astype(F32)

        def keep_hidden(j, value):
            low = value.astype(BF16)
            enc.h[:, at_tile(j, 256)] = low
            hid_t[at_tile(j, 256), :] = low.T

        names = Weights._fields
        width = patches.shape[1]
        for need in forward_block(
            enc, read_patches, length, width, HEADS, ENC_VEC, enc_up, Weights(*wholes[:4]), keep_hidden
        ):
            yield None if need is None else names.index(need)
        for key, out in zip(Saved._fields, enc_saved_out):
            put(getattr(enc, key), out)
        put(hid_t, hid_t_out)
        yield 4
        dec_width = dec.vec.shape[1]
        marks = shown[...]
        slot_col = lax.broadcasted_iota(jnp.int32, (padded_slots, 1), 0)
        empty = jnp.where(slot_col < slots, 1.0, 0.0) - jnp.sum(marks.astype(F32), 1, keepdims=True)

        def embed(j):
            value = dot(enc.h[...], column_tile(wholes[4], j, 256)) + dec.vec[0:1, at_tile(j, 256)]
            high = value.astype(BF16)
            low = (value - high.astype(F32)).astype(BF16)
            dec_in[:, at_tile(j, 256)] = (
                dot(marks, high) + dot(marks, low) + empty * dec.vec[1:2, at_tile(j, 256)]
            )

        loop(dec_width // 256, embed)
        put(dec_in, dec_in_out)
        yield None

        def read_in(rows, lanes=slice(None)):
            return dec_in[rows, lanes]

        def keep_decoded(j, value):
            decoded_out[:, at_tile(j, 256)] = value[:slots].astype(BF16)

        for need in forward_block(
            dec, read_in, padded_slots, dec_width, DHEADS, DEC_VEC, dec_up, Weights(*wholes[5:]), keep_decoded
        ):
            yield None if need is None else 5 + names.index(need)
        for key, out in zip(Saved._fields, dec_saved_out):
            put(getattr(dec, key), out)

    last = {"vec": 0}
    for chunk, part in enumerate(gather.chunks):
        if part is not None:
            last[part[0]] = chunk
    ready = -1
    work = compute()
    need = next(work)
    ended = False
    copied = set()
    for done in gather.steps():
        if done is not None:
            ready = done
            for m in range(count):
                if last[m] <= ready and m not in copied:
                    copied.add(m)
                    put(wholes[m], wholes_out[m])
        budget = PIECES
        while not ended and budget > 0 and (need is None or last[need] <= ready):
            try:
                need = next(work)
            except StopIteration:
                ended = True
            budget -= 1
    while not ended:
        try:
            need = next(work)
        except StopIteration:
            ended = True
    gather.finish()
    for copy in outgoing:
        copy.wait()


def forward_all(shards, vectors, patches, index, segments, row):
    shapes = [s.shape for s in shards]
    sizes = [v.shape[0] for v in vectors]
    count = len(shapes)
    length, width = patches.shape
    slots = -(-row // 32) * 32
    dec_width = 32 * sizes[8]
    ff, dec_ff = 32 * sizes[ENC_UP_ROW], 32 * sizes[DEC_UP_ROW]
    enc_own, enc_saved = block_buffers(length, width, ff, HEADS)
    dec_own, dec_saved = block_buffers(slots, dec_width, dec_ff, DHEADS)
    whole_shapes = [((4, 8 * r, c), BF16) for r, c in shapes]
    vec_shapes = [((8, width), F32), ((16, dec_width), F32)]
    extra = [((width, length), BF16), ((slots, dec_width), F32)]
    apart = [((length, length), F32), ((slots, slots), F32)]
    outs = whole_shapes + vec_shapes + list(enc_saved) + list(dec_saved) + extra + apart
    outs += [((slots, length), BF16), ((length, slots), BF16)]
    any_space = pl.BlockSpec(memory_space=pl.ANY)
    vmem = pl.BlockSpec(memory_space=pltpu.VMEM)
    out_specs = [any_space] * len(outs) + [vmem]
    out_shape = [jax.ShapeDtypeStruct(*o) for o in outs] + [jax.ShapeDtypeStruct((row, dec_width), BF16)]
    chunk_count = 1 + len(chunks_of(shapes)) + count
    scratch = whole_shapes + [((padded(r), c // 2), BF16) for r, c in shapes] * 2
    scratch += [((VEC_ROWS, 128), F32), ((4, 4, 2, VEC_ROWS, 128), F32)]
    scratch += list(enc_own) + list(enc_saved)
    scratch += list(dec_own) + list(dec_saved)
    scratch += vec_shapes + [((1, ff), F32), ((1, dec_ff), F32)] + extra + outs[-2:]
    scratch = [pltpu.VMEM(*s) for s in scratch]
    scratch += [
        pltpu.SemaphoreType.DMA((chunk_count, 11)),
        pltpu.SemaphoreType.DMA((chunk_count, 11)),
        pltpu.SemaphoreType.DMA((len(outs),)),
    ]
    cfg = (shapes, sizes, length, row, slots)

    def body(*refs):
        forward_kernel(cfg, refs)

    seg_row = jnp.pad(segments.reshape(1, row), ((0, 0), (0, slots - row)), constant_values=2)
    results = pl.pallas_call(
        body,
        out_shape=out_shape,
        in_specs=[vmem] * (count + len(sizes) + 3),
        out_specs=out_specs,
        scratch_shapes=scratch,
        compiler_params=pltpu.CompilerParams(
            collective_id=0, has_side_effects=True, vmem_limit_bytes=VMEM_BYTES
        ),
        name="gather_forward",
    )(*shards, *[v.reshape(1, -1) for v in vectors], patches, index.reshape(1, length), seg_row)
    it = iter(results)
    take = lambda n: [next(it) for _ in range(n)]
    wholes = take(count)
    enc_vec, dec_vec = take(2)
    enc_kept = fill(types.SimpleNamespace(), Saved, take(fields(Saved)))
    dec_kept = fill(types.SimpleNamespace(), Saved, take(fields(Saved)))
    hid_t, dec_in, enc_kept.apart, dec_kept.apart, shown, shown_t, decoded = take(7)
    return wholes, enc_vec, dec_vec, enc_kept, dec_kept, hid_t, dec_in, shown, shown_t, decoded


class Scatter:
    def __init__(self, at, shapes, grads, outs, bufs, vec, send_sem, recv_sem):
        self.at, self.shapes, self.grads, self.outs = at, shapes, grads, outs
        self.bufs, self.vec = bufs, vec
        self.send_sem, self.recv_sem = send_sem, recv_sem
        self.started = []
        self.parts = []
        self.begun = 0
        self.order = 0

    def send(self, src, dst, p, slot, partner):
        copy = pltpu.make_async_remote_copy(
            src_ref=src,
            dst_ref=dst,
            send_sem=self.send_sem.at[p, slot],
            recv_sem=self.recv_sem.at[p, slot],
            device_id=(partner,),
            device_id_type=MESH,
        )
        copy.start()
        self.started.append(copy)
        return copy

    def lanes(self, part, core):
        m, lane, lanes = part
        return pl.ds(pl.multiple_of(core * (self.shapes[m][1] // 2) + lane, 128), lanes)

    def block(self, part, z, yx):
        if part is None:
            return self.vec.tiles.at[z, yx, self.at.c]
        rows = 2 * self.shapes[part[0]][0]
        return self.grads[part[0]].at[z, pl.ds(pl.multiple_of(yx * rows, 16), rows), self.lanes(part, self.at.c)]

    def plane(self, part, z):
        return self.grads[part[0]].at[z, :, self.lanes(part, self.at.c)]

    def add(self, part, dst, src):
        if part is None:
            dst[...] += src[...]
            return
        rows = dst.shape[0]
        step = 48 if rows % 48 == 0 else 32

        def body(i):
            rows_here = at_tile(i, step)
            dst[rows_here, :] = dst[rows_here, :] + src[rows_here, :]

        loop(rows // step, body)

    def advance(self, entry):
        for copy in entry.flights:
            copy.wait_recv()
        if entry.part is None:
            self.finish_vec(entry.stage)
            flights = self.start_vec(entry.p, entry.stage)
        else:
            self.finish_stage(entry.part, entry.stage, entry.bufs)
            flights = self.start_stage(entry.p, entry.part, entry.stage, entry.bufs)
        self.order += 1
        vars(entry).update(stage=entry.stage + 1, flights=flights, tick=self.begun, order=self.order)

    def finish_vec(self, k):
        at, vec = self.at, self.vec
        if k == 1:
            own = vec.tiles.at[:, :, at.c]
            own[...] += vec.got0[...]
        elif k == 2:
            for j in range(2):
                for z in range(4):
                    self.block(None, z, at.bit1 * at.stride1 + j * at.stride2)[...] += vec.got1[j, z]
        elif k == 3:
            for z in range(4):
                self.block(None, z, at.here)[...] += vec.got2[z]
        elif k == 4:
            vec.sum[...] = self.block(None, at.z, at.here)[...] + vec.got3[0] + vec.got3[1] + vec.got3[2]

    def start_vec(self, p, k):
        at, vec, every = self.at, self.vec, slice(None)
        if k == 0:
            return [self.send(vec.tiles.at[:, :, 1 - at.c], vec.got0, p, 0, at.core)]
        if k == 1:
            away = (1 - at.bit1) * at.stride1
            return [
                self.send(self.block(None, every, away + j * at.stride2), vec.got1.at[j], p, 1 + j, at.first)
                for j in range(2)
            ]
        if k == 2:
            return [self.send(self.block(None, every, at.yx(False, True)), vec.got2, p, 3, at.second)]
        if k == 3:
            return [
                self.send(self.block(None, at.zs[i], at.here), vec.got3.at[i - 1], p, 3 + i, at.columns[i])
                for i in range(1, 4)
            ]
        return []

    def finish_stage(self, part, k, bufs):
        at = self.at
        got0, got1, got2, got3, final, got4 = bufs
        m, lane, lanes = part
        if k == 1:
            for z in range(4):
                self.add(part, self.plane(part, z), got0.at[z])
        elif k == 2:
            for j in range(2):
                for z in range(4):
                    self.add(part, self.block(part, z, at.bit1 * at.stride1 + j * at.stride2), got1.at[j, z])
        elif k == 3:
            for z in range(4):
                self.add(part, self.block(part, z, at.here), got2.at[z])
        elif k == 4:
            total = self.block(part, at.z, at.here)[...].astype(F32)
            for i in range(3):
                total = total + got3[i].astype(F32)
            rows = self.shapes[m][0]
            final[0] = total[:rows]
            final[1] = total[rows:]
        elif k == 5:
            half = self.shapes[m][1] // 2
            here = pl.ds(pl.multiple_of(at.c * half + lane, 128), lanes)
            there = pl.ds(pl.multiple_of((1 - at.c) * half + lane, 128), lanes)
            self.outs[m][:, here] = final[at.c]
            self.outs[m][:, there] = got4[...]

    def start_stage(self, p, part, k, bufs):
        at, every = self.at, slice(None)
        got0, got1, got2, got3, final, got4 = bufs
        m, lane, lanes = part
        away = (1 - at.bit1) * at.stride1
        if k == 0:
            return [self.send(self.grads[m].at[:, :, self.lanes(part, 1 - at.c)], got0, p, 0, at.core)]
        if k == 1:
            return [
                self.send(self.block(part, every, away + j * at.stride2), got1.at[j], p, 1 + j, at.first)
                for j in range(2)
            ]
        if k == 2:
            return [self.send(self.block(part, every, at.yx(False, True)), got2, p, 3, at.second)]
        if k == 3:
            return [
                self.send(self.block(part, at.zs[i], at.here), got3.at[i - 1], p, 3 + i, at.columns[i])
                for i in range(1, 4)
            ]
        if k == 4:
            return [self.send(final.at[1 - at.c], got4, p, 7, at.core)]
        return []

    def emit(self, *names):
        for m in names:
            for part in [None] if m is None else lane_parts(self.shapes, m):
                bufs = None if part is None else self.bufs[len(self.parts)]
                entry = types.SimpleNamespace(p=len(self.parts), part=part, stage=0, flights=[], bufs=bufs)
                self.parts.append(entry)
                self.advance(entry)

    def flying(self):
        return sorted((e for e in self.parts if e.stage < 6), key=lambda e: e.order)

    def tick(self, patience):
        self.begun += 1
        for entry in self.flying():
            if self.begun - entry.tick >= patience:
                self.advance(entry)

    def finish(self):
        while self.flying():
            self.advance(self.flying()[0])
        for copy in self.started:
            copy.wait_send()


def lane_parts(shapes, m):
    half = shapes[m][1] // 2
    if 32 * shapes[m][0] * shapes[m][1] * 2 <= 3 * 2**20:
        return [(m, 0, half)]
    low = half // 256 * 128
    return [(m, 0, half - low), (m, half - low, low)]


def scatter_shapes(shapes, order):
    scratch = []
    for name in order:
        for m, _, lanes in lane_parts(shapes, name):
            r = shapes[m][0]
            scratch.append(((4, 8 * r, lanes), BF16))
            scratch.append(((2, 4, 2 * r, lanes), BF16))
            scratch.append(((4, 2 * r, lanes), BF16))
            scratch.append(((3, 2 * r, lanes), BF16))
            scratch.append(((2, r, lanes), F32))
            scratch.append(((r, lanes), F32))
    return scratch


def collect(whole, width, d):
    lane = lax.broadcasted_iota(jnp.int32, (whole.shape[0], 128), 1)
    t, shift = divmod(d * width, 128)
    tile = whole[:, t * 128 : (t + 1) * 128]
    if shift:
        tile = pltpu.roll(tile, 128 - shift, 1)
    if shift + width > 128:
        after = pltpu.roll(whole[:, (t + 1) * 128 : (t + 2) * 128], 128 - shift, 1)
        tile = jnp.where(lane < 128 - shift, tile, after)
    return jnp.where(lane < width, tile, 0.0)


def norm_back(x, gain, grad):
    centred = x - jnp.mean(x, -1, keepdims=True)
    rate = lax.rsqrt(jnp.mean(centred * centred, -1, keepdims=True) + EPSILON)
    unit = centred * rate
    inner = grad * gain
    back = rate * (inner - jnp.mean(inner, -1, keepdims=True) - unit * jnp.mean(inner * unit, -1, keepdims=True))
    return back, grad * unit


def back_buffers(length, width, ff):
    wide, tall = ((length, width), BF16), ((width, length), BF16)
    wide32, tall32 = ((length, width), F32), ((width, length), F32)
    return Back(
        wide32, wide, ((length, ff), BF16), wide32, wide, tall, tall32, wide32, wide32, wide, wide, wide
    )


def row_chunk(length):
    return length // 2


def backward_block(b, need, read, length, width, heads, vec, up_grad, whole, emit):
    head = width // heads
    per = 128 // head
    scale = head ** (-0.5)
    size = 256
    chunk = row_chunk(length)
    ff = b.gu.shape[1]

    def keep(index, value, j=None):
        if j is None:
            b.dvec[index : index + 1, :] = value
        else:
            b.dvec[index : index + 1, at_tile(j, size)] = value

    def low(j):
        value = b.g[:, at_tile(j, size)]
        keep(vec.bd, jnp.sum(value, 0, keepdims=True), j)
        b.gz[:, at_tile(j, size)] = value.astype(BF16)

    loop(width // size, low)
    blocks = ff // 4 // size

    def feed(j):
        place = (j // blocks, at_tile(lax.rem(j, blocks), size), slice(None))
        grad = dot_nt(b.gz[...], whole.down[place]) * b.slope[:, at_tile(j, size)].astype(F32)
        up_grad[:, at_tile(j, size)] = jnp.sum(grad, 0, keepdims=True)
        b.gu[:, at_tile(j, size)] = grad.astype(BF16)
        whole.down[place] = dot(b.aT[at_tile(j, size), :], b.gz[...]).astype(BF16)

    count = ff // size
    for part in range(4):
        need(("down", part), ("slope", part), ("aT", part))
        loop(count // 4, lambda i, part=part: feed(i + part * (count // 4)))
        if part < 3:
            yield
    emit("down")
    yield
    need("up", "h2T")

    def lift(j, first):
        columns = at_tile(j, width)
        tile = whole.up[:, :, columns]
        part = dot_nt(b.gu[:, columns], tile.reshape(width, width))
        b.acc[...] = part if first else b.acc[...] + part

        def grad(i):
            lanes = pl.ds(pl.multiple_of(j * width + i * size, size), size)
            value = dot(b.h2T[...], b.gu[:, lanes]).astype(BF16)
            whole.up[:, :, lanes] = value.reshape(4, width // 4, size)

        loop(width // size, grad)

    lift(0, True)
    yield
    for j in range(1, ff // width):
        lift(j, False)
        if j < ff // width - 1:
            yield
    emit("up")
    yield
    need("v1", "out", "oT")
    zero = jnp.zeros((1, width), F32)

    def norm_two(i, sums):
        rows = at_tile(i, chunk)
        grad = b.acc[rows, :]
        back, terms = norm_back(b.v1[rows, :], b.vec[vec.gain2 : vec.gain2 + 1, :], grad)
        total = b.g[rows, :] + back
        b.g[rows, :] = total
        b.gz[rows, :] = total.astype(BF16)
        return (
            sums[0] + jnp.sum(terms, 0, keepdims=True),
            sums[1] + jnp.sum(grad, 0, keepdims=True),
            sums[2] + jnp.sum(total, 0, keepdims=True),
        )

    gain_sum, shift_sum, out_sum = lax.fori_loop(0, length // chunk, norm_two, (zero, zero, zero))
    keep(vec.gain2, gain_sum)
    keep(vec.bias2, shift_sum)
    keep(vec.bo, out_sum)
    span = width // 2
    for i in range(2):
        tile = whole.out[2 * i : 2 * i + 2].reshape(span, width)
        b.go[:, i * span : (i + 1) * span] = dot_nt(b.gz[...], tile).astype(BF16)

    def out_grad(j):
        value = dot(b.oT[...], b.gz[:, at_tile(j, size)]).astype(BF16)
        whole.out[:, :, at_tile(j, size)] = value.reshape(4, width // 4, size)

    loop(width // size, out_grad)
    emit("out")
    turn(b.go, b.goT, width)
    yield
    need("q", "k", "v", "qT", "kT", "lse", "apart")
    b.dk[...] = jnp.zeros((length, width), F32)
    b.dv[...] = jnp.zeros((length, width), F32)

    def attend(h):
        group = at_tile(h // per, 128)
        mine = at_tile(h, head)
        lane = lax.broadcasted_iota(jnp.int32, (length, 128), 1) // head == lax.rem(h, per)

        def only(ref):
            return jnp.where(lane, ref[:, group], jnp.zeros((), BF16))

        scores = dot(only(b.k), b.qT[group, :]) * (scale * LOG2E) + b.apart[...]
        probs = jnp.exp2(scores - b.lse[h])
        b.dv[:, group] += dot(probs.astype(BF16), only(b.go))
        back = dot(only(b.v), b.goT[group, :])
        centre = jnp.sum(probs * back, 0, keepdims=True)
        grad = (probs * (back - centre) * scale).astype(BF16)
        b.dk[:, group] += dot(grad, only(b.q))
        b.dqT[mine, :] = dot(b.kT[mine, :], grad)

    parts = 8 if heads % 8 == 0 else 4
    for part in range(parts):
        loop(heads // parts, lambda i, part=part: attend(i + part * (heads // parts)))
        yield
    need("qkv", "hT")

    def query_grad(j):
        lanes = at_tile(j, 128)
        value = b.dqT[lanes, :].T
        b.dvec[vec.bq : vec.bq + 1, lanes] = jnp.sum(value, 0, keepdims=True)
        b.gq0[:, lanes] = value.astype(BF16)

    def rest_grad(j):
        lanes = at_tile(j, 128)
        value = b.dv[:, lanes]
        b.dvec[vec.bv : vec.bv + 1, lanes] = jnp.sum(value, 0, keepdims=True)
        b.gq2[:, lanes] = value.astype(BF16)
        b.gq1[:, lanes] = b.dk[:, lanes].astype(BF16)

    loop(width // 128, query_grad)
    loop(width // 128, rest_grad)
    for third in range(3):
        gq = (b.gq0, b.gq1, b.gq2)[third]
        tile = whole.qkv[:, :, third * width : (third + 1) * width].reshape(width, width)
        part = dot_nt(gq[...], tile)
        b.acc[...] = part if third == 0 else b.acc[...] + part

        def grad(i, gq=gq, third=third):
            value = dot(b.hT[...], gq[:, at_tile(i, size)]).astype(BF16)
            whole.qkv[:, :, pl.ds(pl.multiple_of(third * width + i * size, size), size)] = value.reshape(
                4, width // 4, size
            )

        loop(width // size, grad)
    emit("qkv")
    yield
    need("x")

    def norm_one(i, sums):
        rows = at_tile(i, chunk)
        grad = b.acc[rows, :]
        back, terms = norm_back(read(rows), b.vec[vec.gain1 : vec.gain1 + 1, :], grad)
        b.g[rows, :] = b.g[rows, :] + back
        return (sums[0] + jnp.sum(terms, 0, keepdims=True), sums[1] + jnp.sum(grad, 0, keepdims=True))

    gain_sum, shift_sum = lax.fori_loop(0, length // chunk, norm_one, (zero, zero))
    keep(vec.gain1, gain_sum)
    keep(vec.bias1, shift_sum)
    yield


class Inputs:
    def __init__(self, sem):
        self.sem, self.count, self.flights = sem, 0, {}

    def fetch(self, name, src, dst):
        copy = pltpu.make_async_copy(src, dst, self.sem.at[self.count])
        copy.start()
        self.count += 1
        self.flights[name] = copy

    def need(self, *names):
        for name in names:
            if name in self.flights:
                self.flights.pop(name).wait()

    def finish(self):
        self.need(*list(self.flights))


def fetch_block(inputs, weights, saved, whole, b):
    quarter = b.slope.shape[1] // 4
    for i in range(4):
        part = pl.ds(i * quarter, quarter)
        inputs.fetch(("down", i), weights.down.at[i], whole.down.at[i])
        inputs.fetch(("slope", i), saved.slope.at[:, part], b.slope.at[:, part])
        inputs.fetch(("aT", i), saved.aT.at[part], b.aT.at[part])
    for key, src, dst in (
        ("up", weights.up, whole.up),
        ("h2T", saved.h2T, b.h2T),
        ("v1", saved.v1, b.v1),
        ("out", weights.out, whole.out),
        ("oT", saved.oT, b.oT),
        ("q", saved.q, b.q),
        ("k", saved.k, b.k),
        ("v", saved.v, b.v),
        ("qT", saved.qT, b.qT),
        ("kT", saved.kT, b.kT),
        ("lse", saved.lse, b.lse),
        ("apart", saved.apart, b.apart),
        ("qkv", weights.qkv, whole.qkv),
        ("hT", saved.hT, b.hT),
    ):
        inputs.fetch(key, src, dst)


def decoder_back_kernel(cfg, refs):
    shapes, slots, padded_slots, width, length, parts = cfg
    it = iter(refs)

    def take(n):
        return [next(it) for _ in range(n)]

    cotangent, dec_vec = take(2)
    weights, embed_in = Weights(*take(4)), next(it)
    saved = Read(*take(fields(Read)))
    dec_in, shown, shown_t, hid_t = take(4)
    outs = take(3)
    qkv_out, embed_out, hidden_out, dvec_out, up_out = take(5)
    whole, embed_whole = Weights(*take(4)), next(it)
    b = fill(types.SimpleNamespace(), Read, take(fields(Read)))
    here_in, here_shown, here_shown_t, here_hid_t = take(4)
    fill(b, Back, take(fields(Back)))
    b.dvec, up_grad, grad_hidden = take(3)
    bufs = [take(6) for _ in range(parts)]
    send_sem, recv_sem, in_sem, out_sem = take(4)
    b.vec = dec_vec
    inputs = Inputs(in_sem)
    fetch_block(inputs, weights, saved, whole, b)
    inputs.fetch("x", dec_in, here_in)
    inputs.fetch(0, shown, here_shown)
    inputs.fetch(1, shown_t, here_shown_t)
    inputs.fetch(2, hid_t, here_hid_t)
    inputs.fetch(3, embed_in, embed_whole)
    at = Place()
    at.greet()
    sent = ("out", "up", "down")
    scatter = Scatter(at, shapes, [whole.out, whole.up, whole.down], outs, bufs, None, send_sem, recv_sem)
    b.dvec[...] = jnp.zeros(b.dvec.shape, F32)
    for j in range(width // 128):
        lanes = slice(j * 128, (j + 1) * 128)
        b.g[slots // 16 * 16 :, lanes] = jnp.zeros((padded_slots - slots // 16 * 16, 128), F32)
        b.g[:slots, lanes] = cotangent[:, lanes].astype(F32)

    def emit(name):
        if name == "down":
            at.meet()
        if name in sent:
            scatter.emit(sent.index(name))

    def read(rows):
        return here_in[rows, :]

    for _ in backward_block(
        b, inputs.need, read, padded_slots, width, DHEADS, DEC_VEC, up_grad, whole, emit
    ):
        scatter.tick(DEC_PATIENCE)
    outgoing = []

    def put(src, dst):
        copy = pltpu.make_async_copy(src, dst, out_sem.at[len(outgoing)])
        copy.start()
        outgoing.append(copy)

    put(whole.qkv, qkv_out)
    inputs.need(0, 1, 2, 3)
    slot_col = lax.broadcasted_iota(jnp.int32, (padded_slots, 1), 0)
    empty = jnp.where(slot_col < slots, 1.0, 0.0) - jnp.sum(here_shown[...].astype(F32), 1, keepdims=True)

    def embed(j):
        lanes = at_tile(j, 256)
        value = b.g[:, lanes]
        b.dvec[1:2, lanes] = jnp.sum(empty * value, 0, keepdims=True)
        high = value.astype(BF16)
        low = (value - high.astype(F32)).astype(BF16)
        rows = dot(here_shown_t[...], high) + dot(here_shown_t[...], low)
        b.dvec[0:1, lanes] = jnp.sum(rows, 0, keepdims=True)
        b.gz[:length, lanes] = rows.astype(BF16)

    loop(width // 256, embed)
    wide = embed_whole.shape[1] * 4
    for i in range(2):
        tile = embed_whole[2 * i : 2 * i + 2].reshape(wide // 2, width)
        grad_hidden[:, i * (wide // 2) : (i + 1) * (wide // 2)] = dot_nt(b.gz[:length, :], tile)

    def embed_grad(j):
        value = dot(here_hid_t[...], b.gz[:length, at_tile(j, 256)]).astype(BF16)
        embed_whole[:, :, at_tile(j, 256)] = value.reshape(4, wide // 4, 256)

    loop(width // 256, embed_grad)
    put(embed_whole, embed_out)
    put(grad_hidden, hidden_out)
    put(b.dvec, dvec_out)
    put(up_grad, up_out)
    inputs.finish()
    scatter.finish()
    for copy in outgoing:
        copy.wait()


def struct(shape):
    return jax.ShapeDtypeStruct(*shape)


def decoder_back(weights, kept, cotangent, dec_vec, dec_in, shown, shown_t, hid_t, row):
    wide = [(w.shape[1] // 8, w.shape[2]) for w in weights]
    shapes = wide[1:4]
    slots, width = dec_in.shape
    length = shown.shape[1]
    ff = wide[2][1]
    any_space = pl.BlockSpec(memory_space=pl.ANY)
    vmem = pl.BlockSpec(memory_space=pltpu.VMEM)
    back = back_buffers(slots, width, ff)
    whole_shapes = [(w.shape, BF16) for w in weights]
    read = [getattr(kept, key) for key in Read._fields]
    read_shapes = [(a.shape, a.dtype) for a in read]
    other = [(a.shape, a.dtype) for a in (dec_in, shown, shown_t, hid_t)]
    results = [((16, width), F32), ((1, ff), F32), ((length, hid_t.shape[0]), F32)]
    scratch = [pltpu.VMEM(*s) for s in whole_shapes + read_shapes + other + list(back) + results]
    sums = scatter_shapes(shapes, (2, 1, 0))
    scratch += [pltpu.VMEM(*s) for s in sums]
    scratch += [
        pltpu.SemaphoreType.DMA((8, 8)),
        pltpu.SemaphoreType.DMA((8, 8)),
        pltpu.SemaphoreType.DMA((32,)),
        pltpu.SemaphoreType.DMA((8,)),
    ]
    outs = [(s, F32) for s in shapes]
    out_shape = [struct(s) for s in outs + [whole_shapes[0], whole_shapes[4], results[2], results[0], results[1]]]
    cfg = (shapes, row, slots, width, length, len(sums) // 6)

    def body(*refs):
        decoder_back_kernel(cfg, refs)

    return pl.pallas_call(
        body,
        out_shape=out_shape,
        in_specs=[vmem] * 2 + [any_space] * (5 + len(read) + 4),
        out_specs=[vmem] * 3 + [any_space] * 5,
        scratch_shapes=scratch,
        compiler_params=pltpu.CompilerParams(
            collective_id=1, has_side_effects=True, vmem_limit_bytes=VMEM_BYTES
        ),
        name="decoder_back",
    )(cotangent, dec_vec, *weights, *read, dec_in, shown, shown_t, hid_t)


def encoder_back_kernel(cfg, refs):
    shapes, sizes, length, width, parts = cfg
    count = len(shapes)
    it = iter(refs)

    def take(n):
        return [next(it) for _ in range(n)]

    enc_vec, dec_dvec, dec_up_grad = take(3)
    weights = Weights(*take(4))
    dec_grads = take(2)
    saved = Read(*take(fields(Read)))
    patches, hidden = take(2)
    outs = take(count)
    vec_outs = take(len(sizes))
    patch_out = next(it)
    whole = Weights(*take(4))
    dec_whole = take(2)
    b = fill(types.SimpleNamespace(), Read, take(fields(Read)))
    x = next(it)
    fill(b, Back, take(fields(Back)))
    b.dvec, up_grad = take(2)
    bufs = [take(6) for _ in range(parts)]
    vec = VecBufs(*take(6))
    send_sem, recv_sem, in_sem, out_sem = take(4)
    b.vec = enc_vec
    inputs = Inputs(in_sem)
    inputs.fetch(0, dec_grads[0], dec_whole[0])
    inputs.fetch("g", hidden, b.g)
    inputs.fetch(1, dec_grads[1], dec_whole[1])
    fetch_block(inputs, weights, saved, whole, b)
    inputs.fetch("x", patches, x)
    at = Place()
    at.greet()
    at.meet()
    scatter = Scatter(at, shapes, dec_whole + list(whole), outs, bufs, vec, send_sem, recv_sem)
    for m in range(2):
        inputs.need(m)
        scatter.emit(m)

    def emit(name):
        scatter.emit(2 + Weights._fields.index(name))

    def read(rows):
        return x[rows, :].astype(F32)

    inputs.need("g")
    for _ in backward_block(b, inputs.need, read, length, width, HEADS, ENC_VEC, up_grad, whole, emit):
        scatter.tick(ENC_PATIENCE)
    copy = pltpu.make_async_copy(b.g, patch_out, out_sem.at[0])
    copy.start()
    enc_dvec, dec_dvec = b.dvec[...], dec_dvec[...]
    ups, dec_ups = up_grad[...], dec_up_grad[...]
    for d in range(32):
        tile = vec.tiles.at[d // 8, d // 2 % 4, d % 2]
        tile[0:8] = collect(enc_dvec, sizes[0], d)
        row = lax.broadcasted_iota(jnp.int32, (8, 128), 0)
        up = jnp.broadcast_to(collect(ups, sizes[ENC_UP_ROW], d), (8, 128))
        dec_up = jnp.broadcast_to(collect(dec_ups, sizes[DEC_UP_ROW], d), (8, 128))
        both = collect(dec_dvec, sizes[8], d)
        tile[8:16] = both[:8]
        tile[16:24] = jnp.where(row == ENC_UP_ROW - 16, up, jnp.where(row == DEC_UP_ROW - 16, dec_up, both[8:]))
    scatter.emit(None)
    inputs.finish()
    scatter.finish()
    for k, ref in enumerate(vec_outs):
        ref[...] = vec.sum[k : k + 1, : sizes[k]]
    copy.wait()


def encoder_back(weights, dec_grads, kept, enc_vec, dec_dvec, dec_up_grad, patches, grad_hidden, sizes):
    shapes = [(w.shape[1] // 8, w.shape[2]) for w in list(dec_grads) + list(weights)]
    length, width = patches.shape
    ff = weights[2].shape[2]
    any_space = pl.BlockSpec(memory_space=pl.ANY)
    vmem = pl.BlockSpec(memory_space=pltpu.VMEM)
    back = back_buffers(length, width, ff)
    whole_shapes = [(w.shape, BF16) for w in list(weights) + list(dec_grads)]
    read = [getattr(kept, key) for key in Read._fields]
    read_shapes = [(a.shape, a.dtype) for a in read]
    scratch = whole_shapes + read_shapes + [(patches.shape, BF16)] + list(back)
    scratch += [((8, width), F32), ((1, ff), F32)]
    sums = scatter_shapes(shapes, (0, 1, 5, 4, 3, 2))
    scratch += sums
    tile = (VEC_ROWS, 128)
    scratch += [((4, 4, 2) + tile, F32), ((4, 4) + tile, F32), ((2, 4) + tile, F32), ((4,) + tile, F32)]
    scratch += [((3,) + tile, F32), (tile, F32)]
    scratch = [pltpu.VMEM(*s) for s in scratch]
    scratch += [
        pltpu.SemaphoreType.DMA((14, 8)),
        pltpu.SemaphoreType.DMA((14, 8)),
        pltpu.SemaphoreType.DMA((32,)),
        pltpu.SemaphoreType.DMA((1,)),
    ]
    outs = [(s, F32) for s in shapes] + [((1, s), F32) for s in sizes] + [((length, width), F32)]
    cfg = (shapes, sizes, length, width, len(sums) // 6)

    def body(*refs):
        encoder_back_kernel(cfg, refs)

    results = pl.pallas_call(
        body,
        out_shape=[struct(s) for s in outs],
        in_specs=[vmem] * 3 + [any_space] * (4 + 2 + len(read) + 2),
        out_specs=[vmem] * (len(shapes) + len(sizes)) + [any_space],
        scratch_shapes=scratch,
        compiler_params=pltpu.CompilerParams(
            collective_id=2, has_side_effects=True, vmem_limit_bytes=VMEM_BYTES
        ),
        name="encoder_back",
    )(enc_vec, dec_dvec, dec_up_grad, *weights, *dec_grads, *read, patches, grad_hidden)
    count = len(shapes)
    return results[:count], results[count : count + len(sizes)], results[-1]


def settle(arrays):
    count = len(arrays)
    vmem = pl.BlockSpec(memory_space=pltpu.VMEM)

    def body(*refs):
        for src, dst in zip(refs[:count], refs[count:]):
            rows = src.shape[0]
            if rows % 16 == 0 and rows > 128:
                loop(rows // 16, lambda i, src=src, dst=dst: dst.__setitem__(at_tile(i, 16), src[at_tile(i, 16)]))
            else:
                dst[...] = src[...]

    return pl.pallas_call(
        body,
        out_shape=[jax.ShapeDtypeStruct(a.shape, a.dtype) for a in arrays],
        in_specs=[vmem] * count,
        out_specs=[vmem] * count,
        compiler_params=pltpu.CompilerParams(vmem_limit_bytes=VMEM_BYTES),
        name="settle",
    )(*arrays)


def widen(value):
    return value.astype(jnp.float32)


def layer_norm(stream, gain, shift):
    row_mean = jnp.mean(stream, -1, keepdims=True)
    centred = stream - row_mean
    row_var = jnp.mean(centred * centred, -1, keepdims=True)
    return centred * lax.rsqrt(row_var + EPSILON) * gain + shift


def norm_pull(stream, gain, shift, grad_out):
    pull = jax.vjp(layer_norm, stream, gain, shift)[1]
    return pull(grad_out)


def gelu_exact(value):
    return jax.nn.gelu(value, approximate=False)


def split_heads(rows, head_count):
    batch, length, model_width = rows.shape
    return rows.reshape(batch, length, head_count, model_width // head_count)


def masked_scores(query_heads, key_heads, same_doc, score_scale):
    scores = (
        jnp.einsum("bqhd,bkhd->bhqk", query_heads, key_heads, preferred_element_type=jnp.float32)
        * score_scale
    )
    return jnp.where(same_doc[:, None], scores, -1000000000.0)


def attend_forward(query_rows, key_rows, value_rows, same_doc, head_count, score_scale):
    batch, length, model_width = query_rows.shape
    scores = masked_scores(
        split_heads(query_rows, head_count),
        split_heads(key_rows, head_count),
        same_doc,
        score_scale,
    )
    row_max = jnp.max(scores, -1, keepdims=True)
    expo = jnp.exp(scores - row_max)
    row_sum = jnp.sum(expo, -1, keepdims=True)
    att_probs = (expo / row_sum).astype(jnp.bfloat16)
    mixed = jnp.einsum(
        "bhqk,bkhd->bqhd",
        att_probs,
        split_heads(value_rows, head_count),
        preferred_element_type=jnp.float32,
    )
    return (mixed.reshape(batch, length, model_width), row_max + jnp.log(row_sum))


def attend_backward(
    query_rows, key_rows, value_rows, same_doc, log_total, grad_mixed, head_count, score_scale
):
    batch, length, model_width = query_rows.shape
    query_heads = split_heads(query_rows, head_count)
    key_heads = split_heads(key_rows, head_count)
    value_heads = split_heads(value_rows, head_count)
    grad_heads = split_heads(grad_mixed, head_count)
    att_probs = jnp.exp(masked_scores(query_heads, key_heads, same_doc, score_scale) - log_total)
    grad_value = jnp.einsum(
        "bhqk,bqhd->bkhd",
        att_probs.astype(jnp.bfloat16),
        grad_heads,
        preferred_element_type=jnp.float32,
    )
    grad_probs = jnp.einsum(
        "bqhd,bkhd->bhqk", grad_heads, value_heads, preferred_element_type=jnp.float32
    )
    centre = jnp.sum(att_probs * grad_probs, -1, keepdims=True)
    grad_scores = (att_probs * (grad_probs - centre) * score_scale).astype(jnp.bfloat16)
    grad_query = jnp.einsum(
        "bhqk,bkhd->bqhd", grad_scores, key_heads, preferred_element_type=jnp.float32
    )
    grad_key = jnp.einsum(
        "bhqk,bqhd->bkhd", grad_scores, query_heads, preferred_element_type=jnp.float32
    )
    rows = batch * length
    return (
        grad_query.reshape(rows, model_width),
        grad_key.reshape(rows, model_width),
        grad_value.reshape(rows, model_width),
    )


def block_forward(stream, params, seg_ids, head_count):
    (
        gain_one,
        shift_one,
        w_qkv,
        query_bias,
        value_bias,
        w_out,
        out_bias,
        gain_two,
        shift_two,
        w_up,
        up_bias,
        w_down,
        down_bias,
    ) = params
    row_count, model_width = stream.shape
    batch, length = seg_ids.shape
    score_scale = (model_width // head_count) ** (-0.5)
    normed = layer_norm(stream, widen(gain_one), widen(shift_one)).astype(jnp.bfloat16)
    joined = jnp.dot(normed, w_qkv, preferred_element_type=jnp.float32)
    query_rows = (joined[:, :model_width] + widen(query_bias)).astype(jnp.bfloat16)
    key_rows = joined[:, model_width : 2 * model_width].astype(jnp.bfloat16)
    value_rows = (joined[:, 2 * model_width :] + widen(value_bias)).astype(jnp.bfloat16)
    same_doc = seg_ids[:, :, None] == seg_ids[:, None, :]
    shape_three = (batch, length, model_width)
    mixed, log_total = attend_forward(
        query_rows.reshape(shape_three),
        key_rows.reshape(shape_three),
        value_rows.reshape(shape_three),
        same_doc,
        head_count,
        score_scale,
    )
    attended = mixed.reshape(row_count, model_width).astype(jnp.bfloat16)
    middle = stream + jnp.dot(attended, w_out, preferred_element_type=jnp.float32) + widen(out_bias)
    normed_two = layer_norm(middle, widen(gain_two), widen(shift_two)).astype(jnp.bfloat16)
    hidden_up = jnp.dot(normed_two, w_up, preferred_element_type=jnp.float32) + widen(up_bias)
    activated = gelu_exact(hidden_up).astype(jnp.bfloat16)
    result = (
        middle + jnp.dot(activated, w_down, preferred_element_type=jnp.float32) + widen(down_bias)
    )
    saved = (
        stream,
        middle,
        normed,
        query_rows,
        key_rows,
        value_rows,
        log_total,
        attended,
        normed_two,
        hidden_up,
        activated,
    )
    return (result, saved)


def back_feed(grad_out, params, saved):
    (
        gain_one,
        shift_one,
        w_qkv,
        query_bias,
        value_bias,
        w_out,
        out_bias,
        gain_two,
        shift_two,
        w_up,
        up_bias,
        w_down,
        down_bias,
    ) = params
    (
        stream,
        middle,
        normed,
        query_rows,
        key_rows,
        value_rows,
        log_total,
        attended,
        normed_two,
        hidden_up,
        activated,
    ) = saved
    grad_low = grad_out.astype(jnp.bfloat16)
    grad_down_bias = jnp.sum(grad_out, 0)
    grad_down = jnp.einsum("rf,rw->fw", activated, grad_low, preferred_element_type=jnp.float32)
    grad_act = jnp.einsum("rw,fw->rf", grad_low, w_down, preferred_element_type=jnp.float32)
    grad_hidden = jax.vjp(gelu_exact, hidden_up)[1](grad_act)[0]
    grad_hidden_low = grad_hidden.astype(jnp.bfloat16)
    grad_up_bias = jnp.sum(grad_hidden, 0)
    grad_up = jnp.einsum(
        "rd,rf->df", normed_two, grad_hidden_low, preferred_element_type=jnp.float32
    )
    grad_normed_two = jnp.einsum(
        "rf,df->rd", grad_hidden_low, w_up, preferred_element_type=jnp.float32
    )
    grad_mid_norm, grad_gain_two, grad_shift_two = norm_pull(
        middle, widen(gain_two), widen(shift_two), grad_normed_two
    )
    grad_middle = grad_out + grad_mid_norm
    return (
        grad_middle,
        (grad_gain_two, grad_shift_two, grad_up, grad_up_bias, grad_down, grad_down_bias),
    )


def back_attend(grad_middle, params, seg_ids, head_count, saved):
    (
        gain_one,
        shift_one,
        w_qkv,
        query_bias,
        value_bias,
        w_out,
        out_bias,
        gain_two,
        shift_two,
        w_up,
        up_bias,
        w_down,
        down_bias,
    ) = params
    (
        stream,
        middle,
        normed,
        query_rows,
        key_rows,
        value_rows,
        log_total,
        attended,
        normed_two,
        hidden_up,
        activated,
    ) = saved
    row_count, model_width = stream.shape
    batch, length = seg_ids.shape
    score_scale = (model_width // head_count) ** (-0.5)
    grad_middle_low = grad_middle.astype(jnp.bfloat16)
    grad_out_bias = jnp.sum(grad_middle, 0)
    grad_w_out = jnp.einsum(
        "rv,rw->vw", attended, grad_middle_low, preferred_element_type=jnp.float32
    )
    grad_attended = jnp.einsum(
        "rw,vw->rv", grad_middle_low, w_out, preferred_element_type=jnp.float32
    ).astype(jnp.bfloat16)
    same_doc = seg_ids[:, :, None] == seg_ids[:, None, :]
    shape_three = (batch, length, model_width)
    grad_query, grad_key, grad_value = attend_backward(
        query_rows.reshape(shape_three),
        key_rows.reshape(shape_three),
        value_rows.reshape(shape_three),
        same_doc,
        log_total,
        grad_attended.reshape(shape_three),
        head_count,
        score_scale,
    )
    grad_query_bias = jnp.sum(grad_query, 0)
    grad_value_bias = jnp.sum(grad_value, 0)
    grad_joined = jnp.concatenate([grad_query, grad_key, grad_value], 1).astype(jnp.bfloat16)
    grad_qkv = jnp.einsum("rd,rc->dc", normed, grad_joined, preferred_element_type=jnp.float32)
    grad_normed = jnp.einsum("rc,dc->rd", grad_joined, w_qkv, preferred_element_type=jnp.float32)
    grad_in_norm, grad_gain_one, grad_shift_one = norm_pull(
        stream, widen(gain_one), widen(shift_one), grad_normed
    )
    grads = (
        grad_gain_one,
        grad_shift_one,
        grad_qkv,
        grad_query_bias,
        grad_value_bias,
        grad_w_out,
        grad_out_bias,
    )
    return (grad_middle + grad_in_norm, grads)


def block_backward(grad_out, params, seg_ids, head_count, saved):
    grad_middle, feed_grads = back_feed(grad_out, params, saved)
    grad_in, attend_grads = back_attend(grad_middle, params, seg_ids, head_count, saved)
    return (grad_in, attend_grads + feed_grads)


def by_collectives(a):
    seq_count = a.segments.shape[0] // ROW
    seg_ids = a.segments.reshape(seq_count, ROW)
    vis_slots = a.visible_index.reshape(seq_count, VIS)
    enc_seg = jnp.take_along_axis(seg_ids, vis_slots, 1)
    seq_index = jnp.arange(seq_count, dtype=jnp.int32)[:, None]
    matrices = [lax.all_gather(m, AXIS, axis=0, tiled=True) for m in matrices_of(a)]
    joined = lax.all_gather(jnp.concatenate(vectors_of(a)), AXIS, axis=0)
    sizes = [v.shape[0] for v in vectors_of(a)]
    vectors, start = [], 0
    for size in sizes:
        vectors.append(joined[:, start : start + size].reshape(-1))
        start += size
    whole = Arguments(a.patches, a.visible_index, a.segments, a.cotangent, *in_order(matrices, vectors))
    hidden, enc_saved = block_forward(widen(a.patches), encoder_of(whole), enc_seg, HEADS)
    hidden_low = hidden.astype(jnp.bfloat16)
    embedded = jnp.dot(hidden_low, whole.embed_weight, preferred_element_type=jnp.float32) + widen(
        whole.embed_bias
    )
    embedded = embedded.reshape(seq_count, VIS, DD)
    dec_in = (
        jnp.broadcast_to(widen(whole.mask_token), (seq_count, ROW, DD))
        .at[seq_index, vis_slots]
        .set(embedded)
    )
    dec_in = dec_in.reshape(seq_count * ROW, DD)
    decoded, dec_saved = block_forward(dec_in, decoder_of(whole), seg_ids, DHEADS)
    grad_dec_in, dec_grads = block_backward(
        widen(a.cotangent), decoder_of(whole), seg_ids, DHEADS, dec_saved
    )
    grad_dec_in = grad_dec_in.reshape(seq_count, ROW, DD)
    shown_slots = jnp.zeros((seq_count, ROW), jnp.float32).at[seq_index, vis_slots].set(1.0)
    grad_mask = jnp.sum((1.0 - shown_slots)[:, :, None] * grad_dec_in, (0, 1))
    grad_embedded = grad_dec_in[seq_index, vis_slots].reshape(seq_count * VIS, DD)
    grad_embed_b = jnp.sum(grad_embedded, 0)
    grad_embedded_low = grad_embedded.astype(jnp.bfloat16)
    grad_embed_w = jnp.einsum(
        "rd,re->de", hidden_low, grad_embedded_low, preferred_element_type=jnp.float32
    )
    grad_hidden = jnp.einsum(
        "re,de->rd", grad_embedded_low, whole.embed_weight, preferred_element_type=jnp.float32
    )
    grad_patches, enc_grads = block_backward(grad_hidden, encoder_of(whole), enc_seg, HEADS, enc_saved)
    grads = Arguments(None, None, None, None, *enc_grads, grad_embed_w, grad_embed_b, grad_mask, *dec_grads)
    sums = [lax.psum_scatter(m, AXIS, scatter_dimension=0, tiled=True) for m in matrices_of(grads)]
    joined = jnp.concatenate([v.reshape(-1, size) for v, size in zip(vectors_of(grads), sizes)], 1)
    joined = lax.psum_scatter(joined, AXIS, scatter_dimension=0, tiled=True).reshape(-1)
    vector_sums, start = [], 0
    for size in sizes:
        vector_sums.append(joined[start : start + size])
        start += size
    return (decoded.astype(jnp.bfloat16), grad_patches) + in_order(sums, vector_sums)


def fits(a):
    return (
        lax.axis_size(AXIS) == 32
        and a.segments.shape[0] == ROW
        and a.patches.shape[0] == VIS
        and all(m.shape[0] % 8 == 0 and m.shape[1] % 256 == 0 for m in matrices_of(a))
        and all(v.shape[0] <= 128 for v in vectors_of(a))
    )


def by_kernels(a):
    vectors = vectors_of(a)
    sizes = [v.shape[0] for v in vectors]
    wholes, enc_vec, dec_vec, enc_kept, dec_kept, hid_t, dec_in, shown, shown_t, decoded = forward_all(
        matrices_of(a), vectors, a.patches, a.visible_index, a.segments, ROW
    )
    *dec_sums, qkv, embed, grad_hidden, dec_dvec, dec_up = decoder_back(
        wholes[5:] + [wholes[4]], dec_kept, a.cotangent, dec_vec, dec_in, shown, shown_t, hid_t, ROW
    )
    (dec_qkv, embed, *enc_sums), vec_sums, grad_patches = encoder_back(
        wholes[:4], [qkv, embed], enc_kept, enc_vec, dec_dvec, dec_up, a.patches, grad_hidden, sizes
    )
    sums = in_order(list(enc_sums) + [embed, dec_qkv] + list(dec_sums), vec_sums)
    results = settle((decoded, grad_patches) + sums)
    shapes = (None,) * 4 + tuple(v.shape for v in a[4:])
    return tuple(results[:2]) + tuple(r.reshape(-1) if len(s) == 1 else r for r, s in zip(results[2:], shapes[4:]))


def on_device(*arguments):
    a = Arguments(*arguments)
    return by_kernels(a) if fits(a) else by_collectives(a)


def solution(mesh):
    count = len(Arguments._fields)
    vectors = vectors_of(Arguments(*range(count)))
    specs = [P(AXIS) if i in (1, 2) or i in vectors else P(AXIS, None) for i in range(count)]
    return jax.shard_map(
        on_device,
        mesh=mesh,
        in_specs=tuple(specs),
        out_specs=tuple([P(AXIS, None)] * 2 + specs[4:]),
        check_vma=False,
    )
```
